32 devices in a mesh: ingest: 4 (over x, core), run: 8 (over z, y).
Axes of the slice: x: 2, y: 2, z: 4, core: 2. Of those that a mesh axis runs over, the one named last changes fastest.
Arguments:
- embeddings: bfloat16 [32768, 768], P(('ingest', 'run')), may hold values from -2000 to 2000, as said below
- cluster_id: int32 [32768], P(('ingest', 'run')), may hold values from 0 to 11, as said below
- rank: int32 [32768], P(('ingest', 'run')), may hold values from 0 to 4095, as said below
- run_len: int32 [12], replicated, may hold values from 2 to 4, as said below
Outputs:
- best_cosine: float32 [32768], P(('ingest', 'run'))
The draws below stay inside these ranges and needn't reach their ends.
Inputs may be any that keep to these rules, and one draw needn't show every extreme that they name: All lengths are even. For each ingest index i, the lengths of the 3 clusters c with c // 3 == i are 4, 2 and 2 in some order (sum 8). Cluster c owns the run devices of ingest index c // 3 from the sum of the lengths of the earlier clusters of that index on, for run_len[c] devices. `cluster_id`: cluster c holds exactly run_len[c] * 1024 rows. The ranks of a cluster's rows are 0 up to its row count - 1, each once. A row of cluster c with rank k belongs to owner slot k % 1024 of run device (start of c) + k // 1024 of ingest index c // 3. Every device holds rows of exactly 16 owner devices, exactly 64 rows of each, and those fill one aligned group of 64 slots of that owner. `embeddings`: rows of one cluster share a direction of their cluster; some rows are near copies of an earlier row of their cluster.
All inputs are finite; a program needn't handle non-finite values.
Results may differ from the reference program's by a relative error of at most 0.00059.
Values may be sent and summed in bfloat16 or wider, within the bound.
No kernel may reach another device: no remote copies, remote signals or barrier semaphores. Data moves between devices by JAX's collectives and lax.ppermute only.
A program may use at most 64 MiB of HBM per device.

```python
import jax
import jax.numpy as jnp
import numpy as np
from jax import lax

D = 768
ROWS_DEV = 1024
RUNS = 3
NCL = 12
MAXRUN = 4
CAP = 64
ROWS = 32768
N_INGEST = 4
N_RUN = 8
DEVICES = 32


def pair_lengths():
    values = [1] * RUNS
    extra = N_RUN // 2 - RUNS
    index = 0
    while extra > 0:
        added = min(MAXRUN // 2 - 1, extra)
        values[index] += added
        extra -= added
        index += 1
    return np.array(values, np.int32)


def layout(key):
    groups = NCL // RUNS
    base = jnp.asarray(pair_lengths())
    keys = jax.random.split(jax.random.fold_in(key, 101), groups)
    pairs = jax.vmap(lambda sub_key: jax.random.permutation(sub_key, base))(keys)
    return (2 * pairs).astype(jnp.int32)


def pick_offsets(key, devices, run_total):
    needed = jnp.array([1, devices - 1, devices // 2, run_total, devices - run_total], jnp.int32)
    number = jnp.arange(devices, dtype=jnp.int32)
    is_needed = jnp.any(number[:, None] == needed[None, :], axis=1)
    shuffled = jax.random.permutation(jax.random.fold_in(key, 202), devices).astype(jnp.int32)
    score = jnp.where(is_needed, number - devices, shuffled)
    chosen = jnp.argsort(score, stable=True)[:devices // 2].astype(jnp.int32)
    mixing = jax.random.permutation(jax.random.fold_in(key, 205), devices // 2)
    return chosen[mixing].astype(jnp.int32)


def placement(key):
    lengths = layout(key)
    groups = NCL // RUNS
    devices = ROWS // ROWS_DEV
    run_total = devices // groups
    starts = jnp.cumsum(lengths, axis=1) - lengths
    slot = jnp.arange(ROWS, dtype=jnp.int32)
    owner_device = slot // ROWS_DEV
    within = slot % ROWS_DEV
    group = owner_device // run_total
    place = owner_device % run_total
    row_starts = starts[group]
    member = jnp.sum((row_starts <= place[:, None]).astype(jnp.int32), axis=1) - 1
    cluster = (group * RUNS + member).astype(jnp.int32)
    begin = jnp.take_along_axis(row_starts, member[:, None], axis=1)[:, 0]
    order = ((place - begin) * ROWS_DEV + within).astype(jnp.int32)
    offsets = pick_offsets(key, devices, run_total)
    source = (owner_device + offsets[within // CAP]) % devices
    local = jax.vmap(lambda sub_key: jax.random.permutation(sub_key, ROWS_DEV))(jax.random.split(jax.random.fold_in(key, 303), devices)).astype(jnp.int32)
    target = (source * ROWS_DEV + local[source, within]).astype(jnp.int32)
    return (cluster, order, target)


def draw_run_len(key, part):
    return layout(key).reshape(NCL)


def draw_cluster_id(key, part):
    cluster, order, target = placement(key)
    return jnp.zeros((ROWS,), jnp.int32).at[target].set(cluster)


def draw_rank(key, part):
    cluster, order, target = placement(key)
    return jnp.zeros((ROWS,), jnp.int32).at[target].set(order)


def draw_embeddings(key, part):
    cluster, order, target = placement(key)
    keys = jax.random.split(jax.random.fold_in(key, 404), 8)
    centres = jax.random.normal(keys[0], (NCL, D), jnp.float32)
    strength = jax.random.uniform(keys[1], (NCL,), jnp.float32, 0.3, 1.5)
    noise = jax.random.normal(keys[2], (ROWS, D), jnp.float32)
    row_scale = jnp.exp(jax.random.uniform(keys[3], (ROWS, 1), jnp.float32, 0.0, 2.3025851))
    base = strength[cluster][:, None] * centres[cluster] + noise
    twin = (jax.random.randint(keys[4], (ROWS,), 0, 10) < 3) & (order > 0)
    back = 1 + jax.random.randint(keys[5], (ROWS,), 0, 1 << 20) % jnp.maximum(order, 1)
    partner = jnp.maximum(jnp.arange(ROWS, dtype=jnp.int32) - back, 0)
    jitter = jax.random.normal(keys[6], (ROWS, D), jnp.float32)
    vectors = jnp.where(twin[:, None], base[partner] + 0.15 * jitter, base)
    column_scale = jnp.exp(jax.random.uniform(keys[7], (1, D), jnp.float32, 0.0, 2.3025851))
    vectors = jnp.clip(vectors * column_scale * row_scale, -2000.0, 2000.0)
    return jnp.zeros((ROWS, D), jnp.float32).at[target].set(vectors).astype(jnp.bfloat16)


def setup_inputs(seed: int = 0) -> dict:
    key_of = jax.random.split(jax.random.key(seed), 5)
    embeddings = draw_embeddings(jax.random.fold_in(key_of[4], 71), 0)
    cluster_id = draw_cluster_id(jax.random.fold_in(key_of[4], 71), 0)
    rank = draw_rank(jax.random.fold_in(key_of[4], 71), 0)
    run_len = draw_run_len(jax.random.fold_in(key_of[4], 71), 0)
    return {"embeddings": embeddings, "cluster_id": cluster_id, "rank": rank, "run_len": run_len}


EPSILON = 1e-06

def reference(embeddings, cluster_id, rank, run_len):
    widened = embeddings.astype(jnp.float32)
    unit_vectors = (widened * lax.rsqrt(lax.optimization_barrier(jnp.sum(widened * widened, axis=1, keepdims=True)) + EPSILON)).astype(jnp.bfloat16)
    run_lengths = run_len.reshape(N_INGEST, RUNS)
    run_starts = (jnp.cumsum(run_lengths, axis=1) - run_lengths).reshape(NCL).astype(jnp.int32)
    cluster_base = ((cluster_id // RUNS * N_RUN + run_starts[cluster_id]) * ROWS_DEV).astype(jnp.int32)
    slot_index = (cluster_base + rank).astype(jnp.int32)
    ordered = jnp.zeros((ROWS, D), jnp.bfloat16).at[slot_index].set(unit_vectors)
    lowest = jnp.zeros((ROWS,), jnp.int32).at[slot_index].set(cluster_base)
    margin = (MAXRUN - 1) * ROWS_DEV
    padded = jnp.concatenate([jnp.zeros((margin, D), jnp.bfloat16), ordered], axis=0)

    def per_device(device):
        first_row = (device * ROWS_DEV).astype(jnp.int32)
        own_block = lax.dynamic_slice_in_dim(ordered, first_row, ROWS_DEV, 0)
        nearby = lax.dynamic_slice_in_dim(padded, first_row, MAXRUN * ROWS_DEV, 0)
        scores = jnp.dot(own_block, nearby.T, preferred_element_type=jnp.float32)
        candidate = first_row - margin + jnp.arange(MAXRUN * ROWS_DEV, dtype=jnp.int32)
        mine_rows = first_row + jnp.arange(ROWS_DEV, dtype=jnp.int32)
        floor_rows = lax.dynamic_slice_in_dim(lowest, first_row, ROWS_DEV, 0)
        allowed = (candidate[None, :] >= floor_rows[:, None]) & (candidate[None, :] < mine_rows[:, None])
        top_score = lax.optimization_barrier(jnp.max(jnp.where(allowed, scores, jnp.float32(-2.0)), axis=1))
        return jnp.maximum(jnp.float32(-1.0), top_score)
    best_slots = lax.map(per_device, jnp.arange(DEVICES, dtype=jnp.int32)).reshape(ROWS)
    return best_slots[slot_index]
```

```python
import functools

import jax
import jax.numpy as jnp
from jax import lax
from jax.experimental import pallas as pl
from jax.experimental.pallas import tpu as pltpu
from jax.sharding import PartitionSpec as P

EPSILON = 1e-06
AXES = ("ingest", "run")
TILE = 256
MEMORY = 60 * 1024 * 1024


class Plan:
    def __init__(self, ingest, run, clusters, rows):
        self.ingest, self.run, self.clusters, self.rows = ingest, run, clusters, rows
        self.devices = ingest * run
        self.per_group = clusters // ingest
        self.cap = 2 * rows // self.devices
        self.reach = min(8, run // 2)
        self.width = run // ingest
        self.pairs = run // 2

    def device(self, group, slot):
        core, chip = slot % 2, slot // 2
        column, place = chip // self.width, chip % self.width
        odd = column % 2
        place = place + odd * (self.width - 1 - 2 * place)
        return (2 * column + core) * self.run + group * self.width + place

    def slot(self, device_ingest, device_run):
        core, column = device_ingest % 2, device_ingest // 2
        place = device_run % self.width
        place = place + (column % 2) * (self.width - 1 - 2 * place)
        return device_run // self.width, 2 * (column * self.width + place) + core

    def splits(self):
        def parts(total, count, top):
            if count == 0:
                if total == 0:
                    yield ()
                return
            for first in range(min(top, total), 0, -1):
                for rest in parts(total - first, count - 1, first):
                    yield (first, *rest)

        return list(parts(self.pairs, self.per_group, self.reach // 2))

    def links(self):
        found = [set() for _ in range(self.reach // 2)]
        for split in self.splits():
            begin = 0
            for length in split:
                for first in range(length):
                    for second in range(first + 1, length):
                        found[second - first].add(begin + first)
                begin += length
        return [sorted(chips) for chips in found]


def cluster_starts(plan, run_len_ref):
    starts = []
    for cluster in range(plan.clusters):
        base = cluster // plan.per_group * plan.per_group
        mine = run_len_ref[cluster]
        total = jnp.int32(0)
        for other in range(base, base + plan.per_group):
            if other == cluster:
                continue
            theirs = run_len_ref[other]
            ahead = (theirs >= mine) if other < cluster else (theirs > mine)
            total = total + jnp.where(ahead, theirs, 0)
        starts.append(total)
    return starts


def row_owner(plan, run_len_ref, cluster, rank):
    starts = cluster_starts(plan, run_len_ref)
    begin = jnp.zeros_like(cluster)
    group = jnp.zeros_like(cluster)
    for number, start in enumerate(starts):
        here = cluster == number
        begin = jnp.where(here, start, begin)
        group = jnp.where(here, number // plan.per_group, group)
    owner = plan.device(group, begin + rank // plan.rows)
    return owner, rank % plan.rows


def pack_kernel(plan, run_len_ref, cluster_ref, rank_ref, rows_ref, out_ref, group_ref, unit_ref):
    step = 128

    @pl.loop(0, plan.rows // step)
    def _(number):
        here = pl.ds(pl.multiple_of(number * step, step), step)
        widened = rows_ref[here, :].astype(jnp.float32)
        total = jnp.sum(widened * widened, axis=1, keepdims=True) + EPSILON
        unit_ref[here, :] = (widened * lax.rsqrt(total)).astype(jnp.bfloat16)

    owner, within = row_owner(plan, run_len_ref, cluster_ref[...], rank_ref[...])
    number = lax.broadcasted_iota(jnp.int32, (plan.devices, plan.rows), 0)
    group = jnp.max(
        jnp.where(number == owner, within // plan.cap + 1, 0), axis=1, keepdims=True
    )
    group_ref[...] = jnp.broadcast_to(group, group_ref.shape)
    position = owner * plan.cap + within % plan.cap

    @pl.loop(0, plan.devices * plan.cap // TILE)
    def _(tile):
        row = lax.broadcasted_iota(jnp.int32, (TILE, plan.rows), 0) + tile * TILE
        chosen = jnp.where(row == position, 1.0, 0.0).astype(jnp.bfloat16)
        moved = jnp.dot(chosen, unit_ref[...], preferred_element_type=jnp.float32)
        here = pl.ds(pl.multiple_of(tile * TILE, TILE), TILE)
        out_ref[here, :] = moved.astype(jnp.bfloat16)


def sort_kernel(plan, group_ref, arrived_ref, out_ref):
    for source in range(plan.devices):
        group = group_ref[source, 0]

        @pl.when(group > 0)
        def _():
            here = pl.ds(pl.multiple_of((group - 1) * plan.cap, plan.cap), plan.cap)
            out_ref[here, :] = arrived_ref[source * plan.cap : (source + 1) * plan.cap, :]


def block_best(keys_ref, queries_ref, best_ref):
    rows = keys_ref.shape[0]

    @pl.loop(0, rows // TILE)
    def _(tile):
        keys = keys_ref[pl.ds(pl.multiple_of(tile * TILE, TILE), TILE), :]
        scores = lax.dot_general(
            keys, queries_ref[...], (((1,), (1,)), ((), ())), preferred_element_type=jnp.float32
        )
        best_ref[...] = jnp.maximum(best_ref[...], jnp.max(scores, axis=0, keepdims=True))


def triangle_best(rows_ref, best_ref):
    rows = rows_ref.shape[0]
    for first in range(0, rows, TILE):
        scores = lax.dot_general(
            rows_ref[first : first + TILE, :],
            rows_ref[first:, :],
            (((1,), (1,)), ((), ())),
            preferred_element_type=jnp.float32,
        )
        key = lax.broadcasted_iota(jnp.int32, (TILE, TILE), 0)
        query = lax.broadcasted_iota(jnp.int32, (TILE, TILE), 1)
        corner = jnp.max(
            jnp.where(key < query, scores[:, :TILE], -2.0), axis=0, keepdims=True
        )
        here = slice(first, first + TILE)
        best_ref[:, here] = jnp.maximum(best_ref[:, here], corner)
        if first + TILE < rows:
            rest = jnp.max(scores[:, TILE:], axis=0, keepdims=True)
            there = slice(first + TILE, rows)
            best_ref[:, there] = jnp.maximum(best_ref[:, there], rest)


def best_kernel(plan, run_len_ref, place_ref, group_ref, own_ref, mate_ref, *rest):
    behind, (out_ref, best_ref, blocks_ref) = rest[:-3], rest[-3:]
    group, slot = plan.slot(place_ref[0], place_ref[1])
    begin = jnp.int32(0)
    for number, start in enumerate(cluster_starts(plan, run_len_ref)):
        here = (number // plan.per_group == group) & (start <= slot)
        begin = jnp.where(here, jnp.maximum(begin, start), begin)
    best_ref[...] = jnp.full(best_ref.shape, -1.0, jnp.float32)
    triangle_best(own_ref, best_ref)

    @pl.when(slot % 2 == 1)
    def _():
        block_best(mate_ref, own_ref, best_ref)

    for distance in range(1, plan.reach // 2):
        first, second = behind[2 * distance - 2], behind[2 * distance - 1]

        @pl.when(slot - slot % 2 - 2 * distance >= begin)
        def _():
            block_best(first, own_ref, best_ref)
            block_best(second, own_ref, best_ref)

    for number in range(plan.rows // plan.cap):
        part = best_ref[:, number * plan.cap : (number + 1) * plan.cap]
        blocks_ref[number : number + 1, : plan.cap] = part
    for source in range(plan.devices):
        chosen = jnp.maximum(group_ref[source, 0] - 1, 0)
        out_ref[source : source + 1, :] = blocks_ref[pl.ds(chosen, 1), :]


def unpack_kernel(plan, run_len_ref, cluster_ref, rank_ref, reply_ref, out_ref):
    owner, within = row_owner(plan, run_len_ref, cluster_ref[...], rank_ref[...])
    number = lax.broadcasted_iota(jnp.int32, (plan.devices, plan.rows), 0)
    chosen = jnp.where(number == owner, 1.0, 0.0)
    columns = lax.dot_general(
        reply_ref[:, : plan.cap],
        chosen,
        (((0,), (0,)), ((), ())),
        precision=lax.Precision.HIGHEST,
        preferred_element_type=jnp.float32,
    )
    lane = lax.broadcasted_iota(jnp.int32, (plan.cap, plan.rows), 0)
    out_ref[...] = jnp.sum(
        jnp.where(lane == within % plan.cap, columns, 0.0), axis=0, keepdims=True
    )


SMEM = pl.BlockSpec(memory_space=pltpu.SMEM)
VMEM = pl.BlockSpec(memory_space=pltpu.VMEM)


def call(kernel, plan, shapes, specs, scratch=(), flops=0, moved=0):
    return pl.pallas_call(
        functools.partial(kernel, plan),
        out_shape=shapes,
        in_specs=specs,
        out_specs=[VMEM] * len(shapes),
        scratch_shapes=scratch,
        compiler_params=pltpu.CompilerParams(vmem_limit_bytes=MEMORY),
        cost_estimate=pl.CostEstimate(flops=flops, bytes_accessed=moved, transcendentals=0),
    )


def exchange(block):
    return lax.all_to_all(block, AXES, split_axis=0, concat_axis=0, tiled=True)


def local(embeddings, cluster_id, rank, run_len):
    rows, width = embeddings.shape
    plan = Plan(lax.axis_size("ingest"), lax.axis_size("run"), run_len.shape[0], rows)
    clusters, ranks = cluster_id.reshape(1, rows), rank.reshape(1, rows)
    slots = plan.devices * plan.cap
    wide = jax.ShapeDtypeStruct
    outgoing, groups = call(
        pack_kernel,
        plan,
        [wide((slots, width), jnp.bfloat16), wide((plan.devices, 128), jnp.int32)],
        [SMEM, VMEM, VMEM, VMEM],
        [pltpu.VMEM((rows, width), jnp.bfloat16)],
        2 * slots * rows * width,
        3 * rows * width * 2,
    )(run_len, clusters, ranks, embeddings)
    groups = exchange(groups)
    arrived = exchange(outgoing)
    (own,) = call(
        sort_kernel, plan, [wide((rows, width), jnp.bfloat16)], [SMEM, VMEM],
        moved=3 * rows * width * 2,
    )(groups, arrived)

    def swap(block):
        pairs = [
            (i * plan.run + r, (i ^ 1) * plan.run + r)
            for i in range(plan.ingest)
            for r in range(plan.run)
        ]
        return lax.ppermute(block, AXES, pairs)

    mate = swap(own)
    behind = []
    for distance, chips in enumerate(plan.links()):
        if distance == 0:
            continue
        pairs = [
            (plan.device(i, 2 * chip + core), plan.device(i, 2 * (chip + distance) + core))
            for i in range(plan.ingest)
            for chip in chips
            for core in range(2)
        ]
        moved = lax.ppermute(own, AXES, pairs)
        behind += [moved, swap(moved)]
    place = jnp.stack([lax.axis_index("ingest"), lax.axis_index("run")]).astype(jnp.int32)
    (replies,) = call(
        best_kernel,
        plan,
        [wide((plan.devices, 128), jnp.float32)],
        [SMEM, SMEM, SMEM] + [VMEM] * (2 + len(behind)),
        [pltpu.VMEM((1, rows), jnp.float32), pltpu.VMEM((rows // plan.cap, 128), jnp.float32)],
        2 * rows * rows * width * 3,
        4 * rows * width * 2,
    )(run_len, place, groups, own, mate, *behind)
    returned = exchange(replies)
    (best,) = call(
        unpack_kernel, plan, [wide((1, rows), jnp.float32)], [SMEM, VMEM, VMEM, VMEM],
        moved=4 * rows * 4,
    )(run_len, clusters, ranks, returned)
    return best.reshape(rows)


def solution(mesh):
    return jax.shard_map(
        local,
        mesh=mesh,
        in_specs=(P(AXES, None), P(AXES), P(AXES), P()),
        out_specs=P(AXES),
        check_vma=False,
    )
```

```python
import functools

import jax
import jax.numpy as jnp
from jax import lax
from jax.experimental import pallas as pl
from jax.experimental.pallas import tpu as pltpu
from jax.sharding import PartitionSpec as P

EPSILON = 1e-06
AXES = ("ingest", "run")
TILE = 256
CHUNKS = 2
MEMORY = 60 * 1024 * 1024


class Plan:
    def __init__(self, ingest, run, clusters, rows, features):
        self.ingest, self.run, self.clusters, self.rows = ingest, run, clusters, rows
        self.devices = ingest * run
        self.per_group = clusters // ingest
        self.cap = 2 * rows // self.devices
        self.reach = min(8, run // 2)
        self.width = run // ingest
        self.pairs = run // 2
        self.blocks = rows // self.cap
        self.layers, self.lanes = ingest, ingest * self.width
        self.slice = self.cap // self.lanes
        self.part = self.blocks * self.slice
        self.chunks = tuple(features // CHUNKS for _ in range(CHUNKS))
        mean = rows // self.layers
        self.room = mean + mean // 8
        self.stride = -(-self.room // 128) * 128

    def staged(self):
        powers = all(n & (n - 1) == 0 for n in (self.layers, self.lanes, self.width))
        return (
            powers
            and self.cap % (8 * self.lanes) == 0
            and self.part == 128
            and self.room % 16 == 0
            and min(self.chunks) >= self.stride
            and self.links()[1:] == [[0]]
        )

    def device(self, group, slot):
        core, chip = slot % 2, slot // 2
        column, place = chip // self.width, chip % self.width
        odd = column % 2
        place = place + odd * (self.width - 1 - 2 * place)
        return (2 * column + core) * self.run + group * self.width + place

    def slot(self, device_ingest, device_run):
        core, column = device_ingest % 2, device_ingest // 2
        place = device_run % self.width
        place = place + (column % 2) * (self.width - 1 - 2 * place)
        return device_run // self.width, 2 * (column * self.width + place) + core

    def splits(self):
        def parts(total, count, top):
            if count == 0:
                if total == 0:
                    yield ()
                return
            for first in range(min(top, total), 0, -1):
                for rest in parts(total - first, count - 1, first):
                    yield (first, *rest)

        return list(parts(self.pairs, self.per_group, self.reach // 2))

    def links(self):
        found = [set() for _ in range(self.reach // 2)]
        for split in self.splits():
            begin = 0
            for length in split:
                for first in range(length):
                    for second in range(first + 1, length):
                        found[second - first].add(begin + first)
                begin += length
        return [sorted(chips) for chips in found]


def cluster_starts(plan, run_len_ref):
    starts = []
    for cluster in range(plan.clusters):
        base = cluster // plan.per_group * plan.per_group
        mine = run_len_ref[cluster]
        total = jnp.int32(0)
        for other in range(base, base + plan.per_group):
            if other == cluster:
                continue
            theirs = run_len_ref[other]
            ahead = (theirs >= mine) if other < cluster else (theirs > mine)
            total = total + jnp.where(ahead, theirs, 0)
        starts.append(total)
    return starts


def row_slot(plan, run_len_ref, cluster, rank):
    starts = cluster_starts(plan, run_len_ref)
    begin = jnp.zeros_like(cluster)
    group = jnp.zeros_like(cluster)
    for number, start in enumerate(starts):
        here = cluster == number
        begin = jnp.where(here, start, begin)
        group = jnp.where(here, number // plan.per_group, group)
    return group, begin + rank // plan.rows, rank % plan.rows


def row_owner(plan, run_len_ref, cluster, rank):
    group, slot, within = row_slot(plan, run_len_ref, cluster, rank)
    return plan.device(group, slot), within


def pack_kernel(plan, run_len_ref, cluster_ref, rank_ref, rows_ref, out_ref, group_ref, unit_ref):
    step = 128

    @pl.loop(0, plan.rows // step)
    def _(number):
        here = pl.ds(pl.multiple_of(number * step, step), step)
        widened = rows_ref[here, :].astype(jnp.float32)
        total = jnp.sum(widened * widened, axis=1, keepdims=True) + EPSILON
        unit_ref[here, :] = (widened * lax.rsqrt(total)).astype(jnp.bfloat16)

    owner, within = row_owner(plan, run_len_ref, cluster_ref[...], rank_ref[...])
    number = lax.broadcasted_iota(jnp.int32, (plan.devices, plan.rows), 0)
    group = jnp.max(
        jnp.where(number == owner, within // plan.cap + 1, 0), axis=1, keepdims=True
    )
    group_ref[...] = jnp.broadcast_to(group, group_ref.shape)
    position = owner * plan.cap + within % plan.cap

    @pl.loop(0, plan.devices * plan.cap // TILE)
    def _(tile):
        row = lax.broadcasted_iota(jnp.int32, (TILE, plan.rows), 0) + tile * TILE
        chosen = jnp.where(row == position, 1.0, 0.0).astype(jnp.bfloat16)
        moved = jnp.dot(chosen, unit_ref[...], preferred_element_type=jnp.float32)
        here = pl.ds(pl.multiple_of(tile * TILE, TILE), TILE)
        out_ref[here, :] = moved.astype(jnp.bfloat16)


def sort_kernel(plan, group_ref, arrived_ref, out_ref):
    for source in range(plan.devices):
        group = group_ref[source, 0]

        @pl.when(group > 0)
        def _():
            here = pl.ds(pl.multiple_of((group - 1) * plan.cap, plan.cap), plan.cap)
            out_ref[here, :] = arrived_ref[source * plan.cap : (source + 1) * plan.cap, :]


def block_best(keys_ref, queries_ref, best_ref):
    rows = keys_ref.shape[0]

    @pl.loop(0, rows // TILE)
    def _(tile):
        keys = keys_ref[pl.ds(pl.multiple_of(tile * TILE, TILE), TILE), :]
        scores = lax.dot_general(
            keys, queries_ref[...], (((1,), (1,)), ((), ())), preferred_element_type=jnp.float32
        )
        best_ref[...] = jnp.maximum(best_ref[...], jnp.max(scores, axis=0, keepdims=True))


def triangle_best(rows_ref, best_ref):
    rows = rows_ref.shape[0]
    for first in range(0, rows, TILE):
        scores = lax.dot_general(
            rows_ref[first : first + TILE, :],
            rows_ref[first:, :],
            (((1,), (1,)), ((), ())),
            preferred_element_type=jnp.float32,
        )
        key = lax.broadcasted_iota(jnp.int32, (TILE, TILE), 0)
        query = lax.broadcasted_iota(jnp.int32, (TILE, TILE), 1)
        corner = jnp.max(
            jnp.where(key < query, scores[:, :TILE], -2.0), axis=0, keepdims=True
        )
        here = slice(first, first + TILE)
        best_ref[:, here] = jnp.maximum(best_ref[:, here], corner)
        if first + TILE < rows:
            rest = jnp.max(scores[:, TILE:], axis=0, keepdims=True)
            there = slice(first + TILE, rows)
            best_ref[:, there] = jnp.maximum(best_ref[:, there], rest)


def best_kernel(plan, run_len_ref, place_ref, group_ref, own_ref, mate_ref, *rest):
    behind, (out_ref, best_ref, blocks_ref) = rest[:-3], rest[-3:]
    group, slot = plan.slot(place_ref[0], place_ref[1])
    begin = jnp.int32(0)
    for number, start in enumerate(cluster_starts(plan, run_len_ref)):
        here = (number // plan.per_group == group) & (start <= slot)
        begin = jnp.where(here, jnp.maximum(begin, start), begin)
    best_ref[...] = jnp.full(best_ref.shape, -1.0, jnp.float32)
    triangle_best(own_ref, best_ref)

    @pl.when(slot % 2 == 1)
    def _():
        block_best(mate_ref, own_ref, best_ref)

    for distance in range(1, plan.reach // 2):
        first, second = behind[2 * distance - 2], behind[2 * distance - 1]

        @pl.when(slot - slot % 2 - 2 * distance >= begin)
        def _():
            block_best(first, own_ref, best_ref)
            block_best(second, own_ref, best_ref)

    for number in range(plan.rows // plan.cap):
        part = best_ref[:, number * plan.cap : (number + 1) * plan.cap]
        blocks_ref[number : number + 1, : plan.cap] = part
    for source in range(plan.devices):
        chosen = jnp.maximum(group_ref[source, 0] - 1, 0)
        out_ref[source : source + 1, :] = blocks_ref[pl.ds(chosen, 1), :]


def unpack_kernel(plan, run_len_ref, cluster_ref, rank_ref, reply_ref, out_ref):
    owner, within = row_owner(plan, run_len_ref, cluster_ref[...], rank_ref[...])
    number = lax.broadcasted_iota(jnp.int32, (plan.devices, plan.rows), 0)
    chosen = jnp.where(number == owner, 1.0, 0.0)
    columns = lax.dot_general(
        reply_ref[:, : plan.cap],
        chosen,
        (((0,), (0,)), ((), ())),
        precision=lax.Precision.HIGHEST,
        preferred_element_type=jnp.float32,
    )
    lane = lax.broadcasted_iota(jnp.int32, (plan.cap, plan.rows), 0)
    out_ref[...] = jnp.sum(
        jnp.where(lane == within % plan.cap, columns, 0.0), axis=0, keepdims=True
    )


def lane_of(plan, slot):
    device = plan.device(0, slot)
    return device // plan.run * plan.width + device % plan.run


def lane_device(plan, layer, lane):
    return lane // plan.width * plan.run + layer * plan.width + lane % plan.width


def my_lane(plan):
    run = lax.axis_index("run")
    return lax.axis_index("ingest") * plan.width + run % plan.width, run // plan.width


def spread_kernel(plan, run_len_ref, cluster_ref, rank_ref, rows_ref, *rest):
    outs, (unit_ref,) = rest[:-1], rest[-1:]
    step = 128

    @pl.loop(0, plan.rows // step)
    def _(number):
        here = pl.ds(pl.multiple_of(number * step, step), step)
        widened = rows_ref[here, :].astype(jnp.float32)
        total = jnp.sum(widened * widened, axis=1, keepdims=True) + EPSILON
        unit_ref[here, :] = (widened * lax.rsqrt(total)).astype(jnp.bfloat16)

    lane, _ = my_lane(plan)
    group, slot, within = row_slot(plan, run_len_ref, cluster_ref[...], rank_ref[...])
    owner = group * plan.run + slot
    number = lax.broadcasted_iota(jnp.int32, (plan.devices, plan.rows), 0)
    member = number == owner
    block = jnp.max(jnp.where(member, within // plan.cap + 1, 0), axis=1, keepdims=True)
    present = jnp.where(block > 0, 1.0, 0.0)
    before = lax.broadcasted_iota(jnp.int32, (plan.devices, plan.devices), 0) > (
        lax.broadcasted_iota(jnp.int32, (plan.devices, plan.devices), 1)
    )
    order = jnp.dot(
        jnp.where(before, 1.0, 0.0),
        jnp.broadcast_to(present, (plan.devices, 128)),
        preferred_element_type=jnp.float32,
    )
    mine = jnp.sum(jnp.where(member, order[:, :1], 0.0), axis=0, keepdims=True)
    residue = within % plan.cap
    target = (
        (residue // plan.slice ^ lane) * plan.part
        + mine.astype(jnp.int32) * plan.slice
        + residue % plan.slice
    )
    per = len(outs) // len(plan.chunks)
    tile = 2 * plan.part

    for pair in range(plan.lanes // 2):
        row = lax.broadcasted_iota(jnp.int32, (tile, plan.rows), 0) + pair * tile
        chosen = jnp.where(row == target, 1.0, 0.0).astype(jnp.bfloat16)
        moved = jnp.dot(chosen, unit_ref[...], preferred_element_type=jnp.float32)
        moved = moved.astype(jnp.bfloat16)
        for half in range(2):
            first = 0
            for chunk, width in enumerate(plan.chunks):
                outs[chunk * per + 2 * pair + half][: plan.part, :] = moved[
                    half * plan.part : (half + 1) * plan.part, first : first + width
                ]
                first += width

    place = lax.broadcasted_iota(jnp.int32, (plan.devices, plan.part), 1) // plan.slice
    here = (place.astype(jnp.float32) == order[:, :1]) & (block > 0)
    who = lax.broadcasted_iota(jnp.int32, (plan.devices, plan.part), 0)
    owners = jnp.sum(jnp.where(here, who, 0), axis=0, keepdims=True)
    blocks = jnp.sum(jnp.where(here, block - 1, 0), axis=0, keepdims=True)
    line = lax.broadcasted_iota(jnp.int32, (16, plan.part), 0)
    table = jnp.where(line == 0, owners, jnp.where(line == 1, blocks, 0))
    for out in outs[:per]:
        out[plan.part :, : plan.part] = table.astype(jnp.float32).astype(jnp.bfloat16)


def permute_into(target, first, inputs_ref, outs, room, stride):
    columns = inputs_ref.shape[0]
    for number, out in enumerate(outs):
        row = lax.broadcasted_iota(jnp.int32, (room, columns), 0) + first + number * stride
        chosen = jnp.where(row == target, 1.0, 0.0).astype(jnp.bfloat16)
        moved = jnp.dot(chosen, inputs_ref[...], preferred_element_type=jnp.float32)
        out[:room, :] = moved.astype(jnp.bfloat16)


def route_kernel(plan, *refs):
    ins, rest = refs[: plan.lanes], refs[plan.lanes :]
    outs, (target_ref, inputs_ref, owner_ref, block_ref, value_ref) = rest[:-5], rest[-5:]
    _, layer = my_lane(plan)
    for number, part in enumerate(ins):
        inputs_ref[number * plan.part : (number + 1) * plan.part, :] = part[: plan.part, :]
        table = part[plan.part :, : plan.part].astype(jnp.float32)
        owner_ref[number : number + 1, :] = table[0:1, :].astype(jnp.int32)
        block_ref[number : number + 1, :] = table[1:2, :].astype(jnp.int32)
    owner = owner_ref[...]
    shape = (plan.part, plan.part)
    earlier = lax.broadcasted_iota(jnp.int32, shape, 0) < lax.broadcasted_iota(jnp.int32, shape, 1)
    earlier = jnp.where(earlier, 1.0, 0.0)
    ones = jnp.ones(shape, jnp.float32)
    shape = (plan.lanes, plan.lanes)
    above = lax.broadcasted_iota(jnp.int32, shape, 0) > lax.broadcasted_iota(jnp.int32, shape, 1)
    above = jnp.where(above, 1.0, 0.0)
    target = jnp.zeros(owner.shape, jnp.int32)
    most = jnp.float32(0.0)
    for other in range(plan.layers):
        chosen = owner // plan.run == other
        marks = jnp.where(chosen, 1.0, 0.0)
        lines = jnp.dot(marks, ones, preferred_element_type=jnp.float32)
        count = jnp.dot(marks, earlier, preferred_element_type=jnp.float32) + jnp.dot(
            above, lines, preferred_element_type=jnp.float32
        )
        count = count.astype(jnp.int32)
        there = jnp.where(count < plan.room, (layer ^ other) * plan.stride + count, -1)
        target = jnp.where(chosen, there, target)
        most = jnp.maximum(most, jnp.sum(marks))
    full = jnp.where(most > plan.room, 1.0, 0.0)
    value = owner % plan.run * plan.blocks + block_ref[...] + 1
    for number in range(plan.lanes):
        here = slice(number * plan.part, (number + 1) * plan.part)
        target_ref[:, here] = target[number : number + 1, :]
        value_ref[:, here] = value[number : number + 1, :].astype(jnp.float32)
    target = target_ref[...]
    values = jnp.broadcast_to(value_ref[...], (8, plan.rows)).astype(jnp.bfloat16)
    for number, out in enumerate(outs):
        row = lax.broadcasted_iota(jnp.int32, (plan.stride, plan.rows), 0) + number * plan.stride
        chosen = jnp.where(row == target, 1.0, 0.0).astype(jnp.bfloat16)
        moved = jnp.dot(
            chosen[: plan.room, :], inputs_ref[...], preferred_element_type=jnp.float32
        )
        out[: plan.room, :] = moved.astype(jnp.bfloat16)
        listed = lax.dot_general(
            values, chosen, (((1,), (1,)), ((), ())), preferred_element_type=jnp.float32
        )
        line = lax.broadcasted_iota(jnp.int32, (16, plan.stride), 0)
        table = jnp.where(line == 0, listed[0:1, :], jnp.where(line == 1, full, 0.0))
        out[plan.room :, : plan.stride] = table.astype(jnp.bfloat16)


def route_more_kernel(plan, target_ref, *refs):
    ins, outs, inputs_ref = refs[: plan.lanes], refs[plan.lanes : -1], refs[-1]
    for number, part in enumerate(ins):
        inputs_ref[number * plan.part : (number + 1) * plan.part, :] = part[...]
    permute_into(target_ref[...], 0, inputs_ref, outs, plan.room, plan.stride)


def gather_rows(plan, ins, inputs_ref):
    for number, part in enumerate(ins):
        first = number * plan.stride
        inputs_ref[first : first + plan.room, :] = part[: plan.room, :]
        if plan.stride > plan.room:
            inputs_ref[first + plan.room : first + plan.stride, :] = jnp.zeros(
                (plan.stride - plan.room, inputs_ref.shape[1]), jnp.bfloat16
            )


def sort_parts(plan, target, inputs_ref, outs, ahead_ref, sorted_ref):
    tile = 2 * plan.part
    for pair in range(plan.lanes // 2):
        row = lax.broadcasted_iota(jnp.int32, (tile, inputs_ref.shape[0]), 0) + pair * tile
        chosen = jnp.where(row == target, 1.0, 0.0).astype(jnp.bfloat16)
        moved = jnp.dot(chosen, inputs_ref[...], preferred_element_type=jnp.float32)
        moved = moved.astype(jnp.bfloat16)
        sorted_ref[pair * tile : (pair + 1) * tile, :] = moved
        outs[2 * pair][...] = moved[: plan.part, :]
        outs[2 * pair + 1][...] = moved[plan.part :, :]
    lane, _ = my_lane(plan)
    for slot in range(2):
        part = lane_of(plan, slot) ^ lane
        ahead_ref[slot * plan.part : (slot + 1) * plan.part, :] = sorted_ref[
            pl.ds(pl.multiple_of(part * plan.part, plan.part), plan.part), :
        ]


def deliver_kernel(plan, *refs):
    ins, rest = refs[: plan.layers], refs[plan.layers :]
    outs, (ahead_ref, target_ref, full_ref, inputs_ref, sorted_ref) = rest[:-5], rest[-5:]
    lane, _ = my_lane(plan)
    gather_rows(plan, ins, inputs_ref)
    full = jnp.zeros((8, 128), jnp.float32)
    for number, part in enumerate(ins):
        table = part[plan.room :, : plan.stride].astype(jnp.float32)
        value = table[0:1, :].astype(jnp.int32) - 1
        full = jnp.maximum(full, jnp.broadcast_to(table[1:2, :128], (8, 128)))
        slot = value // plan.blocks
        within = lax.broadcasted_iota(jnp.int32, value.shape, 1) % plan.slice
        target = (lane_of(plan, slot) ^ lane) * plan.part + value % plan.blocks * plan.slice + within
        target_ref[:, number * plan.stride : (number + 1) * plan.stride] = jnp.where(
            value >= 0, target, -1
        )
    full_ref[...] = full.astype(jnp.int32)
    sort_parts(plan, target_ref[...], inputs_ref, outs, ahead_ref, sorted_ref)


def deliver_more_kernel(plan, target_ref, *refs):
    ins, rest = refs[: plan.layers], refs[plan.layers :]
    outs, (ahead_ref, inputs_ref, sorted_ref) = rest[:-3], rest[-3:]
    gather_rows(plan, ins, inputs_ref)
    sort_parts(plan, target_ref[...], inputs_ref, outs, ahead_ref, sorted_ref)


def join_kernel(plan, *refs):
    ins, (own_ref, behind_ref) = refs[:-2], refs[-2:]
    for number, part in enumerate(ins[: plan.lanes]):
        own_ref[number * plan.part : (number + 1) * plan.part, :] = part[...]
    for number, part in enumerate(ins[plan.lanes :]):
        behind_ref[number * 2 * plan.part : (number + 1) * 2 * plan.part, :] = part[...]


def wide_best(keys, queries_ref, best_ref):
    @pl.loop(0, keys[0].shape[0] // TILE)
    def _(tile):
        here = pl.ds(pl.multiple_of(tile * TILE, TILE), TILE)
        block = jnp.concatenate([part[here, :] for part in keys], axis=1)
        scores = lax.dot_general(
            block, queries_ref[...], (((1,), (1,)), ((), ())), preferred_element_type=jnp.float32
        )
        best_ref[...] = jnp.maximum(best_ref[...], jnp.max(scores, axis=0, keepdims=True))


def staged_best_kernel(plan, run_len_ref, *refs):
    count = len(plan.chunks)
    own, mate, behind, far = (refs[n * count : (n + 1) * count] for n in range(4))
    out_ref, best_ref, queries_ref, lines_ref = refs[4 * count :]
    ingest, run = lax.axis_index("ingest"), lax.axis_index("run")
    lane, _ = my_lane(plan)
    group, slot = plan.slot(ingest, run)
    begin = jnp.int32(0)
    for number, start in enumerate(cluster_starts(plan, run_len_ref)):
        here = (number // plan.per_group == group) & (start <= slot)
        begin = jnp.where(here, jnp.maximum(begin, start), begin)
    first = 0
    for part in own:
        queries_ref[:, first : first + part.shape[1]] = part[...]
        first += part.shape[1]

    def slots(row):
        block = row // plan.slice % plan.blocks
        return block * plan.cap + (row // plan.part ^ lane) * plan.slice + row % plan.slice

    best_ref[...] = jnp.full(best_ref.shape, -1.0, jnp.float32)
    query = slots(lax.broadcasted_iota(jnp.int32, (1, plan.rows), 1))

    @pl.loop(0, plan.rows // TILE)
    def _(tile):
        key = slots(lax.broadcasted_iota(jnp.int32, (TILE, 1), 0) + tile * TILE)
        block = queries_ref[pl.ds(pl.multiple_of(tile * TILE, TILE), TILE), :]
        scores = lax.dot_general(
            block, queries_ref[...], (((1,), (1,)), ((), ())), preferred_element_type=jnp.float32
        )
        top = jnp.max(jnp.where(key < query, scores, -2.0), axis=0, keepdims=True)
        best_ref[...] = jnp.maximum(best_ref[...], top)

    @pl.when(slot % 2 == 1)
    def _():
        wide_best(mate, queries_ref, best_ref)

    @pl.when(slot - slot % 2 - 2 >= begin)
    def _():
        wide_best(behind, queries_ref, best_ref)
        wide_best(far, queries_ref, best_ref)

    for number in range(plan.lanes):
        lines_ref[number : number + 1, :] = best_ref[
            :, number * plan.part : (number + 1) * plan.part
        ]
    for device in range(plan.devices):
        out_ref[device] = lines_ref[...]


def staged_unpack_kernel(plan, run_len_ref, cluster_ref, rank_ref, reply_ref, out_ref):
    group, slot, within = row_slot(plan, run_len_ref, cluster_ref[...], rank_ref[...])
    residue = within % plan.cap
    line = plan.device(group, slot) * plan.lanes + (residue // plan.slice ^ lane_of(plan, slot))
    column = within // plan.cap * plan.slice + residue % plan.slice
    number = lax.broadcasted_iota(jnp.int32, (plan.devices * plan.lanes, plan.rows), 0)
    columns = lax.dot_general(
        reply_ref[...],
        jnp.where(number == line, 1.0, 0.0),
        (((0,), (0,)), ((), ())),
        precision=lax.Precision.HIGHEST,
        preferred_element_type=jnp.float32,
    )
    place = lax.broadcasted_iota(jnp.int32, (plan.part, plan.rows), 0)
    out_ref[...] = jnp.sum(jnp.where(place == column, columns, 0.0), axis=0, keepdims=True)


SMEM = pl.BlockSpec(memory_space=pltpu.SMEM)
VMEM = pl.BlockSpec(memory_space=pltpu.VMEM)


def call(kernel, plan, shapes, specs, scratch=(), flops=0, moved=0):
    return pl.pallas_call(
        functools.partial(kernel, plan),
        out_shape=shapes,
        in_specs=specs,
        out_specs=[VMEM] * len(shapes),
        scratch_shapes=scratch,
        compiler_params=pltpu.CompilerParams(vmem_limit_bytes=MEMORY),
        cost_estimate=pl.CostEstimate(flops=flops, bytes_accessed=moved, transcendentals=0),
    )


def exchange(block):
    return lax.all_to_all(block, AXES, split_axis=0, concat_axis=0, tiled=True)


def direct(plan, embeddings, clusters, ranks, run_len):
    rows, width = embeddings.shape
    slots = plan.devices * plan.cap
    wide = jax.ShapeDtypeStruct
    outgoing, groups = call(
        pack_kernel,
        plan,
        [wide((slots, width), jnp.bfloat16), wide((plan.devices, 128), jnp.int32)],
        [SMEM, VMEM, VMEM, VMEM],
        [pltpu.VMEM((rows, width), jnp.bfloat16)],
        2 * slots * rows * width,
        3 * rows * width * 2,
    )(run_len, clusters, ranks, embeddings)
    groups = exchange(groups)
    arrived = exchange(outgoing)
    (own,) = call(
        sort_kernel, plan, [wide((rows, width), jnp.bfloat16)], [SMEM, VMEM],
        moved=3 * rows * width * 2,
    )(groups, arrived)

    def swap(block):
        pairs = [
            (i * plan.run + r, (i ^ 1) * plan.run + r)
            for i in range(plan.ingest)
            for r in range(plan.run)
        ]
        return lax.ppermute(block, AXES, pairs)

    mate = swap(own)
    behind = []
    for distance, chips in enumerate(plan.links()):
        if distance == 0:
            continue
        pairs = [
            (plan.device(i, 2 * chip + core), plan.device(i, 2 * (chip + distance) + core))
            for i in range(plan.ingest)
            for chip in chips
            for core in range(2)
        ]
        moved = lax.ppermute(own, AXES, pairs)
        behind += [moved, swap(moved)]
    place = jnp.stack([lax.axis_index("ingest"), lax.axis_index("run")]).astype(jnp.int32)
    (replies,) = call(
        best_kernel,
        plan,
        [wide((plan.devices, 128), jnp.float32)],
        [SMEM, SMEM, SMEM] + [VMEM] * (2 + len(behind)),
        [pltpu.VMEM((1, rows), jnp.float32), pltpu.VMEM((rows // plan.cap, 128), jnp.float32)],
        2 * rows * rows * width * 3,
        4 * rows * width * 2,
    )(run_len, place, groups, own, mate, *behind)
    returned = exchange(replies)
    (best,) = call(
        unpack_kernel, plan, [wide((1, rows), jnp.float32)], [SMEM, VMEM, VMEM, VMEM],
        moved=4 * rows * 4,
    )(run_len, clusters, ranks, returned)
    return best


def staged(plan, embeddings, clusters, ranks, run_len):
    rows, width = embeddings.shape
    wide = jax.ShapeDtypeStruct
    half = jnp.bfloat16
    lanes, layers = range(plan.lanes), range(plan.layers)

    def along_lanes(block, change):
        pairs = [
            (lane_device(plan, layer, lane), lane_device(plan, layer, lane ^ change))
            for layer in layers
            for lane in lanes
        ]
        return lax.ppermute(block, AXES, pairs)

    def along_layers(block, change):
        pairs = [
            (lane_device(plan, layer, lane), lane_device(plan, layer ^ change, lane))
            for layer in layers
            for lane in lanes
        ]
        return lax.ppermute(block, AXES, pairs)

    def chip_to_chip(block, routes):
        pairs = [
            (plan.device(layer, 2 * first + core), plan.device(layer, 2 * second + core))
            for layer in layers
            for first, second in routes
            for core in range(2)
        ]
        return lax.ppermute(block, AXES, pairs)

    far_first = sorted(lanes, key=lambda change: -(change & 1) - (change // plan.width // 2))

    def swap_lanes(blocks):
        return [
            along_lanes(blocks[change], change) if change else blocks[0] for change in far_first
        ], far_first

    def by_change(moved):
        arrays, order = moved
        return [arrays[order.index(change)] for change in lanes]

    sizes = [plan.part + 16] + [plan.part] * (len(plan.chunks) - 1)
    spread = call(
        spread_kernel,
        plan,
        [wide((size, f), half) for size, f in zip(sizes, plan.chunks) for _ in lanes],
        [SMEM, VMEM, VMEM, VMEM],
        [pltpu.VMEM((rows, width), half)],
        2 * rows * rows * width,
        3 * rows * width * 2,
    )(run_len, clusters, ranks, embeddings)
    owns, mates, behinds, fars = [], [], [], []
    table = targets = full = None
    for chunk, f in enumerate(plan.chunks):
        spec = dict(flops=2 * rows * rows * f, moved=3 * rows * f * 2)
        parts = by_change(swap_lanes(spread[chunk * plan.lanes : (chunk + 1) * plan.lanes]))
        rooms = [wide((plan.room + (0 if chunk else 16), f), half) for _ in layers]
        inputs = pltpu.VMEM((rows, f), half)
        if chunk == 0:
            *routed, table = call(
                route_kernel,
                plan,
                [*rooms, wide((1, rows), jnp.int32)],
                [VMEM] * plan.lanes,
                [
                    inputs,
                    pltpu.VMEM((plan.lanes, plan.part), jnp.int32),
                    pltpu.VMEM((plan.lanes, plan.part), jnp.int32),
                    pltpu.VMEM((1, rows), jnp.float32),
                ],
                **spec,
            )(*parts)
        else:
            routed = call(
                route_more_kernel, plan, rooms, [VMEM] * (1 + plan.lanes), [inputs], **spec
            )(table, *parts)
        moved = {change: along_layers(routed[change], change) for change in reversed(layers[1:])}
        arrived = [routed[0]] + [moved[change] for change in layers[1:]]
        shapes = [wide((plan.part, f), half) for _ in lanes] + [wide((2 * plan.part, f), half)]
        scratch = [pltpu.VMEM((plan.layers * plan.stride, f), half), inputs]
        if chunk == 0:
            *parts, ahead, targets, full = call(
                deliver_kernel,
                plan,
                [
                    *shapes,
                    wide((1, plan.layers * plan.stride), jnp.int32),
                    wide((8, 128), jnp.int32),
                ],
                [VMEM] * plan.layers,
                scratch,
                **spec,
            )(*arrived)
        else:
            *parts, ahead = call(
                deliver_more_kernel, plan, shapes, [VMEM] * (1 + plan.layers), scratch, **spec
            )(targets, *arrived)
        near = chip_to_chip(ahead, [(0, 1), (3, 2)])
        parts = by_change(swap_lanes(parts))
        side = chip_to_chip(ahead, [(2, 1)])
        corner = chip_to_chip(near, [(2, 1)])
        own, behind = call(
            join_kernel,
            plan,
            [wide((rows, f), half)] * 2,
            [VMEM] * (plan.lanes + 4),
            moved=4 * rows * f * 2,
        )(*parts, ahead, near, side, corner)
        owns.append(own)
        behinds.append(behind)
        mates.append(along_lanes(own, plan.width))
        fars.append(along_lanes(behind, plan.width))
    (replies,) = call(
        staged_best_kernel,
        plan,
        [wide((plan.devices, plan.lanes, 128), jnp.float32)],
        [SMEM] + [VMEM] * (4 * len(plan.chunks)),
        [
            pltpu.VMEM((1, rows), jnp.float32),
            pltpu.VMEM((rows, width), half),
            pltpu.VMEM((plan.lanes, 128), jnp.float32),
        ],
        2 * rows * rows * width * 3,
        4 * rows * width * 2,
    )(run_len, *owns, *mates, *behinds, *fars)
    returned = exchange(replies).reshape(plan.devices * plan.lanes, 128)
    (best,) = call(
        staged_unpack_kernel,
        plan,
        [wide((1, rows), jnp.float32)],
        [SMEM, VMEM, VMEM, VMEM],
        moved=4 * rows * 4,
    )(run_len, clusters, ranks, returned)
    return best, full[0, 0]


def local(embeddings, cluster_id, rank, run_len):
    rows, width = embeddings.shape
    plan = Plan(lax.axis_size("ingest"), lax.axis_size("run"), run_len.shape[0], rows, width)
    given = (embeddings, cluster_id.reshape(1, rows), rank.reshape(1, rows), run_len)
    if not plan.staged():
        return direct(plan, *given).reshape(rows)
    best, full = staged(plan, *given)
    best = lax.cond(full > 0, lambda: direct(plan, *given), lambda: best)
    return best.reshape(rows)


def solution(mesh):
    return jax.shard_map(
        local,
        mesh=mesh,
        in_specs=(P(AXES, None), P(AXES), P(AXES), P()),
        out_specs=P(AXES),
        check_vma=False,
    )
```

```python
import functools

import jax
import jax.numpy as jnp
from jax import lax
from jax.experimental import pallas as pl
from jax.experimental.pallas import tpu as pltpu
from jax.sharding import PartitionSpec as P

EPSILON = 1e-06
AXES = ("ingest", "run")
TILE = 256
CHUNKS = 2
MIB = 1024 * 1024


class Plan:
    def __init__(self, ingest, run, clusters, rows, features):
        self.ingest, self.run, self.clusters, self.rows = ingest, run, clusters, rows
        self.devices = ingest * run
        self.per_group = clusters // ingest
        self.cap = 2 * rows // self.devices
        self.reach = min(8, run // 2)
        self.width = run // ingest
        self.pairs = run // 2
        self.blocks = rows // self.cap
        self.layers, self.lanes = ingest, ingest * self.width
        self.slice = self.cap // self.lanes
        self.part = self.blocks * self.slice
        self.chunks = tuple(features // CHUNKS for _ in range(CHUNKS))
        mean = rows // self.layers
        self.room = mean + mean // 8
        self.stride = -(-self.room // 128) * 128

    def staged(self):
        powers = all(n & (n - 1) == 0 for n in (self.layers, self.lanes, self.width))
        return (
            powers
            and self.cap % (8 * self.lanes) == 0
            and self.part == 128
            and self.room % 16 == 0
            and min(self.chunks) >= self.stride
            and self.links()[1:] == [[0]]
        )

    def device(self, group, slot):
        core, chip = slot % 2, slot // 2
        column, place = chip // self.width, chip % self.width
        odd = column % 2
        place = place + odd * (self.width - 1 - 2 * place)
        return (2 * column + core) * self.run + group * self.width + place

    def slot(self, device_ingest, device_run):
        core, column = device_ingest % 2, device_ingest // 2
        place = device_run % self.width
        place = place + (column % 2) * (self.width - 1 - 2 * place)
        return device_run // self.width, 2 * (column * self.width + place) + core

    def splits(self):
        def parts(total, count, top):
            if count == 0:
                if total == 0:
                    yield ()
                return
            for first in range(min(top, total), 0, -1):
                for rest in parts(total - first, count - 1, first):
                    yield (first, *rest)

        return list(parts(self.pairs, self.per_group, self.reach // 2))

    def links(self):
        found = [set() for _ in range(self.reach // 2)]
        for split in self.splits():
            begin = 0
            for length in split:
                for first in range(length):
                    for second in range(first + 1, length):
                        found[second - first].add(begin + first)
                begin += length
        return [sorted(chips) for chips in found]


def cluster_starts(plan, run_len_ref):
    starts = []
    for cluster in range(plan.clusters):
        base = cluster // plan.per_group * plan.per_group
        mine = run_len_ref[cluster]
        total = jnp.int32(0)
        for other in range(base, base + plan.per_group):
            if other == cluster:
                continue
            theirs = run_len_ref[other]
            ahead = (theirs >= mine) if other < cluster else (theirs > mine)
            total = total + jnp.where(ahead, theirs, 0)
        starts.append(total)
    return starts


def row_slot(plan, run_len_ref, cluster, rank):
    starts = cluster_starts(plan, run_len_ref)
    begin = jnp.zeros_like(cluster)
    group = jnp.zeros_like(cluster)
    for number, start in enumerate(starts):
        here = cluster == number
        begin = jnp.where(here, start, begin)
        group = jnp.where(here, number // plan.per_group, group)
    return group, begin + rank // plan.rows, rank % plan.rows


def row_owner(plan, run_len_ref, cluster, rank):
    group, slot, within = row_slot(plan, run_len_ref, cluster, rank)
    return plan.device(group, slot), within


def pack_kernel(plan, run_len_ref, cluster_ref, rank_ref, rows_ref, out_ref, group_ref, unit_ref):
    step = 128

    @pl.loop(0, plan.rows // step)
    def _(number):
        here = pl.ds(pl.multiple_of(number * step, step), step)
        widened = rows_ref[here, :].astype(jnp.float32)
        total = jnp.sum(widened * widened, axis=1, keepdims=True) + EPSILON
        unit_ref[here, :] = (widened * lax.rsqrt(total)).astype(jnp.bfloat16)

    owner, within = row_owner(plan, run_len_ref, cluster_ref[...], rank_ref[...])
    number = lax.broadcasted_iota(jnp.int32, (plan.devices, plan.rows), 0)
    group = jnp.max(
        jnp.where(number == owner, within // plan.cap + 1, 0), axis=1, keepdims=True
    )
    group_ref[...] = jnp.broadcast_to(group, group_ref.shape)
    position = owner * plan.cap + within % plan.cap

    @pl.loop(0, plan.devices * plan.cap // TILE)
    def _(tile):
        row = lax.broadcasted_iota(jnp.int32, (TILE, plan.rows), 0) + tile * TILE
        chosen = jnp.where(row == position, 1.0, 0.0).astype(jnp.bfloat16)
        moved = jnp.dot(chosen, unit_ref[...], preferred_element_type=jnp.float32)
        here = pl.ds(pl.multiple_of(tile * TILE, TILE), TILE)
        out_ref[here, :] = moved.astype(jnp.bfloat16)


def sort_kernel(plan, group_ref, arrived_ref, out_ref):
    for source in range(plan.devices):
        group = group_ref[source, 0]

        @pl.when(group > 0)
        def _():
            here = pl.ds(pl.multiple_of((group - 1) * plan.cap, plan.cap), plan.cap)
            out_ref[here, :] = arrived_ref[source * plan.cap : (source + 1) * plan.cap, :]


def block_best(keys_ref, queries_ref, best_ref):
    rows = keys_ref.shape[0]

    @pl.loop(0, rows // TILE)
    def _(tile):
        keys = keys_ref[pl.ds(pl.multiple_of(tile * TILE, TILE), TILE), :]
        scores = lax.dot_general(
            keys, queries_ref[...], (((1,), (1,)), ((), ())), preferred_element_type=jnp.float32
        )
        best_ref[...] = jnp.maximum(best_ref[...], jnp.max(scores, axis=0, keepdims=True))


def triangle_best(rows_ref, best_ref):
    rows = rows_ref.shape[0]
    for first in range(0, rows, TILE):
        scores = lax.dot_general(
            rows_ref[first : first + TILE, :],
            rows_ref[first:, :],
            (((1,), (1,)), ((), ())),
            preferred_element_type=jnp.float32,
        )
        key = lax.broadcasted_iota(jnp.int32, (TILE, TILE), 0)
        query = lax.broadcasted_iota(jnp.int32, (TILE, TILE), 1)
        corner = jnp.max(
            jnp.where(key < query, scores[:, :TILE], -2.0), axis=0, keepdims=True
        )
        here = slice(first, first + TILE)
        best_ref[:, here] = jnp.maximum(best_ref[:, here], corner)
        if first + TILE < rows:
            rest = jnp.max(scores[:, TILE:], axis=0, keepdims=True)
            there = slice(first + TILE, rows)
            best_ref[:, there] = jnp.maximum(best_ref[:, there], rest)


def best_kernel(plan, run_len_ref, place_ref, group_ref, own_ref, mate_ref, *rest):
    behind, (out_ref, best_ref, blocks_ref) = rest[:-3], rest[-3:]
    group, slot = plan.slot(place_ref[0], place_ref[1])
    begin = jnp.int32(0)
    for number, start in enumerate(cluster_starts(plan, run_len_ref)):
        here = (number // plan.per_group == group) & (start <= slot)
        begin = jnp.where(here, jnp.maximum(begin, start), begin)
    best_ref[...] = jnp.full(best_ref.shape, -1.0, jnp.float32)
    triangle_best(own_ref, best_ref)

    @pl.when(slot % 2 == 1)
    def _():
        block_best(mate_ref, own_ref, best_ref)

    for distance in range(1, plan.reach // 2):
        first, second = behind[2 * distance - 2], behind[2 * distance - 1]

        @pl.when(slot - slot % 2 - 2 * distance >= begin)
        def _():
            block_best(first, own_ref, best_ref)
            block_best(second, own_ref, best_ref)

    for number in range(plan.rows // plan.cap):
        part = best_ref[:, number * plan.cap : (number + 1) * plan.cap]
        blocks_ref[number : number + 1, : plan.cap] = part
    for source in range(plan.devices):
        chosen = jnp.maximum(group_ref[source, 0] - 1, 0)
        out_ref[source : source + 1, :] = blocks_ref[pl.ds(chosen, 1), :]


def unpack_kernel(plan, run_len_ref, cluster_ref, rank_ref, reply_ref, out_ref):
    owner, within = row_owner(plan, run_len_ref, cluster_ref[...], rank_ref[...])
    number = lax.broadcasted_iota(jnp.int32, (plan.devices, plan.rows), 0)
    chosen = jnp.where(number == owner, 1.0, 0.0)
    columns = lax.dot_general(
        reply_ref[:, : plan.cap],
        chosen,
        (((0,), (0,)), ((), ())),
        precision=lax.Precision.HIGHEST,
        preferred_element_type=jnp.float32,
    )
    lane = lax.broadcasted_iota(jnp.int32, (plan.cap, plan.rows), 0)
    out_ref[...] = jnp.sum(
        jnp.where(lane == within % plan.cap, columns, 0.0), axis=0, keepdims=True
    )


def lane_of(plan, slot):
    device = plan.device(0, slot)
    return device // plan.run * plan.width + device % plan.run


def lane_device(plan, layer, lane):
    return lane // plan.width * plan.run + layer * plan.width + lane % plan.width


def my_lane(plan):
    run = lax.axis_index("run")
    return lax.axis_index("ingest") * plan.width + run % plan.width, run // plan.width


def spread_kernel(plan, run_len_ref, cluster_ref, rank_ref, rows_ref, *rest):
    outs, (unit_ref,) = rest[:-1], rest[-1:]
    step = 128

    @pl.loop(0, plan.rows // step)
    def _(number):
        here = pl.ds(pl.multiple_of(number * step, step), step)
        widened = rows_ref[here, :].astype(jnp.float32)
        total = jnp.sum(widened * widened, axis=1, keepdims=True) + EPSILON
        unit_ref[here, :] = (widened * lax.rsqrt(total)).astype(jnp.bfloat16)

    lane, _ = my_lane(plan)
    group, slot, within = row_slot(plan, run_len_ref, cluster_ref[...], rank_ref[...])
    owner = group * plan.run + slot
    number = lax.broadcasted_iota(jnp.int32, (plan.devices, plan.rows), 0)
    member = number == owner
    block = jnp.max(jnp.where(member, within // plan.cap + 1, 0), axis=1, keepdims=True)
    present = jnp.where(block > 0, 1.0, 0.0)
    before = lax.broadcasted_iota(jnp.int32, (plan.devices, plan.devices), 0) > (
        lax.broadcasted_iota(jnp.int32, (plan.devices, plan.devices), 1)
    )
    order = jnp.dot(
        jnp.where(before, 1.0, 0.0),
        jnp.broadcast_to(present, (plan.devices, 128)),
        preferred_element_type=jnp.float32,
    )
    mine = jnp.sum(jnp.where(member, order[:, :1], 0.0), axis=0, keepdims=True)
    residue = within % plan.cap
    target = (
        (residue // plan.slice ^ lane) * plan.part
        + mine.astype(jnp.int32) * plan.slice
        + residue % plan.slice
    )
    per = len(outs) // len(plan.chunks)
    tile = 2 * plan.part

    for pair in range(plan.lanes // 2):
        row = lax.broadcasted_iota(jnp.int32, (tile, plan.rows), 0) + pair * tile
        chosen = jnp.where(row == target, 1.0, 0.0).astype(jnp.bfloat16)
        moved = jnp.dot(chosen, unit_ref[...], preferred_element_type=jnp.float32)
        moved = moved.astype(jnp.bfloat16)
        for half in range(2):
            first = 0
            for chunk, width in enumerate(plan.chunks):
                outs[chunk * per + 2 * pair + half][: plan.part, :] = moved[
                    half * plan.part : (half + 1) * plan.part, first : first + width
                ]
                first += width

    place = lax.broadcasted_iota(jnp.int32, (plan.devices, plan.part), 1) // plan.slice
    here = (place.astype(jnp.float32) == order[:, :1]) & (block > 0)
    who = lax.broadcasted_iota(jnp.int32, (plan.devices, plan.part), 0)
    owners = jnp.sum(jnp.where(here, who, 0), axis=0, keepdims=True)
    blocks = jnp.sum(jnp.where(here, block - 1, 0), axis=0, keepdims=True)
    line = lax.broadcasted_iota(jnp.int32, (16, plan.part), 0)
    table = jnp.where(line == 0, owners, jnp.where(line == 1, blocks, 0))
    for out in outs[:per]:
        out[plan.part :, : plan.part] = table.astype(jnp.float32).astype(jnp.bfloat16)


def permute_into(target, first, inputs_ref, outs, room, stride):
    columns = inputs_ref.shape[0]
    for number, out in enumerate(outs):
        row = lax.broadcasted_iota(jnp.int32, (room, columns), 0) + first + number * stride
        chosen = jnp.where(row == target, 1.0, 0.0).astype(jnp.bfloat16)
        moved = jnp.dot(chosen, inputs_ref[...], preferred_element_type=jnp.float32)
        out[:room, :] = moved.astype(jnp.bfloat16)


def route_kernel(plan, *refs):
    ins, rest = refs[: plan.lanes], refs[plan.lanes :]
    outs, (target_ref, inputs_ref, owner_ref, block_ref, value_ref) = rest[:-5], rest[-5:]
    _, layer = my_lane(plan)
    for number, part in enumerate(ins):
        inputs_ref[number * plan.part : (number + 1) * plan.part, :] = part[: plan.part, :]
        table = part[plan.part :, : plan.part].astype(jnp.float32)
        owner_ref[number : number + 1, :] = table[0:1, :].astype(jnp.int32)
        block_ref[number : number + 1, :] = table[1:2, :].astype(jnp.int32)
    owner = owner_ref[...]
    shape = (plan.part, plan.part)
    earlier = lax.broadcasted_iota(jnp.int32, shape, 0) < lax.broadcasted_iota(jnp.int32, shape, 1)
    earlier = jnp.where(earlier, 1.0, 0.0)
    ones = jnp.ones(shape, jnp.float32)
    shape = (plan.lanes, plan.lanes)
    above = lax.broadcasted_iota(jnp.int32, shape, 0) > lax.broadcasted_iota(jnp.int32, shape, 1)
    above = jnp.where(above, 1.0, 0.0)
    target = jnp.zeros(owner.shape, jnp.int32)
    most = jnp.float32(0.0)
    for other in range(plan.layers):
        chosen = owner // plan.run == other
        marks = jnp.where(chosen, 1.0, 0.0)
        lines = jnp.dot(marks, ones, preferred_element_type=jnp.float32)
        count = jnp.dot(marks, earlier, preferred_element_type=jnp.float32) + jnp.dot(
            above, lines, preferred_element_type=jnp.float32
        )
        count = count.astype(jnp.int32)
        there = jnp.where(count < plan.room, (layer ^ other) * plan.stride + count, -1)
        target = jnp.where(chosen, there, target)
        most = jnp.maximum(most, jnp.sum(marks))
    full = jnp.where(most > plan.room, 1.0, 0.0)
    value = owner % plan.run * plan.blocks + block_ref[...] + 1
    for number in range(plan.lanes):
        here = slice(number * plan.part, (number + 1) * plan.part)
        target_ref[:, here] = target[number : number + 1, :]
        value_ref[:, here] = value[number : number + 1, :].astype(jnp.float32)
    target = target_ref[...]
    values = jnp.broadcast_to(value_ref[...], (8, plan.rows)).astype(jnp.bfloat16)
    for number, out in enumerate(outs):
        row = lax.broadcasted_iota(jnp.int32, (plan.stride, plan.rows), 0) + number * plan.stride
        chosen = jnp.where(row == target, 1.0, 0.0).astype(jnp.bfloat16)
        moved = jnp.dot(
            chosen[: plan.room, :], inputs_ref[...], preferred_element_type=jnp.float32
        )
        out[: plan.room, :] = moved.astype(jnp.bfloat16)
        listed = lax.dot_general(
            values, chosen, (((1,), (1,)), ((), ())), preferred_element_type=jnp.float32
        )
        line = lax.broadcasted_iota(jnp.int32, (16, plan.stride), 0)
        table = jnp.where(line == 0, listed[0:1, :], jnp.where(line == 1, full, 0.0))
        out[plan.room :, : plan.stride] = table.astype(jnp.bfloat16)


def route_more_kernel(plan, target_ref, *refs):
    ins, outs, inputs_ref = refs[: plan.lanes], refs[plan.lanes : -1], refs[-1]
    for number, part in enumerate(ins):
        inputs_ref[number * plan.part : (number + 1) * plan.part, :] = part[...]
    permute_into(target_ref[...], 0, inputs_ref, outs, plan.room, plan.stride)


def gather_rows(plan, ins, inputs_ref):
    for number, part in enumerate(ins):
        first = number * plan.stride
        inputs_ref[first : first + plan.room, :] = part[: plan.room, :]
        if plan.stride > plan.room:
            inputs_ref[first + plan.room : first + plan.stride, :] = jnp.zeros(
                (plan.stride - plan.room, inputs_ref.shape[1]), jnp.bfloat16
            )


def sort_parts(plan, target, inputs_ref, outs, ahead_ref, sorted_ref):
    tile = 2 * plan.part
    for pair in range(plan.lanes // 2):
        row = lax.broadcasted_iota(jnp.int32, (tile, inputs_ref.shape[0]), 0) + pair * tile
        chosen = jnp.where(row == target, 1.0, 0.0).astype(jnp.bfloat16)
        moved = jnp.dot(chosen, inputs_ref[...], preferred_element_type=jnp.float32)
        moved = moved.astype(jnp.bfloat16)
        sorted_ref[pair * tile : (pair + 1) * tile, :] = moved
        outs[2 * pair][...] = moved[: plan.part, :]
        outs[2 * pair + 1][...] = moved[plan.part :, :]
    lane, _ = my_lane(plan)
    for slot in range(2):
        part = lane_of(plan, slot) ^ lane
        ahead_ref[slot * plan.part : (slot + 1) * plan.part, :] = sorted_ref[
            pl.ds(pl.multiple_of(part * plan.part, plan.part), plan.part), :
        ]


def deliver_kernel(plan, *refs):
    ins, rest = refs[: plan.layers], refs[plan.layers :]
    outs, (ahead_ref, target_ref, full_ref, inputs_ref, sorted_ref) = rest[:-5], rest[-5:]
    lane, _ = my_lane(plan)
    gather_rows(plan, ins, inputs_ref)
    full = jnp.zeros((8, 128), jnp.float32)
    for number, part in enumerate(ins):
        table = part[plan.room :, : plan.stride].astype(jnp.float32)
        value = table[0:1, :].astype(jnp.int32) - 1
        full = jnp.maximum(full, jnp.broadcast_to(table[1:2, :128], (8, 128)))
        slot = value // plan.blocks
        within = lax.broadcasted_iota(jnp.int32, value.shape, 1) % plan.slice
        target = (lane_of(plan, slot) ^ lane) * plan.part + value % plan.blocks * plan.slice + within
        target_ref[:, number * plan.stride : (number + 1) * plan.stride] = jnp.where(
            value >= 0, target, -1
        )
    full_ref[...] = full.astype(jnp.int32)
    sort_parts(plan, target_ref[...], inputs_ref, outs, ahead_ref, sorted_ref)


def deliver_more_kernel(plan, target_ref, *refs):
    ins, rest = refs[: plan.layers], refs[plan.layers :]
    outs, (ahead_ref, inputs_ref, sorted_ref) = rest[:-3], rest[-3:]
    gather_rows(plan, ins, inputs_ref)
    sort_parts(plan, target_ref[...], inputs_ref, outs, ahead_ref, sorted_ref)


def join_kernel(plan, *refs):
    ins, (own_ref, behind_ref) = refs[:-2], refs[-2:]
    for number, part in enumerate(ins[: plan.lanes]):
        own_ref[number * plan.part : (number + 1) * plan.part, :] = part[...]
    for number, part in enumerate(ins[plan.lanes :]):
        behind_ref[number * 2 * plan.part : (number + 1) * 2 * plan.part, :] = part[...]


def wide_best(keys, queries_ref, best_ref):
    @pl.loop(0, keys[0].shape[0] // TILE, unroll=True)
    def _(tile):
        here = pl.ds(pl.multiple_of(tile * TILE, TILE), TILE)
        block = jnp.concatenate([part[here, :] for part in keys], axis=1)
        scores = lax.dot_general(
            block, queries_ref[...], (((1,), (1,)), ((), ())), preferred_element_type=jnp.float32
        )
        best_ref[...] = jnp.maximum(best_ref[...], jnp.max(scores, axis=0, keepdims=True))


def staged_best_kernel(plan, run_len_ref, *refs):
    count = len(plan.chunks)
    own, mate, behind, far = (refs[n * count : (n + 1) * count] for n in range(4))
    out_ref, best_ref, queries_ref, lines_ref = refs[4 * count :]
    ingest, run = lax.axis_index("ingest"), lax.axis_index("run")
    lane, _ = my_lane(plan)
    group, slot = plan.slot(ingest, run)
    begin = jnp.int32(0)
    for number, start in enumerate(cluster_starts(plan, run_len_ref)):
        here = (number // plan.per_group == group) & (start <= slot)
        begin = jnp.where(here, jnp.maximum(begin, start), begin)
    first = 0
    for part in own:
        queries_ref[:, first : first + part.shape[1]] = part[...]
        first += part.shape[1]

    def slots(row):
        block = row // plan.slice % plan.blocks
        return block * plan.cap + (row // plan.part ^ lane) * plan.slice + row % plan.slice

    best_ref[...] = jnp.full(best_ref.shape, -1.0, jnp.float32)
    query = slots(lax.broadcasted_iota(jnp.int32, (1, plan.rows), 1))

    @pl.loop(0, plan.rows // TILE, unroll=True)
    def _(tile):
        key = slots(lax.broadcasted_iota(jnp.int32, (TILE, 1), 0) + tile * TILE)
        block = queries_ref[pl.ds(pl.multiple_of(tile * TILE, TILE), TILE), :]
        scores = lax.dot_general(
            block, queries_ref[...], (((1,), (1,)), ((), ())), preferred_element_type=jnp.float32
        )
        top = jnp.max(jnp.where(key < query, scores, -2.0), axis=0, keepdims=True)
        best_ref[...] = jnp.maximum(best_ref[...], top)

    @pl.when(slot % 2 == 1)
    def _():
        wide_best(mate, queries_ref, best_ref)

    @pl.when(slot - slot % 2 - 2 >= begin)
    def _():
        wide_best(behind, queries_ref, best_ref)
        wide_best(far, queries_ref, best_ref)

    for number in range(plan.lanes):
        lines_ref[number : number + 1, :] = best_ref[
            :, number * plan.part : (number + 1) * plan.part
        ]
    for device in range(plan.devices):
        out_ref[device] = lines_ref[...]


def staged_unpack_kernel(plan, run_len_ref, cluster_ref, rank_ref, reply_ref, out_ref):
    group, slot, within = row_slot(plan, run_len_ref, cluster_ref[...], rank_ref[...])
    residue = within % plan.cap
    line = plan.device(group, slot) * plan.lanes + (residue // plan.slice ^ lane_of(plan, slot))
    column = within // plan.cap * plan.slice + residue % plan.slice
    number = lax.broadcasted_iota(jnp.int32, (plan.devices * plan.lanes, plan.rows), 0)
    columns = lax.dot_general(
        reply_ref[...],
        jnp.where(number == line, 1.0, 0.0),
        (((0,), (0,)), ((), ())),
        precision=lax.Precision.HIGHEST,
        preferred_element_type=jnp.float32,
    )
    place = lax.broadcasted_iota(jnp.int32, (plan.part, plan.rows), 0)
    out_ref[...] = jnp.sum(jnp.where(place == column, columns, 0.0), axis=0, keepdims=True)


SMEM = pl.BlockSpec(memory_space=pltpu.SMEM)
VMEM = pl.BlockSpec(memory_space=pltpu.VMEM)


def call(kernel, plan, shapes, specs, scratch=(), flops=0, moved=0, memory=32):
    return pl.pallas_call(
        functools.partial(kernel, plan),
        out_shape=shapes,
        in_specs=specs,
        out_specs=[VMEM] * len(shapes),
        scratch_shapes=scratch,
        compiler_params=pltpu.CompilerParams(vmem_limit_bytes=memory * MIB),
        cost_estimate=pl.CostEstimate(flops=flops, bytes_accessed=moved, transcendentals=0),
    )


def exchange(block):
    return lax.all_to_all(block, AXES, split_axis=0, concat_axis=0, tiled=True)


def direct(plan, embeddings, clusters, ranks, run_len):
    rows, width = embeddings.shape
    slots = plan.devices * plan.cap
    wide = jax.ShapeDtypeStruct
    outgoing, groups = call(
        pack_kernel,
        plan,
        [wide((slots, width), jnp.bfloat16), wide((plan.devices, 128), jnp.int32)],
        [SMEM, VMEM, VMEM, VMEM],
        [pltpu.VMEM((rows, width), jnp.bfloat16)],
        2 * slots * rows * width,
        3 * rows * width * 2,
    )(run_len, clusters, ranks, embeddings)
    groups = exchange(groups)
    arrived = exchange(outgoing)
    (own,) = call(
        sort_kernel, plan, [wide((rows, width), jnp.bfloat16)], [SMEM, VMEM],
        moved=3 * rows * width * 2,
    )(groups, arrived)

    def swap(block):
        pairs = [
            (i * plan.run + r, (i ^ 1) * plan.run + r)
            for i in range(plan.ingest)
            for r in range(plan.run)
        ]
        return lax.ppermute(block, AXES, pairs)

    mate = swap(own)
    behind = []
    for distance, chips in enumerate(plan.links()):
        if distance == 0:
            continue
        pairs = [
            (plan.device(i, 2 * chip + core), plan.device(i, 2 * (chip + distance) + core))
            for i in range(plan.ingest)
            for chip in chips
            for core in range(2)
        ]
        moved = lax.ppermute(own, AXES, pairs)
        behind += [moved, swap(moved)]
    place = jnp.stack([lax.axis_index("ingest"), lax.axis_index("run")]).astype(jnp.int32)
    (replies,) = call(
        best_kernel,
        plan,
        [wide((plan.devices, 128), jnp.float32)],
        [SMEM, SMEM, SMEM] + [VMEM] * (2 + len(behind)),
        [pltpu.VMEM((1, rows), jnp.float32), pltpu.VMEM((rows // plan.cap, 128), jnp.float32)],
        2 * rows * rows * width * 3,
        4 * rows * width * 2,
    )(run_len, place, groups, own, mate, *behind)
    returned = exchange(replies)
    (best,) = call(
        unpack_kernel, plan, [wide((1, rows), jnp.float32)], [SMEM, VMEM, VMEM, VMEM],
        moved=4 * rows * 4,
    )(run_len, clusters, ranks, returned)
    return best


def staged(plan, embeddings, clusters, ranks, run_len):
    rows, width = embeddings.shape
    wide = jax.ShapeDtypeStruct
    half = jnp.bfloat16
    lanes, layers = range(plan.lanes), range(plan.layers)

    def along_lanes(block, change):
        pairs = [
            (lane_device(plan, layer, lane), lane_device(plan, layer, lane ^ change))
            for layer in layers
            for lane in lanes
        ]
        return lax.ppermute(block, AXES, pairs)

    def along_layers(block, change):
        pairs = [
            (lane_device(plan, layer, lane), lane_device(plan, layer ^ change, lane))
            for layer in layers
            for lane in lanes
        ]
        return lax.ppermute(block, AXES, pairs)

    def chip_to_chip(block, routes):
        pairs = [
            (plan.device(layer, 2 * first + core), plan.device(layer, 2 * second + core))
            for layer in layers
            for first, second in routes
            for core in range(2)
        ]
        return lax.ppermute(block, AXES, pairs)

    far_first = sorted(lanes, key=lambda change: -(change & 1) - (change // plan.width // 2))

    def swap_lanes(blocks):
        return [
            along_lanes(blocks[change], change) if change else blocks[0] for change in far_first
        ], far_first

    def by_change(moved):
        arrays, order = moved
        return [arrays[order.index(change)] for change in lanes]

    sizes = [plan.part + 16] + [plan.part] * (len(plan.chunks) - 1)
    spread = call(
        spread_kernel,
        plan,
        [wide((size, f), half) for size, f in zip(sizes, plan.chunks) for _ in lanes],
        [SMEM, VMEM, VMEM, VMEM],
        [pltpu.VMEM((rows, width), half)],
        2 * rows * rows * width,
        3 * rows * width * 2,
    )(run_len, clusters, ranks, embeddings)
    owns, mates, behinds, fars = [], [], [], []
    table = targets = full = None
    for chunk, f in enumerate(plan.chunks):
        if chunk:
            spread, routed = lax.optimization_barrier((spread, routed))
        spec = dict(flops=2 * rows * rows * f, moved=3 * rows * f * 2, memory=12)
        parts = by_change(swap_lanes(spread[chunk * plan.lanes : (chunk + 1) * plan.lanes]))
        rooms = [wide((plan.room + (0 if chunk else 16), f), half) for _ in layers]
        inputs = pltpu.VMEM((rows, f), half)
        if chunk == 0:
            *routed, table = call(
                route_kernel,
                plan,
                [*rooms, wide((1, rows), jnp.int32)],
                [VMEM] * plan.lanes,
                [
                    inputs,
                    pltpu.VMEM((plan.lanes, plan.part), jnp.int32),
                    pltpu.VMEM((plan.lanes, plan.part), jnp.int32),
                    pltpu.VMEM((1, rows), jnp.float32),
                ],
                **spec,
            )(*parts)
        else:
            routed = call(
                route_more_kernel, plan, rooms, [VMEM] * (1 + plan.lanes), [inputs], **spec
            )(table, *parts)
        moved = {change: along_layers(routed[change], change) for change in reversed(layers[1:])}
        arrived = [routed[0]] + [moved[change] for change in layers[1:]]
        shapes = [wide((plan.part, f), half) for _ in lanes] + [wide((2 * plan.part, f), half)]
        scratch = [pltpu.VMEM((plan.layers * plan.stride, f), half), inputs]
        if chunk == 0:
            *parts, ahead, targets, full = call(
                deliver_kernel,
                plan,
                [
                    *shapes,
                    wide((1, plan.layers * plan.stride), jnp.int32),
                    wide((8, 128), jnp.int32),
                ],
                [VMEM] * plan.layers,
                scratch,
                **spec,
            )(*arrived)
        else:
            *parts, ahead = call(
                deliver_more_kernel, plan, shapes, [VMEM] * (1 + plan.layers), scratch, **spec
            )(targets, *arrived)
        near = chip_to_chip(ahead, [(0, 1), (3, 2)])
        parts = by_change(swap_lanes(parts))
        side = chip_to_chip(ahead, [(2, 1)])
        corner = chip_to_chip(near, [(2, 1)])
        own, behind = call(
            join_kernel,
            plan,
            [wide((rows, f), half)] * 2,
            [VMEM] * (plan.lanes + 4),
            moved=4 * rows * f * 2,
            memory=8,
        )(*parts, ahead, near, side, corner)
        owns.append(own)
        behinds.append(behind)
        mates.append(along_lanes(own, plan.width))
        fars.append(along_lanes(behind, plan.width))
    (replies,) = call(
        staged_best_kernel,
        plan,
        [wide((plan.devices, plan.lanes, 128), jnp.float32)],
        [SMEM] + [VMEM] * (4 * len(plan.chunks)),
        [
            pltpu.VMEM((1, rows), jnp.float32),
            pltpu.VMEM((rows, width), half),
            pltpu.VMEM((plan.lanes, 128), jnp.float32),
        ],
        2 * rows * rows * width * 3,
        4 * rows * width * 2,
    )(run_len, *owns, *mates, *behinds, *fars)
    returned = exchange(replies).reshape(plan.devices * plan.lanes, 128)
    (best,) = call(
        staged_unpack_kernel,
        plan,
        [wide((1, rows), jnp.float32)],
        [SMEM, VMEM, VMEM, VMEM],
        moved=4 * rows * 4,
        memory=8,
    )(run_len, clusters, ranks, returned)
    return best, full[0, 0]


def local(embeddings, cluster_id, rank, run_len):
    rows, width = embeddings.shape
    plan = Plan(lax.axis_size("ingest"), lax.axis_size("run"), run_len.shape[0], rows, width)
    given = (embeddings, cluster_id.reshape(1, rows), rank.reshape(1, rows), run_len)
    if not plan.staged():
        return direct(plan, *given).reshape(rows)
    best, full = staged(plan, *given)
    best = lax.cond(full > 0, lambda: direct(plan, *given), lambda: best)
    return best.reshape(rows)


def solution(mesh):
    return jax.shard_map(
        local,
        mesh=mesh,
        in_specs=(P(AXES, None), P(AXES), P(AXES), P()),
        out_specs=P(AXES),
        check_vma=False,
    )
```

```python
import functools

import jax
import jax.numpy as jnp
from jax import lax
from jax.experimental import pallas as pl
from jax.experimental.pallas import tpu as pltpu
from jax.sharding import PartitionSpec as P

EPSILON = 1e-06
AXES = ("ingest", "run")
TILE = 256
CHUNKS = 2
MIB = 1024 * 1024


class Plan:
    def __init__(self, ingest, run, clusters, rows, features):
        self.ingest, self.run, self.clusters, self.rows = ingest, run, clusters, rows
        self.devices = ingest * run
        self.per_group = clusters // ingest
        self.cap = 2 * rows // self.devices
        self.reach = min(8, run // 2)
        self.width = run // ingest
        self.pairs = run // 2
        self.blocks = rows // self.cap
        self.layers, self.lanes = ingest, ingest * self.width
        self.slice = self.cap // self.lanes
        self.part = self.blocks * self.slice
        self.chunks = tuple(features // CHUNKS for _ in range(CHUNKS))
        mean = rows // self.layers
        self.room = mean + mean // 8
        self.stride = -(-self.room // 128) * 128

    def staged(self):
        powers = all(n & (n - 1) == 0 for n in (self.layers, self.lanes, self.width))
        return (
            powers
            and self.cap % (8 * self.lanes) == 0
            and self.part == 128
            and self.room % 16 == 0
            and min(self.chunks) >= self.stride
            and self.links()[1:] == [[0]]
        )

    def device(self, group, slot):
        core, chip = slot % 2, slot // 2
        column, place = chip // self.width, chip % self.width
        odd = column % 2
        place = place + odd * (self.width - 1 - 2 * place)
        return (2 * column + core) * self.run + group * self.width + place

    def slot(self, device_ingest, device_run):
        core, column = device_ingest % 2, device_ingest // 2
        place = device_run % self.width
        place = place + (column % 2) * (self.width - 1 - 2 * place)
        return device_run // self.width, 2 * (column * self.width + place) + core

    def splits(self):
        def parts(total, count, top):
            if count == 0:
                if total == 0:
                    yield ()
                return
            for first in range(min(top, total), 0, -1):
                for rest in parts(total - first, count - 1, first):
                    yield (first, *rest)

        return list(parts(self.pairs, self.per_group, self.reach // 2))

    def links(self):
        found = [set() for _ in range(self.reach // 2)]
        for split in self.splits():
            begin = 0
            for length in split:
                for first in range(length):
                    for second in range(first + 1, length):
                        found[second - first].add(begin + first)
                begin += length
        return [sorted(chips) for chips in found]


def cluster_starts(plan, run_len_ref):
    starts = []
    for cluster in range(plan.clusters):
        base = cluster // plan.per_group * plan.per_group
        mine = run_len_ref[cluster]
        total = jnp.int32(0)
        for other in range(base, base + plan.per_group):
            if other == cluster:
                continue
            theirs = run_len_ref[other]
            ahead = (theirs >= mine) if other < cluster else (theirs > mine)
            total = total + jnp.where(ahead, theirs, 0)
        starts.append(total)
    return starts


def row_slot(plan, run_len_ref, cluster, rank):
    starts = cluster_starts(plan, run_len_ref)
    begin = jnp.zeros_like(cluster)
    group = jnp.zeros_like(cluster)
    for number, start in enumerate(starts):
        here = cluster == number
        begin = jnp.where(here, start, begin)
        group = jnp.where(here, number // plan.per_group, group)
    return group, begin + rank // plan.rows, rank % plan.rows


def row_owner(plan, run_len_ref, cluster, rank):
    group, slot, within = row_slot(plan, run_len_ref, cluster, rank)
    return plan.device(group, slot), within


def pack_kernel(plan, run_len_ref, cluster_ref, rank_ref, rows_ref, out_ref, group_ref, unit_ref):
    step = 128

    @pl.loop(0, plan.rows // step)
    def _(number):
        here = pl.ds(pl.multiple_of(number * step, step), step)
        widened = rows_ref[here, :].astype(jnp.float32)
        total = jnp.sum(widened * widened, axis=1, keepdims=True) + EPSILON
        unit_ref[here, :] = (widened * lax.rsqrt(total)).astype(jnp.bfloat16)

    owner, within = row_owner(plan, run_len_ref, cluster_ref[...], rank_ref[...])
    number = lax.broadcasted_iota(jnp.int32, (plan.devices, plan.rows), 0)
    group = jnp.max(
        jnp.where(number == owner, within // plan.cap + 1, 0), axis=1, keepdims=True
    )
    group_ref[...] = jnp.broadcast_to(group, group_ref.shape)
    position = owner * plan.cap + within % plan.cap

    @pl.loop(0, plan.devices * plan.cap // TILE)
    def _(tile):
        row = lax.broadcasted_iota(jnp.int32, (TILE, plan.rows), 0) + tile * TILE
        chosen = jnp.where(row == position, 1.0, 0.0).astype(jnp.bfloat16)
        moved = jnp.dot(chosen, unit_ref[...], preferred_element_type=jnp.float32)
        here = pl.ds(pl.multiple_of(tile * TILE, TILE), TILE)
        out_ref[here, :] = moved.astype(jnp.bfloat16)


def sort_kernel(plan, group_ref, arrived_ref, out_ref):
    for source in range(plan.devices):
        group = group_ref[source, 0]

        @pl.when(group > 0)
        def _():
            here = pl.ds(pl.multiple_of((group - 1) * plan.cap, plan.cap), plan.cap)
            out_ref[here, :] = arrived_ref[source * plan.cap : (source + 1) * plan.cap, :]


def block_best(keys_ref, queries_ref, best_ref):
    rows = keys_ref.shape[0]

    @pl.loop(0, rows // TILE)
    def _(tile):
        keys = keys_ref[pl.ds(pl.multiple_of(tile * TILE, TILE), TILE), :]
        scores = lax.dot_general(
            keys, queries_ref[...], (((1,), (1,)), ((), ())), preferred_element_type=jnp.float32
        )
        best_ref[...] = jnp.maximum(best_ref[...], jnp.max(scores, axis=0, keepdims=True))


def triangle_best(rows_ref, best_ref):
    rows = rows_ref.shape[0]
    for first in range(0, rows, TILE):
        scores = lax.dot_general(
            rows_ref[first : first + TILE, :],
            rows_ref[first:, :],
            (((1,), (1,)), ((), ())),
            preferred_element_type=jnp.float32,
        )
        key = lax.broadcasted_iota(jnp.int32, (TILE, TILE), 0)
        query = lax.broadcasted_iota(jnp.int32, (TILE, TILE), 1)
        corner = jnp.max(
            jnp.where(key < query, scores[:, :TILE], -2.0), axis=0, keepdims=True
        )
        here = slice(first, first + TILE)
        best_ref[:, here] = jnp.maximum(best_ref[:, here], corner)
        if first + TILE < rows:
            rest = jnp.max(scores[:, TILE:], axis=0, keepdims=True)
            there = slice(first + TILE, rows)
            best_ref[:, there] = jnp.maximum(best_ref[:, there], rest)


def best_kernel(plan, run_len_ref, place_ref, group_ref, own_ref, mate_ref, *rest):
    behind, (out_ref, best_ref, blocks_ref) = rest[:-3], rest[-3:]
    group, slot = plan.slot(place_ref[0], place_ref[1])
    begin = jnp.int32(0)
    for number, start in enumerate(cluster_starts(plan, run_len_ref)):
        here = (number // plan.per_group == group) & (start <= slot)
        begin = jnp.where(here, jnp.maximum(begin, start), begin)
    best_ref[...] = jnp.full(best_ref.shape, -1.0, jnp.float32)
    triangle_best(own_ref, best_ref)

    @pl.when(slot % 2 == 1)
    def _():
        block_best(mate_ref, own_ref, best_ref)

    for distance in range(1, plan.reach // 2):
        first, second = behind[2 * distance - 2], behind[2 * distance - 1]

        @pl.when(slot - slot % 2 - 2 * distance >= begin)
        def _():
            block_best(first, own_ref, best_ref)
            block_best(second, own_ref, best_ref)

    for number in range(plan.rows // plan.cap):
        part = best_ref[:, number * plan.cap : (number + 1) * plan.cap]
        blocks_ref[number : number + 1, : plan.cap] = part
    for source in range(plan.devices):
        chosen = jnp.maximum(group_ref[source, 0] - 1, 0)
        out_ref[source : source + 1, :] = blocks_ref[pl.ds(chosen, 1), :]


def unpack_kernel(plan, run_len_ref, cluster_ref, rank_ref, reply_ref, out_ref):
    owner, within = row_owner(plan, run_len_ref, cluster_ref[...], rank_ref[...])
    number = lax.broadcasted_iota(jnp.int32, (plan.devices, plan.rows), 0)
    chosen = jnp.where(number == owner, 1.0, 0.0)
    columns = lax.dot_general(
        reply_ref[:, : plan.cap],
        chosen,
        (((0,), (0,)), ((), ())),
        precision=lax.Precision.HIGHEST,
        preferred_element_type=jnp.float32,
    )
    lane = lax.broadcasted_iota(jnp.int32, (plan.cap, plan.rows), 0)
    out_ref[...] = jnp.sum(
        jnp.where(lane == within % plan.cap, columns, 0.0), axis=0, keepdims=True
    )


def lane_of(plan, slot):
    device = plan.device(0, slot)
    return device // plan.run * plan.width + device % plan.run


def chip_change(plan, change):
    width = plan.width
    return change % width + change // (2 * width) * width, change // width % 2


def lane_change(plan, chip, core):
    width = plan.width
    return chip % width + core * width + chip // width * 2 * width


def lane_device(plan, layer, lane):
    return lane // plan.width * plan.run + layer * plan.width + lane % plan.width


def my_lane(plan):
    run = lax.axis_index("run")
    return lax.axis_index("ingest") * plan.width + run % plan.width, run // plan.width


def spread_kernel(plan, run_len_ref, cluster_ref, rank_ref, rows_ref, *rest):
    outs, (unit_ref,) = rest[:-1], rest[-1:]
    step = 128

    @pl.loop(0, plan.rows // step)
    def _(number):
        here = pl.ds(pl.multiple_of(number * step, step), step)
        widened = rows_ref[here, :].astype(jnp.float32)
        total = jnp.sum(widened * widened, axis=1, keepdims=True) + EPSILON
        unit_ref[here, :] = (widened * lax.rsqrt(total)).astype(jnp.bfloat16)

    lane, _ = my_lane(plan)
    group, slot, within = row_slot(plan, run_len_ref, cluster_ref[...], rank_ref[...])
    owner = group * plan.run + slot
    number = lax.broadcasted_iota(jnp.int32, (plan.devices, plan.rows), 0)
    member = number == owner
    block = jnp.max(jnp.where(member, within // plan.cap + 1, 0), axis=1, keepdims=True)
    present = jnp.where(block > 0, 1.0, 0.0)
    before = lax.broadcasted_iota(jnp.int32, (plan.devices, plan.devices), 0) > (
        lax.broadcasted_iota(jnp.int32, (plan.devices, plan.devices), 1)
    )
    order = jnp.dot(
        jnp.where(before, 1.0, 0.0),
        jnp.broadcast_to(present, (plan.devices, 128)),
        preferred_element_type=jnp.float32,
    )
    mine = jnp.sum(jnp.where(member, order[:, :1], 0.0), axis=0, keepdims=True)
    residue = within % plan.cap
    target = (
        (residue // plan.slice ^ lane) * plan.part
        + mine.astype(jnp.int32) * plan.slice
        + residue % plan.slice
    )
    tile = 2 * plan.part

    for pair in range(plan.lanes // 2):
        row = lax.broadcasted_iota(jnp.int32, (tile, plan.rows), 0) + pair * tile
        chosen = jnp.where(row == target, 1.0, 0.0).astype(jnp.bfloat16)
        moved = jnp.dot(chosen, unit_ref[...], preferred_element_type=jnp.float32)
        moved = moved.astype(jnp.bfloat16)
        outs[2 * pair][: plan.part, :] = moved[: plan.part, :]
        outs[2 * pair + 1][: plan.part, :] = moved[plan.part :, :]

    place = lax.broadcasted_iota(jnp.int32, (plan.devices, plan.part), 1) // plan.slice
    here = (place.astype(jnp.float32) == order[:, :1]) & (block > 0)
    who = lax.broadcasted_iota(jnp.int32, (plan.devices, plan.part), 0)
    owners = jnp.sum(jnp.where(here, who, 0), axis=0, keepdims=True)
    blocks = jnp.sum(jnp.where(here, block - 1, 0), axis=0, keepdims=True)
    line = lax.broadcasted_iota(jnp.int32, (16, plan.part), 0)
    table = jnp.where(line == 0, owners, jnp.where(line == 1, blocks, 0))
    for out in outs:
        out[plan.part :, : plan.part] = table.astype(jnp.float32).astype(jnp.bfloat16)


def permute_into(target, first, inputs_ref, outs, room, stride):
    columns = inputs_ref.shape[0]
    for number, out in enumerate(outs):
        row = lax.broadcasted_iota(jnp.int32, (room, columns), 0) + first + number * stride
        chosen = jnp.where(row == target, 1.0, 0.0).astype(jnp.bfloat16)
        moved = jnp.dot(chosen, inputs_ref[...], preferred_element_type=jnp.float32)
        out[:room, :] = moved.astype(jnp.bfloat16)


def route_kernel(plan, *refs):
    ins, rest = refs[: plan.lanes], refs[plan.lanes :]
    outs, (target_ref, inputs_ref, owner_ref, block_ref, value_ref) = rest[:-5], rest[-5:]
    _, layer = my_lane(plan)
    for number, part in enumerate(ins):
        inputs_ref[number * plan.part : (number + 1) * plan.part, :] = part[
            : plan.part, : plan.chunks[0]
        ]
        table = part[plan.part :, : plan.part].astype(jnp.float32)
        owner_ref[number : number + 1, :] = table[0:1, :].astype(jnp.int32)
        block_ref[number : number + 1, :] = table[1:2, :].astype(jnp.int32)
    owner = owner_ref[...]
    shape = (plan.part, plan.part)
    earlier = lax.broadcasted_iota(jnp.int32, shape, 0) < lax.broadcasted_iota(jnp.int32, shape, 1)
    earlier = jnp.where(earlier, 1.0, 0.0)
    ones = jnp.ones(shape, jnp.float32)
    shape = (plan.lanes, plan.lanes)
    above = lax.broadcasted_iota(jnp.int32, shape, 0) > lax.broadcasted_iota(jnp.int32, shape, 1)
    above = jnp.where(above, 1.0, 0.0)
    target = jnp.zeros(owner.shape, jnp.int32)
    most = jnp.float32(0.0)
    for other in range(plan.layers):
        chosen = owner // plan.run == other
        marks = jnp.where(chosen, 1.0, 0.0)
        lines = jnp.dot(marks, ones, preferred_element_type=jnp.float32)
        count = jnp.dot(marks, earlier, preferred_element_type=jnp.float32) + jnp.dot(
            above, lines, preferred_element_type=jnp.float32
        )
        count = count.astype(jnp.int32)
        there = jnp.where(count < plan.room, (layer ^ other) * plan.stride + count, -1)
        target = jnp.where(chosen, there, target)
        most = jnp.maximum(most, jnp.sum(marks))
    full = jnp.where(most > plan.room, 1.0, 0.0)
    value = owner % plan.run * plan.blocks + block_ref[...] + 1
    for number in range(plan.lanes):
        here = slice(number * plan.part, (number + 1) * plan.part)
        target_ref[:, here] = target[number : number + 1, :]
        value_ref[:, here] = value[number : number + 1, :].astype(jnp.float32)
    target = target_ref[...]
    values = jnp.broadcast_to(value_ref[...], (8, plan.rows)).astype(jnp.bfloat16)
    for number, out in enumerate(outs):
        row = lax.broadcasted_iota(jnp.int32, (plan.stride, plan.rows), 0) + number * plan.stride
        chosen = jnp.where(row == target, 1.0, 0.0).astype(jnp.bfloat16)
        moved = jnp.dot(
            chosen[: plan.room, :], inputs_ref[...], preferred_element_type=jnp.float32
        )
        out[: plan.room, :] = moved.astype(jnp.bfloat16)
        listed = lax.dot_general(
            values, chosen, (((1,), (1,)), ((), ())), preferred_element_type=jnp.float32
        )
        line = lax.broadcasted_iota(jnp.int32, (16, plan.stride), 0)
        table = jnp.where(line == 0, listed[0:1, :], jnp.where(line == 1, full, 0.0))
        out[plan.room :, : plan.stride] = table.astype(jnp.bfloat16)


def route_more_kernel(plan, target_ref, *refs, chunk):
    ins, outs, inputs_ref = refs[: plan.lanes], refs[plan.lanes : -1], refs[-1]
    first = sum(plan.chunks[:chunk])
    for number, part in enumerate(ins):
        inputs_ref[number * plan.part : (number + 1) * plan.part, :] = part[
            : plan.part, first : first + plan.chunks[chunk]
        ]
    permute_into(target_ref[...], 0, inputs_ref, outs, plan.room, plan.stride)


def gather_rows(plan, ins, inputs_ref):
    for number, part in enumerate(ins):
        first = number * plan.stride
        inputs_ref[first : first + plan.room, :] = part[: plan.room, :]
        if plan.stride > plan.room:
            inputs_ref[first + plan.room : first + plan.stride, :] = jnp.zeros(
                (plan.stride - plan.room, inputs_ref.shape[1]), jnp.bfloat16
            )


def sort_parts(plan, target, inputs_ref, outs, ahead_ref, sorted_ref):
    tile = 2 * plan.part
    for chip, out in enumerate(outs):
        row = lax.broadcasted_iota(jnp.int32, (tile, inputs_ref.shape[0]), 0) + chip * tile
        chosen = jnp.where(row == target, 1.0, 0.0).astype(jnp.bfloat16)
        moved = jnp.dot(chosen, inputs_ref[...], preferred_element_type=jnp.float32)
        moved = moved.astype(jnp.bfloat16)
        sorted_ref[chip * tile : (chip + 1) * tile, :] = moved
        out[...] = moved
    lane, _ = my_lane(plan)
    chip, _ = chip_change(plan, lane_of(plan, 0) ^ lane)
    ahead_ref[...] = sorted_ref[pl.ds(pl.multiple_of(chip * tile, tile), tile), :]


def deliver_kernel(plan, *refs):
    ins, rest = refs[: plan.layers], refs[plan.layers :]
    outs, (ahead_ref, target_ref, full_ref, inputs_ref, sorted_ref) = rest[:-5], rest[-5:]
    lane, _ = my_lane(plan)
    gather_rows(plan, ins, inputs_ref)
    full = jnp.zeros((8, 128), jnp.float32)
    for number, part in enumerate(ins):
        table = part[plan.room :, : plan.stride].astype(jnp.float32)
        value = table[0:1, :].astype(jnp.int32) - 1
        full = jnp.maximum(full, jnp.broadcast_to(table[1:2, :128], (8, 128)))
        slot = value // plan.blocks
        within = lax.broadcasted_iota(jnp.int32, value.shape, 1) % plan.slice
        chip, _ = chip_change(plan, lane_of(plan, slot) ^ lane)
        target = (2 * chip + slot % 2) * plan.part + value % plan.blocks * plan.slice + within
        target_ref[:, number * plan.stride : (number + 1) * plan.stride] = jnp.where(
            value >= 0, target, -1
        )
    full_ref[...] = full.astype(jnp.int32)
    sort_parts(plan, target_ref[...], inputs_ref, outs, ahead_ref, sorted_ref)


def deliver_more_kernel(plan, target_ref, *refs):
    ins, rest = refs[: plan.layers], refs[plan.layers :]
    outs, (ahead_ref, inputs_ref, sorted_ref) = rest[:-3], rest[-3:]
    gather_rows(plan, ins, inputs_ref)
    sort_parts(plan, target_ref[...], inputs_ref, outs, ahead_ref, sorted_ref)


def join_kernel(plan, *refs):
    ins, outs = refs[: -(len(refs) // 5)], refs[-(len(refs) // 5) :]
    tile = 2 * plan.part
    for number, part in enumerate(ins):
        out = outs[number // (plan.lanes // 2)]
        first = number % (plan.lanes // 2) * tile
        out[first : first + tile, :] = part[...]


def add_best(keys, queries_ref, best_ref, allowed=None):
    scores = lax.dot_general(
        keys, queries_ref[...], (((1,), (1,)), ((), ())), preferred_element_type=jnp.float32
    )
    if allowed is not None:
        scores = jnp.where(allowed, scores, -2.0)
    best_ref[...] = jnp.maximum(best_ref[...], jnp.max(scores, axis=0, keepdims=True))


def staged_best_kernel(plan, run_len_ref, *refs):
    count = len(plan.chunks)
    own, mate, behind, far = (refs[n * count : (n + 1) * count] for n in range(4))
    out_ref, best_ref, queries_ref, lines_ref = refs[4 * count :]
    ingest, run = lax.axis_index("ingest"), lax.axis_index("run")
    lane, _ = my_lane(plan)
    group, slot = plan.slot(ingest, run)
    core = slot % 2
    begin = jnp.int32(0)
    for number, start in enumerate(cluster_starts(plan, run_len_ref)):
        here = (number // plan.per_group == group) & (start <= slot)
        begin = jnp.where(here, jnp.maximum(begin, start), begin)
    chips = plan.lanes // 2
    for side, parts in enumerate((own, mate)):
        for chip in range(chips):
            there = pl.ds(pl.multiple_of((2 * chip + core) * plan.part, plan.part), plan.part)
            here = slice((side * chips + chip) * plan.part, (side * chips + chip + 1) * plan.part)
            first = 0
            for part in parts:
                queries_ref[here, first : first + part.shape[1]] = part[there, :]
                first += part.shape[1]

    def slots(row):
        line = row // plan.part
        source = lane_change(plan, line % chips, line // chips) ^ lane
        block = row // plan.slice % plan.blocks
        return block * plan.cap + source * plan.slice + row % plan.slice

    best_ref[...] = jnp.full(best_ref.shape, -1.0, jnp.float32)
    query = slots(lax.broadcasted_iota(jnp.int32, (1, plan.rows), 1))
    for first in range(0, plan.rows, TILE):
        key = slots(lax.broadcasted_iota(jnp.int32, (TILE, 1), 0) + first)
        add_best(queries_ref[first : first + TILE, :], queries_ref, best_ref, key < query)

    @pl.when(core == 1)
    def _():
        for parts in (own, mate):
            for pair in range(0, chips, 2):
                keys = [
                    jnp.concatenate([part[2 * n * plan.part : (2 * n + 1) * plan.part, :] for part in parts], axis=1)
                    for n in (pair, pair + 1)
                ]
                add_best(jnp.concatenate(keys, axis=0), queries_ref, best_ref)

    @pl.when(slot - core - 2 >= begin)
    def _():
        for parts in (behind, far):
            for first in range(0, plan.rows, TILE):
                keys = [part[first : first + TILE, :] for part in parts]
                add_best(jnp.concatenate(keys, axis=1), queries_ref, best_ref)

    for number in range(plan.lanes):
        lines_ref[number : number + 1, :] = best_ref[
            :, number * plan.part : (number + 1) * plan.part
        ]
    for device in range(plan.devices):
        out_ref[device] = lines_ref[...]


def staged_unpack_kernel(plan, run_len_ref, cluster_ref, rank_ref, reply_ref, out_ref):
    group, slot, within = row_slot(plan, run_len_ref, cluster_ref[...], rank_ref[...])
    residue = within % plan.cap
    chip, core = chip_change(plan, residue // plan.slice ^ lane_of(plan, slot))
    line = plan.device(group, slot) * plan.lanes + core * (plan.lanes // 2) + chip
    column = within // plan.cap * plan.slice + residue % plan.slice
    number = lax.broadcasted_iota(jnp.int32, (plan.devices * plan.lanes, plan.rows), 0)
    columns = lax.dot_general(
        reply_ref[...],
        jnp.where(number == line, 1.0, 0.0),
        (((0,), (0,)), ((), ())),
        precision=lax.Precision.HIGHEST,
        preferred_element_type=jnp.float32,
    )
    place = lax.broadcasted_iota(jnp.int32, (plan.part, plan.rows), 0)
    out_ref[...] = jnp.sum(jnp.where(place == column, columns, 0.0), axis=0, keepdims=True)


SMEM = pl.BlockSpec(memory_space=pltpu.SMEM)
VMEM = pl.BlockSpec(memory_space=pltpu.VMEM)


def call(kernel, plan, shapes, specs, scratch=(), flops=0, moved=0, memory=32):
    return pl.pallas_call(
        functools.partial(kernel, plan),
        out_shape=shapes,
        in_specs=specs,
        out_specs=[VMEM] * len(shapes),
        scratch_shapes=scratch,
        compiler_params=pltpu.CompilerParams(vmem_limit_bytes=memory * MIB),
        cost_estimate=pl.CostEstimate(flops=flops, bytes_accessed=moved, transcendentals=0),
    )


def exchange(block):
    return lax.all_to_all(block, AXES, split_axis=0, concat_axis=0, tiled=True)


def direct(plan, embeddings, clusters, ranks, run_len):
    rows, width = embeddings.shape
    slots = plan.devices * plan.cap
    wide = jax.ShapeDtypeStruct
    outgoing, groups = call(
        pack_kernel,
        plan,
        [wide((slots, width), jnp.bfloat16), wide((plan.devices, 128), jnp.int32)],
        [SMEM, VMEM, VMEM, VMEM],
        [pltpu.VMEM((rows, width), jnp.bfloat16)],
        2 * slots * rows * width,
        3 * rows * width * 2,
    )(run_len, clusters, ranks, embeddings)
    groups = exchange(groups)
    arrived = exchange(outgoing)
    (own,) = call(
        sort_kernel, plan, [wide((rows, width), jnp.bfloat16)], [SMEM, VMEM],
        moved=3 * rows * width * 2,
    )(groups, arrived)

    def swap(block):
        pairs = [
            (i * plan.run + r, (i ^ 1) * plan.run + r)
            for i in range(plan.ingest)
            for r in range(plan.run)
        ]
        return lax.ppermute(block, AXES, pairs)

    mate = swap(own)
    behind = []
    for distance, chips in enumerate(plan.links()):
        if distance == 0:
            continue
        pairs = [
            (plan.device(i, 2 * chip + core), plan.device(i, 2 * (chip + distance) + core))
            for i in range(plan.ingest)
            for chip in chips
            for core in range(2)
        ]
        moved = lax.ppermute(own, AXES, pairs)
        behind += [moved, swap(moved)]
    place = jnp.stack([lax.axis_index("ingest"), lax.axis_index("run")]).astype(jnp.int32)
    (replies,) = call(
        best_kernel,
        plan,
        [wide((plan.devices, 128), jnp.float32)],
        [SMEM, SMEM, SMEM] + [VMEM] * (2 + len(behind)),
        [pltpu.VMEM((1, rows), jnp.float32), pltpu.VMEM((rows // plan.cap, 128), jnp.float32)],
        2 * rows * rows * width * 3,
        4 * rows * width * 2,
    )(run_len, place, groups, own, mate, *behind)
    returned = exchange(replies)
    (best,) = call(
        unpack_kernel, plan, [wide((1, rows), jnp.float32)], [SMEM, VMEM, VMEM, VMEM],
        moved=4 * rows * 4,
    )(run_len, clusters, ranks, returned)
    return best


def staged(plan, embeddings, clusters, ranks, run_len):
    rows, width = embeddings.shape
    wide = jax.ShapeDtypeStruct
    half = jnp.bfloat16
    lanes, layers = range(plan.lanes), range(plan.layers)

    def along_lanes(block, change):
        pairs = [
            (lane_device(plan, layer, lane), lane_device(plan, layer, lane ^ change))
            for layer in layers
            for lane in lanes
        ]
        return lax.ppermute(block, AXES, pairs)

    def along_layers(block, change):
        pairs = [
            (lane_device(plan, layer, lane), lane_device(plan, layer ^ change, lane))
            for layer in layers
            for lane in lanes
        ]
        return lax.ppermute(block, AXES, pairs)

    def chip_to_chip(block, routes):
        pairs = [
            (plan.device(layer, 2 * first + core), plan.device(layer, 2 * second + core))
            for layer in layers
            for first, second in routes
            for core in range(2)
        ]
        return lax.ppermute(block, AXES, pairs)

    far_first = sorted(lanes, key=lambda change: -(change & 1) - (change // plan.width // 2))

    spread = call(
        spread_kernel,
        plan,
        [wide((plan.part + 16, width), half) for _ in lanes],
        [SMEM, VMEM, VMEM, VMEM],
        [pltpu.VMEM((rows, width), half)],
        2 * rows * rows * width,
        3 * rows * width * 2,
    )(run_len, clusters, ranks, embeddings)
    swapped = {change: along_lanes(spread[change], change) for change in far_first if change}
    spread = [spread[0]] + [swapped[change] for change in lanes[1:]]
    owns, mates, behinds, fars = [], [], [], []
    table = targets = full = None
    for chunk, f in enumerate(plan.chunks):
        spec = dict(flops=2 * rows * rows * f, moved=3 * rows * f * 2, memory=12)
        rooms = [wide((plan.room + (0 if chunk else 16), f), half) for _ in layers]
        inputs = pltpu.VMEM((rows, f), half)
        if chunk == 0:
            *routed, table = call(
                route_kernel,
                plan,
                [*rooms, wide((1, rows), jnp.int32)],
                [VMEM] * plan.lanes,
                [
                    inputs,
                    pltpu.VMEM((plan.lanes, plan.part), jnp.int32),
                    pltpu.VMEM((plan.lanes, plan.part), jnp.int32),
                    pltpu.VMEM((1, rows), jnp.float32),
                ],
                **spec,
            )(*spread)
        else:
            more = functools.partial(route_more_kernel, chunk=chunk)
            routed = call(more, plan, rooms, [VMEM] * (1 + plan.lanes), [inputs], **spec)(
                table, *spread
            )
        far = {change: along_layers(routed[change], change) for change in reversed(layers[1:])}
        arrived = [routed[0]] + [far[change] for change in layers[1:]]
        shapes = [wide((2 * plan.part, f), half) for _ in range(plan.lanes // 2 + 1)]
        scratch = [pltpu.VMEM((plan.layers * plan.stride, f), half), inputs]
        if chunk == 0:
            *parts, ahead, targets, full = call(
                deliver_kernel,
                plan,
                [
                    *shapes,
                    wide((1, plan.layers * plan.stride), jnp.int32),
                    wide((8, 128), jnp.int32),
                ],
                [VMEM] * plan.layers,
                scratch,
                **spec,
            )(*arrived)
        else:
            *parts, ahead = call(
                deliver_more_kernel, plan, shapes, [VMEM] * (1 + plan.layers), scratch, **spec
            )(targets, *arrived)
        near = chip_to_chip(ahead, [(0, 1), (3, 2)])
        parts = [
            along_lanes(part, lane_change(plan, chip, 0)) if chip else part
            for chip, part in enumerate(parts)
        ]
        side = chip_to_chip(ahead, [(2, 1)])
        corner = chip_to_chip(near, [(2, 1)])
        spec = dict(moved=4 * rows * f * 2, memory=8)
        ((own,), (behind,)) = (
            call(join_kernel, plan, [wide((rows, f), half)], [VMEM] * len(group), **spec)(*group)
            for group in (parts, (ahead, near, side, corner))
        )
        owns.append(own)
        behinds.append(behind)
        mates.append(along_lanes(own, plan.width))
        fars.append(along_lanes(behind, plan.width))
    (replies,) = call(
        staged_best_kernel,
        plan,
        [wide((plan.devices, plan.lanes, 128), jnp.float32)],
        [SMEM] + [VMEM] * (4 * len(plan.chunks)),
        [
            pltpu.VMEM((1, rows), jnp.float32),
            pltpu.VMEM((rows, width), half),
            pltpu.VMEM((plan.lanes, 128), jnp.float32),
        ],
        2 * rows * rows * width * 3,
        4 * rows * width * 2,
    )(run_len, *owns, *mates, *behinds, *fars)
    returned = exchange(replies).reshape(plan.devices * plan.lanes, 128)
    (best,) = call(
        staged_unpack_kernel,
        plan,
        [wide((1, rows), jnp.float32)],
        [SMEM, VMEM, VMEM, VMEM],
        moved=4 * rows * 4,
        memory=8,
    )(run_len, clusters, ranks, returned)
    return best, full[0, 0]


def local(embeddings, cluster_id, rank, run_len):
    rows, width = embeddings.shape
    plan = Plan(lax.axis_size("ingest"), lax.axis_size("run"), run_len.shape[0], rows, width)
    given = (embeddings, cluster_id.reshape(1, rows), rank.reshape(1, rows), run_len)
    if not plan.staged():
        return direct(plan, *given).reshape(rows)
    best, full = staged(plan, *given)
    best = lax.cond(full > 0, lambda: direct(plan, *given), lambda: best)
    return best.reshape(rows)


def solution(mesh):
    return jax.shard_map(
        local,
        mesh=mesh,
        in_specs=(P(AXES, None), P(AXES), P(AXES), P()),
        out_specs=P(AXES),
        check_vma=False,
    )
```

```python
import functools

import jax
import jax.numpy as jnp
from jax import lax
from jax.experimental import pallas as pl
from jax.experimental.pallas import tpu as pltpu
from jax.sharding import PartitionSpec as P

EPSILON = 1e-06
AXES = ("ingest", "run")
TILE = 256
SHARES = (1, 1, 1)
MIB = 1024 * 1024


class Plan:
    def __init__(self, ingest, run, clusters, rows, features):
        self.ingest, self.run, self.clusters, self.rows = ingest, run, clusters, rows
        self.devices = ingest * run
        self.per_group = clusters // ingest
        self.cap = 2 * rows // self.devices
        self.reach = min(8, run // 2)
        self.width = run // ingest
        self.pairs = run // 2
        self.blocks = rows // self.cap
        self.layers, self.lanes = ingest, ingest * self.width
        self.slice = self.cap // self.lanes
        self.part = self.blocks * self.slice
        self.chunks = tuple(features * share // sum(SHARES) for share in SHARES)
        mean = rows // self.layers
        self.room = mean + mean // 8
        self.stride = -(-self.room // 128) * 128

    def staged(self):
        powers = all(n & (n - 1) == 0 for n in (self.layers, self.lanes, self.width))
        return (
            powers
            and self.cap % (8 * self.lanes) == 0
            and self.part == 128
            and self.room % 16 == 0
            and all(width % 128 == 0 for width in self.chunks)
            and self.links()[1:] == [[0]]
        )

    def device(self, group, slot):
        core, chip = slot % 2, slot // 2
        column, place = chip // self.width, chip % self.width
        odd = column % 2
        place = place + odd * (self.width - 1 - 2 * place)
        return (2 * column + core) * self.run + group * self.width + place

    def slot(self, device_ingest, device_run):
        core, column = device_ingest % 2, device_ingest // 2
        place = device_run % self.width
        place = place + (column % 2) * (self.width - 1 - 2 * place)
        return device_run // self.width, 2 * (column * self.width + place) + core

    def splits(self):
        def parts(total, count, top):
            if count == 0:
                if total == 0:
                    yield ()
                return
            for first in range(min(top, total), 0, -1):
                for rest in parts(total - first, count - 1, first):
                    yield (first, *rest)

        return list(parts(self.pairs, self.per_group, self.reach // 2))

    def links(self):
        found = [set() for _ in range(self.reach // 2)]
        for split in self.splits():
            begin = 0
            for length in split:
                for first in range(length):
                    for second in range(first + 1, length):
                        found[second - first].add(begin + first)
                begin += length
        return [sorted(chips) for chips in found]


def cluster_starts(plan, run_len_ref):
    starts = []
    for cluster in range(plan.clusters):
        base = cluster // plan.per_group * plan.per_group
        mine = run_len_ref[cluster]
        total = jnp.int32(0)
        for other in range(base, base + plan.per_group):
            if other == cluster:
                continue
            theirs = run_len_ref[other]
            ahead = (theirs >= mine) if other < cluster else (theirs > mine)
            total = total + jnp.where(ahead, theirs, 0)
        starts.append(total)
    return starts


def row_slot(plan, run_len_ref, cluster, rank):
    starts = cluster_starts(plan, run_len_ref)
    begin = jnp.zeros_like(cluster)
    group = jnp.zeros_like(cluster)
    for number, start in enumerate(starts):
        here = cluster == number
        begin = jnp.where(here, start, begin)
        group = jnp.where(here, number // plan.per_group, group)
    return group, begin + rank // plan.rows, rank % plan.rows


def row_owner(plan, run_len_ref, cluster, rank):
    group, slot, within = row_slot(plan, run_len_ref, cluster, rank)
    return plan.device(group, slot), within


def pack_kernel(plan, run_len_ref, cluster_ref, rank_ref, rows_ref, out_ref, group_ref, unit_ref):
    step = 128

    @pl.loop(0, plan.rows // step)
    def _(number):
        here = pl.ds(pl.multiple_of(number * step, step), step)
        widened = rows_ref[here, :].astype(jnp.float32)
        total = jnp.sum(widened * widened, axis=1, keepdims=True) + EPSILON
        unit_ref[here, :] = (widened * lax.rsqrt(total)).astype(jnp.bfloat16)

    owner, within = row_owner(plan, run_len_ref, cluster_ref[...], rank_ref[...])
    number = lax.broadcasted_iota(jnp.int32, (plan.devices, plan.rows), 0)
    group = jnp.max(
        jnp.where(number == owner, within // plan.cap + 1, 0), axis=1, keepdims=True
    )
    group_ref[...] = jnp.broadcast_to(group, group_ref.shape)
    position = owner * plan.cap + within % plan.cap

    @pl.loop(0, plan.devices * plan.cap // TILE)
    def _(tile):
        row = lax.broadcasted_iota(jnp.int32, (TILE, plan.rows), 0) + tile * TILE
        chosen = jnp.where(row == position, 1.0, 0.0).astype(jnp.bfloat16)
        moved = jnp.dot(chosen, unit_ref[...], preferred_element_type=jnp.float32)
        here = pl.ds(pl.multiple_of(tile * TILE, TILE), TILE)
        out_ref[here, :] = moved.astype(jnp.bfloat16)


def sort_kernel(plan, group_ref, arrived_ref, out_ref):
    for source in range(plan.devices):
        group = group_ref[source, 0]

        @pl.when(group > 0)
        def _():
            here = pl.ds(pl.multiple_of((group - 1) * plan.cap, plan.cap), plan.cap)
            out_ref[here, :] = arrived_ref[source * plan.cap : (source + 1) * plan.cap, :]


def block_best(keys_ref, queries_ref, best_ref):
    rows = keys_ref.shape[0]

    @pl.loop(0, rows // TILE)
    def _(tile):
        keys = keys_ref[pl.ds(pl.multiple_of(tile * TILE, TILE), TILE), :]
        scores = lax.dot_general(
            keys, queries_ref[...], (((1,), (1,)), ((), ())), preferred_element_type=jnp.float32
        )
        best_ref[...] = jnp.maximum(best_ref[...], jnp.max(scores, axis=0, keepdims=True))


def triangle_best(rows_ref, best_ref):
    rows = rows_ref.shape[0]
    for first in range(0, rows, TILE):
        scores = lax.dot_general(
            rows_ref[first : first + TILE, :],
            rows_ref[first:, :],
            (((1,), (1,)), ((), ())),
            preferred_element_type=jnp.float32,
        )
        key = lax.broadcasted_iota(jnp.int32, (TILE, TILE), 0)
        query = lax.broadcasted_iota(jnp.int32, (TILE, TILE), 1)
        corner = jnp.max(
            jnp.where(key < query, scores[:, :TILE], -2.0), axis=0, keepdims=True
        )
        here = slice(first, first + TILE)
        best_ref[:, here] = jnp.maximum(best_ref[:, here], corner)
        if first + TILE < rows:
            rest = jnp.max(scores[:, TILE:], axis=0, keepdims=True)
            there = slice(first + TILE, rows)
            best_ref[:, there] = jnp.maximum(best_ref[:, there], rest)


def best_kernel(plan, run_len_ref, place_ref, group_ref, own_ref, mate_ref, *rest):
    behind, (out_ref, best_ref, blocks_ref) = rest[:-3], rest[-3:]
    group, slot = plan.slot(place_ref[0], place_ref[1])
    begin = jnp.int32(0)
    for number, start in enumerate(cluster_starts(plan, run_len_ref)):
        here = (number // plan.per_group == group) & (start <= slot)
        begin = jnp.where(here, jnp.maximum(begin, start), begin)
    best_ref[...] = jnp.full(best_ref.shape, -1.0, jnp.float32)
    triangle_best(own_ref, best_ref)

    @pl.when(slot % 2 == 1)
    def _():
        block_best(mate_ref, own_ref, best_ref)

    for distance in range(1, plan.reach // 2):
        first, second = behind[2 * distance - 2], behind[2 * distance - 1]

        @pl.when(slot - slot % 2 - 2 * distance >= begin)
        def _():
            block_best(first, own_ref, best_ref)
            block_best(second, own_ref, best_ref)

    for number in range(plan.rows // plan.cap):
        part = best_ref[:, number * plan.cap : (number + 1) * plan.cap]
        blocks_ref[number : number + 1, : plan.cap] = part
    for source in range(plan.devices):
        chosen = jnp.maximum(group_ref[source, 0] - 1, 0)
        out_ref[source : source + 1, :] = blocks_ref[pl.ds(chosen, 1), :]


def unpack_kernel(plan, run_len_ref, cluster_ref, rank_ref, reply_ref, out_ref):
    owner, within = row_owner(plan, run_len_ref, cluster_ref[...], rank_ref[...])
    number = lax.broadcasted_iota(jnp.int32, (plan.devices, plan.rows), 0)
    chosen = jnp.where(number == owner, 1.0, 0.0)
    columns = lax.dot_general(
        reply_ref[:, : plan.cap],
        chosen,
        (((0,), (0,)), ((), ())),
        precision=lax.Precision.HIGHEST,
        preferred_element_type=jnp.float32,
    )
    lane = lax.broadcasted_iota(jnp.int32, (plan.cap, plan.rows), 0)
    out_ref[...] = jnp.sum(
        jnp.where(lane == within % plan.cap, columns, 0.0), axis=0, keepdims=True
    )


def lane_of(plan, slot):
    device = plan.device(0, slot)
    return device // plan.run * plan.width + device % plan.run


def chip_change(plan, change):
    width = plan.width
    return change % width + change // (2 * width) * width, change // width % 2


def lane_change(plan, chip, core):
    width = plan.width
    return chip % width + core * width + chip // width * 2 * width


def lane_device(plan, layer, lane):
    return lane // plan.width * plan.run + layer * plan.width + lane % plan.width


def my_lane(plan):
    run = lax.axis_index("run")
    return lax.axis_index("ingest") * plan.width + run % plan.width, run // plan.width


def spread_kernel(plan, run_len_ref, cluster_ref, rank_ref, rows_ref, *rest):
    outs, (unit_ref,) = rest[:-1], rest[-1:]
    step = 128

    @pl.loop(0, plan.rows // step)
    def _(number):
        here = pl.ds(pl.multiple_of(number * step, step), step)
        widened = rows_ref[here, :].astype(jnp.float32)
        total = jnp.sum(widened * widened, axis=1, keepdims=True) + EPSILON
        unit_ref[here, :] = (widened * lax.rsqrt(total)).astype(jnp.bfloat16)

    lane, _ = my_lane(plan)
    group, slot, within = row_slot(plan, run_len_ref, cluster_ref[...], rank_ref[...])
    owner = group * plan.run + slot
    number = lax.broadcasted_iota(jnp.int32, (plan.devices, plan.rows), 0)
    member = number == owner
    block = jnp.max(jnp.where(member, within // plan.cap + 1, 0), axis=1, keepdims=True)
    present = jnp.where(block > 0, 1.0, 0.0)
    before = lax.broadcasted_iota(jnp.int32, (plan.devices, plan.devices), 0) > (
        lax.broadcasted_iota(jnp.int32, (plan.devices, plan.devices), 1)
    )
    order = jnp.dot(
        jnp.where(before, 1.0, 0.0),
        jnp.broadcast_to(present, (plan.devices, 128)),
        preferred_element_type=jnp.float32,
    )
    mine = jnp.sum(jnp.where(member, order[:, :1], 0.0), axis=0, keepdims=True)
    residue = within % plan.cap
    target = (
        (residue // plan.slice ^ lane) * plan.part
        + mine.astype(jnp.int32) * plan.slice
        + residue % plan.slice
    )
    tile = 2 * plan.part

    for pair in range(plan.lanes // 2):
        row = lax.broadcasted_iota(jnp.int32, (tile, plan.rows), 0) + pair * tile
        chosen = jnp.where(row == target, 1.0, 0.0).astype(jnp.bfloat16)
        moved = jnp.dot(chosen, unit_ref[...], preferred_element_type=jnp.float32)
        moved = moved.astype(jnp.bfloat16)
        outs[2 * pair][: plan.part, :] = moved[: plan.part, :]
        outs[2 * pair + 1][: plan.part, :] = moved[plan.part :, :]

    place = lax.broadcasted_iota(jnp.int32, (plan.devices, plan.part), 1) // plan.slice
    here = (place.astype(jnp.float32) == order[:, :1]) & (block > 0)
    who = lax.broadcasted_iota(jnp.int32, (plan.devices, plan.part), 0)
    owners = jnp.sum(jnp.where(here, who, 0), axis=0, keepdims=True)
    blocks = jnp.sum(jnp.where(here, block - 1, 0), axis=0, keepdims=True)
    line = lax.broadcasted_iota(jnp.int32, (16, plan.part), 0)
    table = jnp.where(line == 0, owners, jnp.where(line == 1, blocks, 0))
    for out in outs:
        out[plan.part :, : plan.part] = table.astype(jnp.float32).astype(jnp.bfloat16)


def permute_into(target, first, inputs_ref, outs, room, stride):
    columns = inputs_ref.shape[0]
    for number, out in enumerate(outs):
        row = lax.broadcasted_iota(jnp.int32, (room, columns), 0) + first + number * stride
        chosen = jnp.where(row == target, 1.0, 0.0).astype(jnp.bfloat16)
        moved = jnp.dot(chosen, inputs_ref[...], preferred_element_type=jnp.float32)
        out[:room, :] = moved.astype(jnp.bfloat16)


def route_kernel(plan, *refs):
    ins, rest = refs[: plan.lanes], refs[plan.lanes :]
    outs, (target_ref, inputs_ref, owner_ref, block_ref, value_ref) = rest[:-5], rest[-5:]
    _, layer = my_lane(plan)
    for number, part in enumerate(ins):
        inputs_ref[number * plan.part : (number + 1) * plan.part, :] = part[
            : plan.part, : plan.chunks[0]
        ]
        table = part[plan.part :, : plan.part].astype(jnp.float32)
        owner_ref[number : number + 1, :] = table[0:1, :].astype(jnp.int32)
        block_ref[number : number + 1, :] = table[1:2, :].astype(jnp.int32)
    owner = owner_ref[...]
    shape = (plan.part, plan.part)
    earlier = lax.broadcasted_iota(jnp.int32, shape, 0) < lax.broadcasted_iota(jnp.int32, shape, 1)
    earlier = jnp.where(earlier, 1.0, 0.0)
    ones = jnp.ones(shape, jnp.float32)
    shape = (plan.lanes, plan.lanes)
    above = lax.broadcasted_iota(jnp.int32, shape, 0) > lax.broadcasted_iota(jnp.int32, shape, 1)
    above = jnp.where(above, 1.0, 0.0)
    target = jnp.zeros(owner.shape, jnp.int32)
    most = jnp.float32(0.0)
    for other in range(plan.layers):
        chosen = owner // plan.run == other
        marks = jnp.where(chosen, 1.0, 0.0)
        lines = jnp.dot(marks, ones, preferred_element_type=jnp.float32)
        count = jnp.dot(marks, earlier, preferred_element_type=jnp.float32) + jnp.dot(
            above, lines, preferred_element_type=jnp.float32
        )
        count = count.astype(jnp.int32)
        there = jnp.where(count < plan.room, (layer ^ other) * plan.stride + count, -1)
        target = jnp.where(chosen, there, target)
        most = jnp.maximum(most, jnp.sum(marks))
    full = jnp.where(most > plan.room, 1.0, 0.0)
    value = owner % plan.run * plan.blocks + block_ref[...] + 1
    for number in range(plan.lanes):
        here = slice(number * plan.part, (number + 1) * plan.part)
        target_ref[:, here] = target[number : number + 1, :]
        value_ref[:, here] = value[number : number + 1, :].astype(jnp.float32)
    target = target_ref[...]
    values = jnp.broadcast_to(value_ref[...], (8, plan.rows)).astype(jnp.bfloat16)
    for number, out in enumerate(outs):
        row = lax.broadcasted_iota(jnp.int32, (plan.stride, plan.rows), 0) + number * plan.stride
        chosen = jnp.where(row == target, 1.0, 0.0).astype(jnp.bfloat16)
        moved = jnp.dot(
            chosen[: plan.room, :], inputs_ref[...], preferred_element_type=jnp.float32
        )
        out[: plan.room, :] = moved.astype(jnp.bfloat16)
        listed = lax.dot_general(
            values, chosen, (((1,), (1,)), ((), ())), preferred_element_type=jnp.float32
        )
        line = lax.broadcasted_iota(jnp.int32, (16, 128), 0)
        table = jnp.where(line == 15, full, 0.0)
        for piece in range(plan.stride // 128):
            here = listed[0:1, piece * 128 : (piece + 1) * 128]
            table = jnp.where(line == piece, here, table)
        out[plan.room :, :128] = table.astype(jnp.bfloat16)


def route_more_kernel(plan, target_ref, *refs, chunk):
    ins, outs, inputs_ref = refs[: plan.lanes], refs[plan.lanes : -1], refs[-1]
    first = sum(plan.chunks[:chunk])
    for number, part in enumerate(ins):
        inputs_ref[number * plan.part : (number + 1) * plan.part, :] = part[
            : plan.part, first : first + plan.chunks[chunk]
        ]
    permute_into(target_ref[...], 0, inputs_ref, outs, plan.room, plan.stride)


def gather_rows(plan, ins, inputs_ref):
    for number, part in enumerate(ins):
        first = number * plan.stride
        inputs_ref[first : first + plan.room, :] = part[: plan.room, :]
        if plan.stride > plan.room:
            inputs_ref[first + plan.room : first + plan.stride, :] = jnp.zeros(
                (plan.stride - plan.room, inputs_ref.shape[1]), jnp.bfloat16
            )


def sort_parts(plan, target, inputs_ref, outs, sorted_ref):
    tile = 2 * plan.part
    for chip, out in enumerate(outs):
        row = lax.broadcasted_iota(jnp.int32, (tile, inputs_ref.shape[0]), 0) + chip * tile
        chosen = jnp.where(row == target, 1.0, 0.0).astype(jnp.bfloat16)
        moved = jnp.dot(chosen, inputs_ref[...], preferred_element_type=jnp.float32)
        moved = moved.astype(jnp.bfloat16)
        sorted_ref[chip * tile : (chip + 1) * tile, :] = moved
        out[:tile, :] = moved
    lane, _ = my_lane(plan)
    chip, _ = chip_change(plan, lane_of(plan, 0) ^ lane)
    ahead = sorted_ref[pl.ds(pl.multiple_of(chip * tile, tile), tile), :]
    for out in outs:
        out[tile:, :] = ahead


def deliver_kernel(plan, *refs):
    ins, rest = refs[: plan.layers], refs[plan.layers :]
    outs, (target_ref, full_ref, inputs_ref, sorted_ref) = rest[:-4], rest[-4:]
    lane, _ = my_lane(plan)
    gather_rows(plan, ins, inputs_ref)
    full = jnp.zeros((8, 128), jnp.float32)
    for number, part in enumerate(ins):
        table = part[plan.room :, :128].astype(jnp.float32)
        lines = [table[piece : piece + 1, :] for piece in range(plan.stride // 128)]
        value = jnp.concatenate(lines, axis=1).astype(jnp.int32) - 1
        full = jnp.maximum(full, jnp.broadcast_to(table[15:, :], (8, 128)))
        slot = value // plan.blocks
        within = lax.broadcasted_iota(jnp.int32, value.shape, 1) % plan.slice
        chip, _ = chip_change(plan, lane_of(plan, slot) ^ lane)
        target = (2 * chip + slot % 2) * plan.part + value % plan.blocks * plan.slice + within
        target_ref[:, number * plan.stride : (number + 1) * plan.stride] = jnp.where(
            value >= 0, target, -1
        )
    full_ref[...] = full.astype(jnp.int32)
    sort_parts(plan, target_ref[...], inputs_ref, outs, sorted_ref)


def deliver_more_kernel(plan, target_ref, *refs):
    ins, rest = refs[: plan.layers], refs[plan.layers :]
    outs, (inputs_ref, sorted_ref) = rest[:-2], rest[-2:]
    gather_rows(plan, ins, inputs_ref)
    sort_parts(plan, target_ref[...], inputs_ref, outs, sorted_ref)


def join_kernel(plan, *refs):
    ins, outs = refs[:-2], refs[-2:]
    tile = 2 * plan.part
    for number, part in enumerate(ins):
        for half, out in enumerate(outs):
            out[number * tile : (number + 1) * tile, :] = part[half * tile : (half + 1) * tile, :]


def add_best(keys, queries_ref, best_ref, allowed=None):
    scores = lax.dot_general(
        keys, queries_ref[...], (((1,), (1,)), ((), ())), preferred_element_type=jnp.float32
    )
    if allowed is not None:
        scores = jnp.where(allowed, scores, -2.0)
    best_ref[...] = jnp.maximum(best_ref[...], jnp.max(scores, axis=0, keepdims=True))


def pair_best_kernel(plan, *refs):
    count = len(plan.chunks)
    own, mate = refs[:count], refs[count : 2 * count]
    queries_ref, out_ref, best_ref = refs[2 * count :]
    lane, _ = my_lane(plan)
    _, slot = plan.slot(lax.axis_index("ingest"), lax.axis_index("run"))
    core = slot % 2
    chips = plan.lanes // 2
    for side, parts in enumerate((own, mate)):
        for chip in range(chips):
            there = pl.ds(pl.multiple_of((2 * chip + core) * plan.part, plan.part), plan.part)
            here = slice((side * chips + chip) * plan.part, (side * chips + chip + 1) * plan.part)
            first = 0
            for part in parts:
                queries_ref[here, first : first + part.shape[1]] = part[there, :]
                first += part.shape[1]

    def slots(row):
        line = row // plan.part
        source = lane_change(plan, line % chips, line // chips) ^ lane
        block = row // plan.slice % plan.blocks
        return block * plan.cap + source * plan.slice + row % plan.slice

    best_ref[...] = jnp.full(best_ref.shape, -1.0, jnp.float32)
    query = slots(lax.broadcasted_iota(jnp.int32, (1, plan.rows), 1))
    for first in range(0, plan.rows, TILE):
        key = slots(lax.broadcasted_iota(jnp.int32, (TILE, 1), 0) + first)
        add_best(queries_ref[first : first + TILE, :], queries_ref, best_ref, key < query)

    @pl.when(core == 1)
    def _():
        for parts in (own, mate):
            for pair in range(0, chips, 2):
                keys = []
                for number in (pair, pair + 1):
                    here = slice(2 * number * plan.part, (2 * number + 1) * plan.part)
                    keys.append(jnp.concatenate([part[here, :] for part in parts], axis=1))
                add_best(jnp.concatenate(keys, axis=0), queries_ref, best_ref)

    out_ref[...] = best_ref[...]


def more_best_kernel(plan, run_len_ref, given_ref, queries_ref, *refs, last):
    count = len(plan.chunks)
    behind, (out_ref, best_ref) = refs[:count], refs[count : count + 2]
    group, slot = plan.slot(lax.axis_index("ingest"), lax.axis_index("run"))
    begin = jnp.int32(0)
    for number, start in enumerate(cluster_starts(plan, run_len_ref)):
        here = (number // plan.per_group == group) & (start <= slot)
        begin = jnp.where(here, jnp.maximum(begin, start), begin)
    best_ref[...] = given_ref[...]

    @pl.when(slot - slot % 2 - 2 >= begin)
    def _():
        for first in range(0, plan.rows, TILE):
            keys = [part[first : first + TILE, :] for part in behind]
            add_best(jnp.concatenate(keys, axis=1), queries_ref, best_ref)

    if not last:
        out_ref[...] = best_ref[...]
        return
    lines_ref = refs[-1]
    for number in range(plan.lanes):
        lines_ref[number : number + 1, :] = best_ref[
            :, number * plan.part : (number + 1) * plan.part
        ]
    for device in range(plan.devices):
        out_ref[device] = lines_ref[...]


def staged_unpack_kernel(plan, run_len_ref, cluster_ref, rank_ref, reply_ref, out_ref):
    group, slot, within = row_slot(plan, run_len_ref, cluster_ref[...], rank_ref[...])
    residue = within % plan.cap
    chip, core = chip_change(plan, residue // plan.slice ^ lane_of(plan, slot))
    line = plan.device(group, slot) * plan.lanes + core * (plan.lanes // 2) + chip
    column = within // plan.cap * plan.slice + residue % plan.slice
    number = lax.broadcasted_iota(jnp.int32, (plan.devices * plan.lanes, plan.rows), 0)
    columns = lax.dot_general(
        reply_ref[...],
        jnp.where(number == line, 1.0, 0.0),
        (((0,), (0,)), ((), ())),
        precision=lax.Precision.HIGHEST,
        preferred_element_type=jnp.float32,
    )
    place = lax.broadcasted_iota(jnp.int32, (plan.part, plan.rows), 0)
    out_ref[...] = jnp.sum(jnp.where(place == column, columns, 0.0), axis=0, keepdims=True)


SMEM = pl.BlockSpec(memory_space=pltpu.SMEM)
VMEM = pl.BlockSpec(memory_space=pltpu.VMEM)


def call(kernel, plan, shapes, specs, scratch=(), flops=0, moved=0, memory=32):
    return pl.pallas_call(
        functools.partial(kernel, plan),
        out_shape=shapes,
        in_specs=specs,
        out_specs=[VMEM] * len(shapes),
        scratch_shapes=scratch,
        compiler_params=pltpu.CompilerParams(vmem_limit_bytes=memory * MIB),
        cost_estimate=pl.CostEstimate(flops=flops, bytes_accessed=moved, transcendentals=0),
    )


def exchange(block):
    return lax.all_to_all(block, AXES, split_axis=0, concat_axis=0, tiled=True)


def direct(plan, embeddings, clusters, ranks, run_len):
    rows, width = embeddings.shape
    slots = plan.devices * plan.cap
    wide = jax.ShapeDtypeStruct
    outgoing, groups = call(
        pack_kernel,
        plan,
        [wide((slots, width), jnp.bfloat16), wide((plan.devices, 128), jnp.int32)],
        [SMEM, VMEM, VMEM, VMEM],
        [pltpu.VMEM((rows, width), jnp.bfloat16)],
        2 * slots * rows * width,
        3 * rows * width * 2,
    )(run_len, clusters, ranks, embeddings)
    groups = exchange(groups)
    arrived = exchange(outgoing)
    (own,) = call(
        sort_kernel, plan, [wide((rows, width), jnp.bfloat16)], [SMEM, VMEM],
        moved=3 * rows * width * 2,
    )(groups, arrived)

    def swap(block):
        pairs = [
            (i * plan.run + r, (i ^ 1) * plan.run + r)
            for i in range(plan.ingest)
            for r in range(plan.run)
        ]
        return lax.ppermute(block, AXES, pairs)

    mate = swap(own)
    behind = []
    for distance, chips in enumerate(plan.links()):
        if distance == 0:
            continue
        pairs = [
            (plan.device(i, 2 * chip + core), plan.device(i, 2 * (chip + distance) + core))
            for i in range(plan.ingest)
            for chip in chips
            for core in range(2)
        ]
        moved = lax.ppermute(own, AXES, pairs)
        behind += [moved, swap(moved)]
    place = jnp.stack([lax.axis_index("ingest"), lax.axis_index("run")]).astype(jnp.int32)
    (replies,) = call(
        best_kernel,
        plan,
        [wide((plan.devices, 128), jnp.float32)],
        [SMEM, SMEM, SMEM] + [VMEM] * (2 + len(behind)),
        [pltpu.VMEM((1, rows), jnp.float32), pltpu.VMEM((rows // plan.cap, 128), jnp.float32)],
        2 * rows * rows * width * 3,
        4 * rows * width * 2,
    )(run_len, place, groups, own, mate, *behind)
    returned = exchange(replies)
    (best,) = call(
        unpack_kernel, plan, [wide((1, rows), jnp.float32)], [SMEM, VMEM, VMEM, VMEM],
        moved=4 * rows * 4,
    )(run_len, clusters, ranks, returned)
    return best


def staged(plan, embeddings, clusters, ranks, run_len):
    rows, width = embeddings.shape
    wide = jax.ShapeDtypeStruct
    half = jnp.bfloat16
    lanes, layers = range(plan.lanes), range(plan.layers)

    def along_lanes(block, change):
        pairs = [
            (lane_device(plan, layer, lane), lane_device(plan, layer, lane ^ change))
            for layer in layers
            for lane in lanes
        ]
        return lax.ppermute(block, AXES, pairs)

    def along_layers(block, change):
        pairs = [
            (lane_device(plan, layer, lane), lane_device(plan, layer ^ change, lane))
            for layer in layers
            for lane in lanes
        ]
        return lax.ppermute(block, AXES, pairs)

    far_first = sorted(lanes, key=lambda change: -(change & 1) - (change // plan.width // 2))

    spread = call(
        spread_kernel,
        plan,
        [wide((plan.part + 16, width), half) for _ in lanes],
        [SMEM, VMEM, VMEM, VMEM],
        [pltpu.VMEM((rows, width), half)],
        2 * rows * rows * width,
        3 * rows * width * 2,
    )(run_len, clusters, ranks, embeddings)
    swapped = {change: along_lanes(spread[change], change) for change in far_first if change}
    spread = [spread[0]] + [swapped[change] for change in lanes[1:]]
    pair, mates, behind, fars = [], [], [], []
    table = targets = full = None
    arrivals = []
    for chunk, f in enumerate(plan.chunks):
        spec = dict(flops=2 * rows * rows * f, moved=3 * rows * f * 2, memory=12)
        rooms = [wide((plan.room + (0 if chunk else 16), f), half) for _ in layers]
        inputs = pltpu.VMEM((rows, f), half)
        if chunk == 0:
            *routed, table = call(
                route_kernel,
                plan,
                [*rooms, wide((1, rows), jnp.int32)],
                [VMEM] * plan.lanes,
                [
                    inputs,
                    pltpu.VMEM((plan.lanes, plan.part), jnp.int32),
                    pltpu.VMEM((plan.lanes, plan.part), jnp.int32),
                    pltpu.VMEM((1, rows), jnp.float32),
                ],
                **spec,
            )(*spread)
        else:
            more = functools.partial(route_more_kernel, chunk=chunk)
            routed = call(more, plan, rooms, [VMEM] * (1 + plan.lanes), [inputs], **spec)(
                table, *spread
            )
        moved = {change: along_layers(routed[change], change) for change in reversed(layers[1:])}
        arrived = [routed[0]] + [moved[change] for change in layers[1:]]
        arrivals.append(arrived)
    for chunk, f in enumerate(plan.chunks):
        spec = dict(flops=2 * rows * rows * f, moved=3 * rows * f * 2, memory=12)
        inputs = pltpu.VMEM((rows, f), half)
        arrived = arrivals[chunk]
        if chunk:
            arrived, _ = lax.optimization_barrier((arrived, parts))
        shapes = [wide((4 * plan.part, f), half) for _ in range(plan.lanes // 2)]
        scratch = [pltpu.VMEM((plan.layers * plan.stride, f), half), inputs]
        if chunk == 0:
            *parts, targets, full = call(
                deliver_kernel,
                plan,
                [
                    *shapes,
                    wide((1, plan.layers * plan.stride), jnp.int32),
                    wide((8, 128), jnp.int32),
                ],
                [VMEM] * plan.layers,
                scratch,
                **spec,
            )(*arrived)
        else:
            parts = call(
                deliver_more_kernel, plan, shapes, [VMEM] * (1 + plan.layers), scratch, **spec
            )(targets, *arrived)
        parts = [
            along_lanes(part, lane_change(plan, chip, 0)) if chip else part
            for chip, part in enumerate(parts)
        ]
        spec = dict(moved=8 * rows * f * 2, memory=8)
        joined = call(
            join_kernel, plan, [wide((rows, f), half)] * 2, [VMEM] * len(parts), **spec
        )(*parts)
        for kept, block in zip((pair, behind), joined):
            kept.append(block)
        for kept, block in zip((mates, fars), joined):
            kept.append(along_lanes(block, plan.width))
    line = wide((1, rows), jnp.float32)
    kept = pltpu.VMEM((1, rows), jnp.float32)
    count = len(plan.chunks)
    spec = dict(flops=4 * rows * rows * width, moved=3 * rows * width * 2, memory=24)
    queries, best = call(
        pair_best_kernel,
        plan,
        [wide((rows, width), half), line],
        [VMEM] * (2 * count),
        [kept],
        **spec,
    )(*pair, *mates)
    spec = dict(flops=2 * rows * rows * width, moved=3 * rows * width * 2, memory=24)
    places = [SMEM] + [VMEM] * (2 + count)
    (best,) = call(
        functools.partial(more_best_kernel, last=False), plan, [line], places, [kept], **spec
    )(run_len, best, queries, *behind)
    (replies,) = call(
        functools.partial(more_best_kernel, last=True),
        plan,
        [wide((plan.devices, plan.lanes, 128), jnp.float32)],
        places,
        [kept, pltpu.VMEM((plan.lanes, 128), jnp.float32)],
        **spec,
    )(run_len, best, queries, *fars)
    returned = exchange(replies).reshape(plan.devices * plan.lanes, 128)
    (best,) = call(
        staged_unpack_kernel,
        plan,
        [wide((1, rows), jnp.float32)],
        [SMEM, VMEM, VMEM, VMEM],
        moved=4 * rows * 4,
        memory=8,
    )(run_len, clusters, ranks, returned)
    return best, full[0, 0]


def local(embeddings, cluster_id, rank, run_len):
    rows, width = embeddings.shape
    plan = Plan(lax.axis_size("ingest"), lax.axis_size("run"), run_len.shape[0], rows, width)
    given = (embeddings, cluster_id.reshape(1, rows), rank.reshape(1, rows), run_len)
    if not plan.staged():
        return direct(plan, *given).reshape(rows)
    best, full = staged(plan, *given)
    best = lax.cond(full > 0, lambda: direct(plan, *given), lambda: best)
    return best.reshape(rows)


def solution(mesh):
    return jax.shard_map(
        local,
        mesh=mesh,
        in_specs=(P(AXES, None), P(AXES), P(AXES), P()),
        out_specs=P(AXES),
        check_vma=False,
    )
```

```python
import functools

import jax
import jax.numpy as jnp
from jax import lax
from jax.experimental import pallas as pl
from jax.experimental.pallas import tpu as pltpu
from jax.sharding import PartitionSpec as P

EPSILON = 1e-06
AXES = ("ingest", "run")
TILE = 256
SHARES = (1, 1, 1)
MIB = 1024 * 1024


class Plan:
    def __init__(self, ingest, run, clusters, rows, features):
        self.ingest, self.run, self.clusters, self.rows = ingest, run, clusters, rows
        self.devices = ingest * run
        self.per_group = clusters // ingest
        self.cap = 2 * rows // self.devices
        self.reach = min(8, run // 2)
        self.width = run // ingest
        self.pairs = run // 2
        self.blocks = rows // self.cap
        self.layers, self.lanes = ingest, ingest * self.width
        self.slice = self.cap // self.lanes
        self.part = self.blocks * self.slice
        self.chunks = tuple(features * share // sum(SHARES) for share in SHARES)
        mean = rows // self.layers
        self.room = mean + mean // 8
        self.stride = -(-self.room // 128) * 128

    def staged(self):
        powers = all(n & (n - 1) == 0 for n in (self.layers, self.lanes, self.width))
        return (
            powers
            and self.cap % (8 * self.lanes) == 0
            and self.part == 128
            and self.room % 16 == 0
            and all(width % 128 == 0 for width in self.chunks)
            and self.links()[1:] == [[0]]
        )

    def device(self, group, slot):
        core, chip = slot % 2, slot // 2
        column, place = chip // self.width, chip % self.width
        odd = column % 2
        place = place + odd * (self.width - 1 - 2 * place)
        return (2 * column + core) * self.run + group * self.width + place

    def slot(self, device_ingest, device_run):
        core, column = device_ingest % 2, device_ingest // 2
        place = device_run % self.width
        place = place + (column % 2) * (self.width - 1 - 2 * place)
        return device_run // self.width, 2 * (column * self.width + place) + core

    def splits(self):
        def parts(total, count, top):
            if count == 0:
                if total == 0:
                    yield ()
                return
            for first in range(min(top, total), 0, -1):
                for rest in parts(total - first, count - 1, first):
                    yield (first, *rest)

        return list(parts(self.pairs, self.per_group, self.reach // 2))

    def links(self):
        found = [set() for _ in range(self.reach // 2)]
        for split in self.splits():
            begin = 0
            for length in split:
                for first in range(length):
                    for second in range(first + 1, length):
                        found[second - first].add(begin + first)
                begin += length
        return [sorted(chips) for chips in found]


def cluster_starts(plan, run_len_ref):
    starts = []
    for cluster in range(plan.clusters):
        base = cluster // plan.per_group * plan.per_group
        mine = run_len_ref[cluster]
        total = jnp.int32(0)
        for other in range(base, base + plan.per_group):
            if other == cluster:
                continue
            theirs = run_len_ref[other]
            ahead = (theirs >= mine) if other < cluster else (theirs > mine)
            total = total + jnp.where(ahead, theirs, 0)
        starts.append(total)
    return starts


def row_slot(plan, run_len_ref, cluster, rank):
    starts = cluster_starts(plan, run_len_ref)
    begin = jnp.zeros_like(cluster)
    group = jnp.zeros_like(cluster)
    for number, start in enumerate(starts):
        here = cluster == number
        begin = jnp.where(here, start, begin)
        group = jnp.where(here, number // plan.per_group, group)
    return group, begin + rank // plan.rows, rank % plan.rows


def row_owner(plan, run_len_ref, cluster, rank):
    group, slot, within = row_slot(plan, run_len_ref, cluster, rank)
    return plan.device(group, slot), within


def pack_kernel(plan, run_len_ref, cluster_ref, rank_ref, rows_ref, out_ref, group_ref, unit_ref):
    step = 128

    @pl.loop(0, plan.rows // step)
    def _(number):
        here = pl.ds(pl.multiple_of(number * step, step), step)
        widened = rows_ref[here, :].astype(jnp.float32)
        total = jnp.sum(widened * widened, axis=1, keepdims=True) + EPSILON
        unit_ref[here, :] = (widened * lax.rsqrt(total)).astype(jnp.bfloat16)

    owner, within = row_owner(plan, run_len_ref, cluster_ref[...], rank_ref[...])
    number = lax.broadcasted_iota(jnp.int32, (plan.devices, plan.rows), 0)
    group = jnp.max(
        jnp.where(number == owner, within // plan.cap + 1, 0), axis=1, keepdims=True
    )
    group_ref[...] = jnp.broadcast_to(group, group_ref.shape)
    position = owner * plan.cap + within % plan.cap

    @pl.loop(0, plan.devices * plan.cap // TILE)
    def _(tile):
        row = lax.broadcasted_iota(jnp.int32, (TILE, plan.rows), 0) + tile * TILE
        chosen = jnp.where(row == position, 1.0, 0.0).astype(jnp.bfloat16)
        moved = jnp.dot(chosen, unit_ref[...], preferred_element_type=jnp.float32)
        here = pl.ds(pl.multiple_of(tile * TILE, TILE), TILE)
        out_ref[here, :] = moved.astype(jnp.bfloat16)


def sort_kernel(plan, group_ref, arrived_ref, out_ref):
    for source in range(plan.devices):
        group = group_ref[source, 0]

        @pl.when(group > 0)
        def _():
            here = pl.ds(pl.multiple_of((group - 1) * plan.cap, plan.cap), plan.cap)
            out_ref[here, :] = arrived_ref[source * plan.cap : (source + 1) * plan.cap, :]


def block_best(keys_ref, queries_ref, best_ref):
    rows = keys_ref.shape[0]

    @pl.loop(0, rows // TILE)
    def _(tile):
        keys = keys_ref[pl.ds(pl.multiple_of(tile * TILE, TILE), TILE), :]
        scores = lax.dot_general(
            keys, queries_ref[...], (((1,), (1,)), ((), ())), preferred_element_type=jnp.float32
        )
        best_ref[...] = jnp.maximum(best_ref[...], jnp.max(scores, axis=0, keepdims=True))


def triangle_best(rows_ref, best_ref):
    rows = rows_ref.shape[0]
    for first in range(0, rows, TILE):
        scores = lax.dot_general(
            rows_ref[first : first + TILE, :],
            rows_ref[first:, :],
            (((1,), (1,)), ((), ())),
            preferred_element_type=jnp.float32,
        )
        key = lax.broadcasted_iota(jnp.int32, (TILE, TILE), 0)
        query = lax.broadcasted_iota(jnp.int32, (TILE, TILE), 1)
        corner = jnp.max(
            jnp.where(key < query, scores[:, :TILE], -2.0), axis=0, keepdims=True
        )
        here = slice(first, first + TILE)
        best_ref[:, here] = jnp.maximum(best_ref[:, here], corner)
        if first + TILE < rows:
            rest = jnp.max(scores[:, TILE:], axis=0, keepdims=True)
            there = slice(first + TILE, rows)
            best_ref[:, there] = jnp.maximum(best_ref[:, there], rest)


def best_kernel(plan, run_len_ref, place_ref, group_ref, own_ref, mate_ref, *rest):
    behind, (out_ref, best_ref, blocks_ref) = rest[:-3], rest[-3:]
    group, slot = plan.slot(place_ref[0], place_ref[1])
    begin = jnp.int32(0)
    for number, start in enumerate(cluster_starts(plan, run_len_ref)):
        here = (number // plan.per_group == group) & (start <= slot)
        begin = jnp.where(here, jnp.maximum(begin, start), begin)
    best_ref[...] = jnp.full(best_ref.shape, -1.0, jnp.float32)
    triangle_best(own_ref, best_ref)

    @pl.when(slot % 2 == 1)
    def _():
        block_best(mate_ref, own_ref, best_ref)

    for distance in range(1, plan.reach // 2):
        first, second = behind[2 * distance - 2], behind[2 * distance - 1]

        @pl.when(slot - slot % 2 - 2 * distance >= begin)
        def _():
            block_best(first, own_ref, best_ref)
            block_best(second, own_ref, best_ref)

    for number in range(plan.rows // plan.cap):
        part = best_ref[:, number * plan.cap : (number + 1) * plan.cap]
        blocks_ref[number : number + 1, : plan.cap] = part
    for source in range(plan.devices):
        chosen = jnp.maximum(group_ref[source, 0] - 1, 0)
        out_ref[source : source + 1, :] = blocks_ref[pl.ds(chosen, 1), :]


def unpack_kernel(plan, run_len_ref, cluster_ref, rank_ref, reply_ref, out_ref):
    owner, within = row_owner(plan, run_len_ref, cluster_ref[...], rank_ref[...])
    number = lax.broadcasted_iota(jnp.int32, (plan.devices, plan.rows), 0)
    chosen = jnp.where(number == owner, 1.0, 0.0)
    columns = lax.dot_general(
        reply_ref[:, : plan.cap],
        chosen,
        (((0,), (0,)), ((), ())),
        precision=lax.Precision.HIGHEST,
        preferred_element_type=jnp.float32,
    )
    lane = lax.broadcasted_iota(jnp.int32, (plan.cap, plan.rows), 0)
    out_ref[...] = jnp.sum(
        jnp.where(lane == within % plan.cap, columns, 0.0), axis=0, keepdims=True
    )


def lane_of(plan, slot):
    device = plan.device(0, slot)
    return device // plan.run * plan.width + device % plan.run


def chip_change(plan, change):
    width = plan.width
    return change % width + change // (2 * width) * width, change // width % 2


def lane_change(plan, chip, core):
    width = plan.width
    return chip % width + core * width + chip // width * 2 * width


def lane_device(plan, layer, lane):
    return lane // plan.width * plan.run + layer * plan.width + lane % plan.width


def my_lane(plan):
    run = lax.axis_index("run")
    return lax.axis_index("ingest") * plan.width + run % plan.width, run // plan.width


def spread_kernel(plan, run_len_ref, cluster_ref, rank_ref, rows_ref, *rest):
    outs, (unit_ref,) = rest[:-1], rest[-1:]
    step = 128

    @pl.loop(0, plan.rows // step)
    def _(number):
        here = pl.ds(pl.multiple_of(number * step, step), step)
        widened = rows_ref[here, :].astype(jnp.float32)
        total = jnp.sum(widened * widened, axis=1, keepdims=True) + EPSILON
        unit_ref[here, :] = (widened * lax.rsqrt(total)).astype(jnp.bfloat16)

    lane, _ = my_lane(plan)
    group, slot, within = row_slot(plan, run_len_ref, cluster_ref[...], rank_ref[...])
    owner = group * plan.run + slot
    number = lax.broadcasted_iota(jnp.int32, (plan.devices, plan.rows), 0)
    member = number == owner
    block = jnp.max(jnp.where(member, within // plan.cap + 1, 0), axis=1, keepdims=True)
    present = jnp.where(block > 0, 1.0, 0.0)
    before = lax.broadcasted_iota(jnp.int32, (plan.devices, plan.devices), 0) > (
        lax.broadcasted_iota(jnp.int32, (plan.devices, plan.devices), 1)
    )
    order = jnp.dot(
        jnp.where(before, 1.0, 0.0),
        jnp.broadcast_to(present, (plan.devices, 128)),
        preferred_element_type=jnp.float32,
    )
    mine = jnp.sum(jnp.where(member, order[:, :1], 0.0), axis=0, keepdims=True)
    residue = within % plan.cap
    target = (
        (residue // plan.slice ^ lane) * plan.part
        + mine.astype(jnp.int32) * plan.slice
        + residue % plan.slice
    )
    tile = 2 * plan.part

    for pair in range(plan.lanes // 2):
        row = lax.broadcasted_iota(jnp.int32, (tile, plan.rows), 0) + pair * tile
        chosen = jnp.where(row == target, 1.0, 0.0).astype(jnp.bfloat16)
        moved = jnp.dot(chosen, unit_ref[...], preferred_element_type=jnp.float32)
        moved = moved.astype(jnp.bfloat16)
        for number in range(2):
            here = moved[number * plan.part : (number + 1) * plan.part, :]
            outs[2 * pair + number][: plan.part, :] = here[:, : plan.chunks[0]]
            whole = (2 * pair + number ^ lane) * plan.part
            there = pl.ds(pl.multiple_of(whole, plan.part), plan.part)
            outs[plan.lanes][there, :] = here[:, plan.chunks[0] :]

    place = lax.broadcasted_iota(jnp.int32, (plan.devices, plan.part), 1) // plan.slice
    here = (place.astype(jnp.float32) == order[:, :1]) & (block > 0)
    who = lax.broadcasted_iota(jnp.int32, (plan.devices, plan.part), 0)
    owners = jnp.sum(jnp.where(here, who, 0), axis=0, keepdims=True)
    blocks = jnp.sum(jnp.where(here, block - 1, 0), axis=0, keepdims=True)
    line = lax.broadcasted_iota(jnp.int32, (16, plan.part), 0)
    table = jnp.where(line == 0, owners, jnp.where(line == 1, blocks, 0))
    for out in outs[: plan.lanes]:
        out[plan.part :, : plan.part] = table.astype(jnp.float32).astype(jnp.bfloat16)


def permute_into(target, first, inputs_ref, outs, room, stride):
    columns = inputs_ref.shape[0]
    for number, out in enumerate(outs):
        row = lax.broadcasted_iota(jnp.int32, (room, columns), 0) + first + number * stride
        chosen = jnp.where(row == target, 1.0, 0.0).astype(jnp.bfloat16)
        moved = jnp.dot(chosen, inputs_ref[...], preferred_element_type=jnp.float32)
        out[:room, :] = moved.astype(jnp.bfloat16)


def route_kernel(plan, *refs):
    ins, rest = refs[: plan.lanes], refs[plan.lanes :]
    outs, (target_ref, inputs_ref, owner_ref, block_ref, value_ref) = rest[:-5], rest[-5:]
    _, layer = my_lane(plan)
    for number, part in enumerate(ins):
        inputs_ref[number * plan.part : (number + 1) * plan.part, :] = part[: plan.part, :]
        table = part[plan.part :, : plan.part].astype(jnp.float32)
        owner_ref[number : number + 1, :] = table[0:1, :].astype(jnp.int32)
        block_ref[number : number + 1, :] = table[1:2, :].astype(jnp.int32)
    owner = owner_ref[...]
    shape = (plan.part, plan.part)
    earlier = lax.broadcasted_iota(jnp.int32, shape, 0) < lax.broadcasted_iota(jnp.int32, shape, 1)
    earlier = jnp.where(earlier, 1.0, 0.0)
    ones = jnp.ones(shape, jnp.float32)
    shape = (plan.lanes, plan.lanes)
    above = lax.broadcasted_iota(jnp.int32, shape, 0) > lax.broadcasted_iota(jnp.int32, shape, 1)
    above = jnp.where(above, 1.0, 0.0)
    target = jnp.zeros(owner.shape, jnp.int32)
    most = jnp.float32(0.0)
    for other in range(plan.layers):
        chosen = owner // plan.run == other
        marks = jnp.where(chosen, 1.0, 0.0)
        lines = jnp.dot(marks, ones, preferred_element_type=jnp.float32)
        count = jnp.dot(marks, earlier, preferred_element_type=jnp.float32) + jnp.dot(
            above, lines, preferred_element_type=jnp.float32
        )
        count = count.astype(jnp.int32)
        there = jnp.where(count < plan.room, (layer ^ other) * plan.stride + count, -1)
        target = jnp.where(chosen, there, target)
        most = jnp.maximum(most, jnp.sum(marks))
    full = jnp.where(most > plan.room, 1.0, 0.0)
    value = owner % plan.run * plan.blocks + block_ref[...] + 1
    for number in range(plan.lanes):
        here = slice(number * plan.part, (number + 1) * plan.part)
        target_ref[:, here] = target[number : number + 1, :]
        value_ref[:, here] = value[number : number + 1, :].astype(jnp.float32)
    target = target_ref[...]
    values = jnp.broadcast_to(value_ref[...], (8, plan.rows)).astype(jnp.bfloat16)
    for number, out in enumerate(outs):
        row = lax.broadcasted_iota(jnp.int32, (plan.stride, plan.rows), 0) + number * plan.stride
        chosen = jnp.where(row == target, 1.0, 0.0).astype(jnp.bfloat16)
        moved = jnp.dot(
            chosen[: plan.room, :], inputs_ref[...], preferred_element_type=jnp.float32
        )
        out[: plan.room, :] = moved.astype(jnp.bfloat16)
        listed = lax.dot_general(
            values, chosen, (((1,), (1,)), ((), ())), preferred_element_type=jnp.float32
        )
        line = lax.broadcasted_iota(jnp.int32, (16, 128), 0)
        table = jnp.where(line == 15, full, 0.0)
        for piece in range(plan.stride // 128):
            here = listed[0:1, piece * 128 : (piece + 1) * 128]
            table = jnp.where(line == piece, here, table)
        out[plan.room :, :128] = table.astype(jnp.bfloat16)


def route_more_kernel(plan, target_ref, rows_ref, *refs, chunk):
    outs, inputs_ref = refs[:-1], refs[-1]
    lane, _ = my_lane(plan)
    first = sum(plan.chunks[1:chunk])
    for number in range(plan.lanes):
        whole = pl.multiple_of((number ^ lane) * plan.part, plan.part)
        inputs_ref[number * plan.part : (number + 1) * plan.part, :] = rows_ref[
            pl.ds(whole, plan.part), first : first + plan.chunks[chunk]
        ]
    permute_into(target_ref[...], 0, inputs_ref, outs, plan.room, plan.stride)


def gather_rows(plan, ins, inputs_ref):
    for number, part in enumerate(ins):
        first = number * plan.stride
        inputs_ref[first : first + plan.room, :] = part[: plan.room, :]
        if plan.stride > plan.room:
            inputs_ref[first + plan.room : first + plan.stride, :] = jnp.zeros(
                (plan.stride - plan.room, inputs_ref.shape[1]), jnp.bfloat16
            )


def sort_parts(plan, target, inputs_ref, outs, sorted_ref):
    tile = 2 * plan.part
    for chip, out in enumerate(outs):
        row = lax.broadcasted_iota(jnp.int32, (tile, inputs_ref.shape[0]), 0) + chip * tile
        chosen = jnp.where(row == target, 1.0, 0.0).astype(jnp.bfloat16)
        moved = jnp.dot(chosen, inputs_ref[...], preferred_element_type=jnp.float32)
        moved = moved.astype(jnp.bfloat16)
        sorted_ref[chip * tile : (chip + 1) * tile, :] = moved
        out[:tile, :] = moved
    lane, _ = my_lane(plan)
    chip, _ = chip_change(plan, lane_of(plan, 0) ^ lane)
    ahead = sorted_ref[pl.ds(pl.multiple_of(chip * tile, tile), tile), :]
    for out in outs:
        out[tile:, :] = ahead


def deliver_kernel(plan, *refs):
    ins, rest = refs[: plan.layers], refs[plan.layers :]
    outs, (target_ref, full_ref, inputs_ref, sorted_ref) = rest[:-4], rest[-4:]
    lane, _ = my_lane(plan)
    gather_rows(plan, ins, inputs_ref)
    full = jnp.zeros((8, 128), jnp.float32)
    for number, part in enumerate(ins):
        table = part[plan.room :, :128].astype(jnp.float32)
        lines = [table[piece : piece + 1, :] for piece in range(plan.stride // 128)]
        value = jnp.concatenate(lines, axis=1).astype(jnp.int32) - 1
        full = jnp.maximum(full, jnp.broadcast_to(table[15:, :], (8, 128)))
        slot = value // plan.blocks
        within = lax.broadcasted_iota(jnp.int32, value.shape, 1) % plan.slice
        chip, _ = chip_change(plan, lane_of(plan, slot) ^ lane)
        target = (2 * chip + slot % 2) * plan.part + value % plan.blocks * plan.slice + within
        target_ref[:, number * plan.stride : (number + 1) * plan.stride] = jnp.where(
            value >= 0, target, -1
        )
    full_ref[...] = full.astype(jnp.int32)
    sort_parts(plan, target_ref[...], inputs_ref, outs, sorted_ref)


def deliver_more_kernel(plan, target_ref, *refs):
    ins, rest = refs[: plan.layers], refs[plan.layers :]
    outs, (inputs_ref, sorted_ref) = rest[:-2], rest[-2:]
    gather_rows(plan, ins, inputs_ref)
    sort_parts(plan, target_ref[...], inputs_ref, outs, sorted_ref)


def join_kernel(plan, *refs):
    ins, outs = refs[:-2], refs[-2:]
    tile = 2 * plan.part
    for number, part in enumerate(ins):
        for half, out in enumerate(outs):
            out[number * tile : (number + 1) * tile, :] = part[half * tile : (half + 1) * tile, :]


def add_best(keys, queries_ref, best_ref, allowed=None):
    scores = lax.dot_general(
        keys, queries_ref[...], (((1,), (1,)), ((), ())), preferred_element_type=jnp.float32
    )
    if allowed is not None:
        scores = jnp.where(allowed, scores, -2.0)
    best_ref[...] = jnp.maximum(best_ref[...], jnp.max(scores, axis=0, keepdims=True))


def pair_best_kernel(plan, *refs):
    count = len(plan.chunks)
    own, mate = refs[:count], refs[count : 2 * count]
    queries_ref, out_ref, best_ref = refs[2 * count :]
    lane, _ = my_lane(plan)
    _, slot = plan.slot(lax.axis_index("ingest"), lax.axis_index("run"))
    core = slot % 2
    chips = plan.lanes // 2
    for side, parts in enumerate((own, mate)):
        for chip in range(chips):
            there = pl.ds(pl.multiple_of((2 * chip + core) * plan.part, plan.part), plan.part)
            here = slice((side * chips + chip) * plan.part, (side * chips + chip + 1) * plan.part)
            first = 0
            for part in parts:
                queries_ref[here, first : first + part.shape[1]] = part[there, :]
                first += part.shape[1]

    def slots(row):
        line = row // plan.part
        source = lane_change(plan, line % chips, line // chips) ^ lane
        block = row // plan.slice % plan.blocks
        return block * plan.cap + source * plan.slice + row % plan.slice

    best_ref[...] = jnp.full(best_ref.shape, -1.0, jnp.float32)
    query = slots(lax.broadcasted_iota(jnp.int32, (1, plan.rows), 1))
    for first in range(0, plan.rows, TILE):
        key = slots(lax.broadcasted_iota(jnp.int32, (TILE, 1), 0) + first)
        add_best(queries_ref[first : first + TILE, :], queries_ref, best_ref, key < query)

    @pl.when(core == 1)
    def _():
        for parts in (own, mate):
            for pair in range(0, chips, 2):
                keys = []
                for number in (pair, pair + 1):
                    here = slice(2 * number * plan.part, (2 * number + 1) * plan.part)
                    keys.append(jnp.concatenate([part[here, :] for part in parts], axis=1))
                add_best(jnp.concatenate(keys, axis=0), queries_ref, best_ref)

    out_ref[...] = best_ref[...]


def more_best_kernel(plan, run_len_ref, given_ref, queries_ref, *refs, last):
    count = len(plan.chunks)
    behind, (out_ref, best_ref) = refs[:count], refs[count : count + 2]
    group, slot = plan.slot(lax.axis_index("ingest"), lax.axis_index("run"))
    begin = jnp.int32(0)
    for number, start in enumerate(cluster_starts(plan, run_len_ref)):
        here = (number // plan.per_group == group) & (start <= slot)
        begin = jnp.where(here, jnp.maximum(begin, start), begin)
    best_ref[...] = given_ref[...]

    @pl.when(slot - slot % 2 - 2 >= begin)
    def _():
        for first in range(0, plan.rows, TILE):
            keys = [part[first : first + TILE, :] for part in behind]
            add_best(jnp.concatenate(keys, axis=1), queries_ref, best_ref)

    if not last:
        out_ref[...] = best_ref[...]
        return
    lines_ref = refs[-1]
    for number in range(plan.lanes):
        lines_ref[number : number + 1, :] = best_ref[
            :, number * plan.part : (number + 1) * plan.part
        ]
    for device in range(plan.devices):
        out_ref[device] = lines_ref[...]


def staged_unpack_kernel(plan, run_len_ref, cluster_ref, rank_ref, reply_ref, out_ref):
    group, slot, within = row_slot(plan, run_len_ref, cluster_ref[...], rank_ref[...])
    residue = within % plan.cap
    chip, core = chip_change(plan, residue // plan.slice ^ lane_of(plan, slot))
    line = plan.device(group, slot) * plan.lanes + core * (plan.lanes // 2) + chip
    column = within // plan.cap * plan.slice + residue % plan.slice
    number = lax.broadcasted_iota(jnp.int32, (plan.devices * plan.lanes, plan.rows), 0)
    columns = lax.dot_general(
        reply_ref[...],
        jnp.where(number == line, 1.0, 0.0),
        (((0,), (0,)), ((), ())),
        precision=lax.Precision.HIGHEST,
        preferred_element_type=jnp.float32,
    )
    place = lax.broadcasted_iota(jnp.int32, (plan.part, plan.rows), 0)
    out_ref[...] = jnp.sum(jnp.where(place == column, columns, 0.0), axis=0, keepdims=True)


SMEM = pl.BlockSpec(memory_space=pltpu.SMEM)
VMEM = pl.BlockSpec(memory_space=pltpu.VMEM)


def call(kernel, plan, shapes, specs, scratch=(), flops=0, moved=0, memory=32):
    return pl.pallas_call(
        functools.partial(kernel, plan),
        out_shape=shapes,
        in_specs=specs,
        out_specs=[VMEM] * len(shapes),
        scratch_shapes=scratch,
        compiler_params=pltpu.CompilerParams(vmem_limit_bytes=memory * MIB),
        cost_estimate=pl.CostEstimate(flops=flops, bytes_accessed=moved, transcendentals=0),
    )


def exchange(block):
    return lax.all_to_all(block, AXES, split_axis=0, concat_axis=0, tiled=True)


def direct(plan, embeddings, clusters, ranks, run_len):
    rows, width = embeddings.shape
    slots = plan.devices * plan.cap
    wide = jax.ShapeDtypeStruct
    outgoing, groups = call(
        pack_kernel,
        plan,
        [wide((slots, width), jnp.bfloat16), wide((plan.devices, 128), jnp.int32)],
        [SMEM, VMEM, VMEM, VMEM],
        [pltpu.VMEM((rows, width), jnp.bfloat16)],
        2 * slots * rows * width,
        3 * rows * width * 2,
    )(run_len, clusters, ranks, embeddings)
    groups = exchange(groups)
    arrived = exchange(outgoing)
    (own,) = call(
        sort_kernel, plan, [wide((rows, width), jnp.bfloat16)], [SMEM, VMEM],
        moved=3 * rows * width * 2,
    )(groups, arrived)

    def swap(block):
        pairs = [
            (i * plan.run + r, (i ^ 1) * plan.run + r)
            for i in range(plan.ingest)
            for r in range(plan.run)
        ]
        return lax.ppermute(block, AXES, pairs)

    mate = swap(own)
    behind = []
    for distance, chips in enumerate(plan.links()):
        if distance == 0:
            continue
        pairs = [
            (plan.device(i, 2 * chip + core), plan.device(i, 2 * (chip + distance) + core))
            for i in range(plan.ingest)
            for chip in chips
            for core in range(2)
        ]
        moved = lax.ppermute(own, AXES, pairs)
        behind += [moved, swap(moved)]
    place = jnp.stack([lax.axis_index("ingest"), lax.axis_index("run")]).astype(jnp.int32)
    (replies,) = call(
        best_kernel,
        plan,
        [wide((plan.devices, 128), jnp.float32)],
        [SMEM, SMEM, SMEM] + [VMEM] * (2 + len(behind)),
        [pltpu.VMEM((1, rows), jnp.float32), pltpu.VMEM((rows // plan.cap, 128), jnp.float32)],
        2 * rows * rows * width * 3,
        4 * rows * width * 2,
    )(run_len, place, groups, own, mate, *behind)
    returned = exchange(replies)
    (best,) = call(
        unpack_kernel, plan, [wide((1, rows), jnp.float32)], [SMEM, VMEM, VMEM, VMEM],
        moved=4 * rows * 4,
    )(run_len, clusters, ranks, returned)
    return best


def staged(plan, embeddings, clusters, ranks, run_len):
    rows, width = embeddings.shape
    wide = jax.ShapeDtypeStruct
    half = jnp.bfloat16
    lanes, layers = range(plan.lanes), range(plan.layers)

    def along_lanes(block, change):
        pairs = [
            (lane_device(plan, layer, lane), lane_device(plan, layer, lane ^ change))
            for layer in layers
            for lane in lanes
        ]
        return lax.ppermute(block, AXES, pairs)

    def along_layers(block, change):
        pairs = [
            (lane_device(plan, layer, lane), lane_device(plan, layer ^ change, lane))
            for layer in layers
            for lane in lanes
        ]
        return lax.ppermute(block, AXES, pairs)

    far_first = sorted(lanes[1:], key=lambda change: -(change & 1) - (change // plan.width // 2))

    spread = call(
        spread_kernel,
        plan,
        [wide((plan.part + 16, plan.chunks[0]), half) for _ in lanes]
        + [wide((rows, width - plan.chunks[0]), half)],
        [SMEM, VMEM, VMEM, VMEM],
        [pltpu.VMEM((rows, width), half)],
        2 * rows * rows * width,
        3 * rows * width * 2,
    )(run_len, clusters, ranks, embeddings)
    *spread, later = spread
    swapped = {change: along_lanes(spread[change], change) for change in far_first}
    spread = [spread[0]] + [swapped[change] for change in lanes[1:]]
    pair, mates, behind, fars = [], [], [], []
    table = targets = full = None
    arrivals = []
    for chunk, f in enumerate(plan.chunks):
        spec = dict(flops=2 * rows * rows * f, moved=3 * rows * f * 2, memory=12)
        rooms = [wide((plan.room + (0 if chunk else 16), f), half) for _ in layers]
        inputs = pltpu.VMEM((rows, f), half)
        if chunk == 0:
            *routed, table = call(
                route_kernel,
                plan,
                [*rooms, wide((1, rows), jnp.int32)],
                [VMEM] * plan.lanes,
                [
                    inputs,
                    pltpu.VMEM((plan.lanes, plan.part), jnp.int32),
                    pltpu.VMEM((plan.lanes, plan.part), jnp.int32),
                    pltpu.VMEM((1, rows), jnp.float32),
                ],
                **spec,
            )(*spread)
        else:
            if chunk == 1:
                later, _ = lax.optimization_barrier((later, table))
                groups = [[lane_device(plan, layer, lane) for lane in lanes] for layer in layers]
                later = lax.all_to_all(
                    later, AXES, 0, 0, tiled=True, axis_index_groups=groups
                )
            more = functools.partial(route_more_kernel, chunk=chunk)
            routed = call(more, plan, rooms, [VMEM] * 2, [inputs], **spec)(table, later)
        moved = {change: along_layers(routed[change], change) for change in reversed(layers[1:])}
        arrived = [routed[0]] + [moved[change] for change in layers[1:]]
        arrivals.append(arrived)
    for chunk, f in enumerate(plan.chunks):
        spec = dict(flops=2 * rows * rows * f, moved=3 * rows * f * 2, memory=12)
        inputs = pltpu.VMEM((rows, f), half)
        arrived = arrivals[chunk]
        if chunk:
            arrived, _ = lax.optimization_barrier((arrived, parts))
        shapes = [wide((4 * plan.part, f), half) for _ in range(plan.lanes // 2)]
        scratch = [pltpu.VMEM((plan.layers * plan.stride, f), half), inputs]
        if chunk == 0:
            *parts, targets, full = call(
                deliver_kernel,
                plan,
                [
                    *shapes,
                    wide((1, plan.layers * plan.stride), jnp.int32),
                    wide((8, 128), jnp.int32),
                ],
                [VMEM] * plan.layers,
                scratch,
                **spec,
            )(*arrived)
        else:
            parts = call(
                deliver_more_kernel, plan, shapes, [VMEM] * (1 + plan.layers), scratch, **spec
            )(targets, *arrived)
        parts = [
            along_lanes(part, lane_change(plan, chip, 0)) if chip else part
            for chip, part in enumerate(parts)
        ]
        spec = dict(moved=8 * rows * f * 2, memory=8)
        joined = call(
            join_kernel, plan, [wide((rows, f), half)] * 2, [VMEM] * len(parts), **spec
        )(*parts)
        for kept, block in zip((pair, behind), joined):
            kept.append(block)
        for kept, block in zip((mates, fars), joined):
            kept.append(along_lanes(block, plan.width))
    line = wide((1, rows), jnp.float32)
    kept = pltpu.VMEM((1, rows), jnp.float32)
    count = len(plan.chunks)
    spec = dict(flops=4 * rows * rows * width, moved=3 * rows * width * 2, memory=24)
    queries, best = call(
        pair_best_kernel,
        plan,
        [wide((rows, width), half), line],
        [VMEM] * (2 * count),
        [kept],
        **spec,
    )(*pair, *mates)
    spec = dict(flops=2 * rows * rows * width, moved=3 * rows * width * 2, memory=24)
    places = [SMEM] + [VMEM] * (2 + count)
    (best,) = call(
        functools.partial(more_best_kernel, last=False), plan, [line], places, [kept], **spec
    )(run_len, best, queries, *behind)
    (replies,) = call(
        functools.partial(more_best_kernel, last=True),
        plan,
        [wide((plan.devices, plan.lanes, 128), jnp.float32)],
        places,
        [kept, pltpu.VMEM((plan.lanes, 128), jnp.float32)],
        **spec,
    )(run_len, best, queries, *fars)
    returned = exchange(replies).reshape(plan.devices * plan.lanes, 128)
    (best,) = call(
        staged_unpack_kernel,
        plan,
        [wide((1, rows), jnp.float32)],
        [SMEM, VMEM, VMEM, VMEM],
        moved=4 * rows * 4,
        memory=8,
    )(run_len, clusters, ranks, returned)
    return best, full[0, 0]


def local(embeddings, cluster_id, rank, run_len):
    rows, width = embeddings.shape
    plan = Plan(lax.axis_size("ingest"), lax.axis_size("run"), run_len.shape[0], rows, width)
    given = (embeddings, cluster_id.reshape(1, rows), rank.reshape(1, rows), run_len)
    if not plan.staged():
        return direct(plan, *given).reshape(rows)
    best, full = staged(plan, *given)
    best = lax.cond(full > 0, lambda: direct(plan, *given), lambda: best)
    return best.reshape(rows)


def solution(mesh):
    return jax.shard_map(
        local,
        mesh=mesh,
        in_specs=(P(AXES, None), P(AXES), P(AXES), P()),
        out_specs=P(AXES),
        check_vma=False,
    )
```

```python
import functools

import jax
import jax.numpy as jnp
from jax import lax
from jax.experimental import pallas as pl
from jax.experimental.pallas import tpu as pltpu
from jax.sharding import PartitionSpec as P

EPSILON = 1e-06
AXES = ("ingest", "run")
TILE = 256
SHARES = (1, 1, 1)
MIB = 1024 * 1024


class Plan:
    def __init__(self, ingest, run, clusters, rows, features):
        self.ingest, self.run, self.clusters, self.rows = ingest, run, clusters, rows
        self.devices = ingest * run
        self.per_group = clusters // ingest
        self.cap = 2 * rows // self.devices
        self.reach = min(8, run // 2)
        self.width = run // ingest
        self.pairs = run // 2
        self.blocks = rows // self.cap
        self.layers, self.lanes = ingest, ingest * self.width
        self.slice = self.cap // self.lanes
        self.part = self.blocks * self.slice
        self.chunks = tuple(features * share // sum(SHARES) for share in SHARES)
        mean = rows // self.layers
        self.room = mean + mean // 8
        self.stride = -(-self.room // 128) * 128

    def staged(self):
        powers = all(n & (n - 1) == 0 for n in (self.layers, self.lanes, self.width))
        return (
            powers
            and self.cap % (8 * self.lanes) == 0
            and self.part == 128
            and self.room % 16 == 0
            and all(width % 128 == 0 for width in self.chunks)
            and self.links()[1:] == [[0]]
        )

    def device(self, group, slot):
        core, chip = slot % 2, slot // 2
        column, place = chip // self.width, chip % self.width
        odd = column % 2
        place = place + odd * (self.width - 1 - 2 * place)
        return (2 * column + core) * self.run + group * self.width + place

    def slot(self, device_ingest, device_run):
        core, column = device_ingest % 2, device_ingest // 2
        place = device_run % self.width
        place = place + (column % 2) * (self.width - 1 - 2 * place)
        return device_run // self.width, 2 * (column * self.width + place) + core

    def splits(self):
        def parts(total, count, top):
            if count == 0:
                if total == 0:
                    yield ()
                return
            for first in range(min(top, total), 0, -1):
                for rest in parts(total - first, count - 1, first):
                    yield (first, *rest)

        return list(parts(self.pairs, self.per_group, self.reach // 2))

    def links(self):
        found = [set() for _ in range(self.reach // 2)]
        for split in self.splits():
            begin = 0
            for length in split:
                for first in range(length):
                    for second in range(first + 1, length):
                        found[second - first].add(begin + first)
                begin += length
        return [sorted(chips) for chips in found]


def cluster_starts(plan, run_len_ref):
    starts = []
    for cluster in range(plan.clusters):
        base = cluster // plan.per_group * plan.per_group
        mine = run_len_ref[cluster]
        total = jnp.int32(0)
        for other in range(base, base + plan.per_group):
            if other == cluster:
                continue
            theirs = run_len_ref[other]
            ahead = (theirs >= mine) if other < cluster else (theirs > mine)
            total = total + jnp.where(ahead, theirs, 0)
        starts.append(total)
    return starts


def row_slot(plan, run_len_ref, cluster, rank):
    starts = cluster_starts(plan, run_len_ref)
    begin = jnp.zeros_like(cluster)
    group = jnp.zeros_like(cluster)
    for number, start in enumerate(starts):
        here = cluster == number
        begin = jnp.where(here, start, begin)
        group = jnp.where(here, number // plan.per_group, group)
    return group, begin + rank // plan.rows, rank % plan.rows


def row_owner(plan, run_len_ref, cluster, rank):
    group, slot, within = row_slot(plan, run_len_ref, cluster, rank)
    return plan.device(group, slot), within


def pack_kernel(plan, run_len_ref, cluster_ref, rank_ref, rows_ref, out_ref, group_ref, unit_ref):
    step = 128

    @pl.loop(0, plan.rows // step)
    def _(number):
        here = pl.ds(pl.multiple_of(number * step, step), step)
        widened = rows_ref[here, :].astype(jnp.float32)
        total = jnp.sum(widened * widened, axis=1, keepdims=True) + EPSILON
        unit_ref[here, :] = (widened * lax.rsqrt(total)).astype(jnp.bfloat16)

    owner, within = row_owner(plan, run_len_ref, cluster_ref[...], rank_ref[...])
    number = lax.broadcasted_iota(jnp.int32, (plan.devices, plan.rows), 0)
    group = jnp.max(
        jnp.where(number == owner, within // plan.cap + 1, 0), axis=1, keepdims=True
    )
    group_ref[...] = jnp.broadcast_to(group, group_ref.shape)
    position = owner * plan.cap + within % plan.cap

    @pl.loop(0, plan.devices * plan.cap // TILE)
    def _(tile):
        row = lax.broadcasted_iota(jnp.int32, (TILE, plan.rows), 0) + tile * TILE
        chosen = jnp.where(row == position, 1.0, 0.0).astype(jnp.bfloat16)
        moved = jnp.dot(chosen, unit_ref[...], preferred_element_type=jnp.float32)
        here = pl.ds(pl.multiple_of(tile * TILE, TILE), TILE)
        out_ref[here, :] = moved.astype(jnp.bfloat16)


def sort_kernel(plan, group_ref, arrived_ref, out_ref):
    for source in range(plan.devices):
        group = group_ref[source, 0]

        @pl.when(group > 0)
        def _():
            here = pl.ds(pl.multiple_of((group - 1) * plan.cap, plan.cap), plan.cap)
            out_ref[here, :] = arrived_ref[source * plan.cap : (source + 1) * plan.cap, :]


def block_best(keys_ref, queries_ref, best_ref):
    rows = keys_ref.shape[0]

    @pl.loop(0, rows // TILE)
    def _(tile):
        keys = keys_ref[pl.ds(pl.multiple_of(tile * TILE, TILE), TILE), :]
        scores = lax.dot_general(
            keys, queries_ref[...], (((1,), (1,)), ((), ())), preferred_element_type=jnp.float32
        )
        best_ref[...] = jnp.maximum(best_ref[...], jnp.max(scores, axis=0, keepdims=True))


def triangle_best(rows_ref, best_ref):
    rows = rows_ref.shape[0]
    for first in range(0, rows, TILE):
        scores = lax.dot_general(
            rows_ref[first : first + TILE, :],
            rows_ref[first:, :],
            (((1,), (1,)), ((), ())),
            preferred_element_type=jnp.float32,
        )
        key = lax.broadcasted_iota(jnp.int32, (TILE, TILE), 0)
        query = lax.broadcasted_iota(jnp.int32, (TILE, TILE), 1)
        corner = jnp.max(
            jnp.where(key < query, scores[:, :TILE], -2.0), axis=0, keepdims=True
        )
        here = slice(first, first + TILE)
        best_ref[:, here] = jnp.maximum(best_ref[:, here], corner)
        if first + TILE < rows:
            rest = jnp.max(scores[:, TILE:], axis=0, keepdims=True)
            there = slice(first + TILE, rows)
            best_ref[:, there] = jnp.maximum(best_ref[:, there], rest)


def best_kernel(plan, run_len_ref, place_ref, group_ref, own_ref, mate_ref, *rest):
    behind, (out_ref, best_ref, blocks_ref) = rest[:-3], rest[-3:]
    group, slot = plan.slot(place_ref[0], place_ref[1])
    begin = jnp.int32(0)
    for number, start in enumerate(cluster_starts(plan, run_len_ref)):
        here = (number // plan.per_group == group) & (start <= slot)
        begin = jnp.where(here, jnp.maximum(begin, start), begin)
    best_ref[...] = jnp.full(best_ref.shape, -1.0, jnp.float32)
    triangle_best(own_ref, best_ref)

    @pl.when(slot % 2 == 1)
    def _():
        block_best(mate_ref, own_ref, best_ref)

    for distance in range(1, plan.reach // 2):
        first, second = behind[2 * distance - 2], behind[2 * distance - 1]

        @pl.when(slot - slot % 2 - 2 * distance >= begin)
        def _():
            block_best(first, own_ref, best_ref)
            block_best(second, own_ref, best_ref)

    for number in range(plan.rows // plan.cap):
        part = best_ref[:, number * plan.cap : (number + 1) * plan.cap]
        blocks_ref[number : number + 1, : plan.cap] = part
    for source in range(plan.devices):
        chosen = jnp.maximum(group_ref[source, 0] - 1, 0)
        out_ref[source : source + 1, :] = blocks_ref[pl.ds(chosen, 1), :]


def unpack_kernel(plan, run_len_ref, cluster_ref, rank_ref, reply_ref, out_ref):
    owner, within = row_owner(plan, run_len_ref, cluster_ref[...], rank_ref[...])
    number = lax.broadcasted_iota(jnp.int32, (plan.devices, plan.rows), 0)
    chosen = jnp.where(number == owner, 1.0, 0.0)
    columns = lax.dot_general(
        reply_ref[:, : plan.cap],
        chosen,
        (((0,), (0,)), ((), ())),
        precision=lax.Precision.HIGHEST,
        preferred_element_type=jnp.float32,
    )
    lane = lax.broadcasted_iota(jnp.int32, (plan.cap, plan.rows), 0)
    out_ref[...] = jnp.sum(
        jnp.where(lane == within % plan.cap, columns, 0.0), axis=0, keepdims=True
    )


def lane_of(plan, slot):
    device = plan.device(0, slot)
    return device // plan.run * plan.width + device % plan.run


def chip_change(plan, change):
    width = plan.width
    return change % width + change // (2 * width) * width, change // width % 2


def lane_change(plan, chip, core):
    width = plan.width
    return chip % width + core * width + chip // width * 2 * width


def lane_device(plan, layer, lane):
    return lane // plan.width * plan.run + layer * plan.width + lane % plan.width


def my_lane(plan):
    run = lax.axis_index("run")
    return lax.axis_index("ingest") * plan.width + run % plan.width, run // plan.width


def spread_pair(plan, part, target, rows):
    row = lax.broadcasted_iota(jnp.int32, (2 * plan.part, plan.rows), 0) + part * plan.part
    chosen = jnp.where(row == target, 1.0, 0.0).astype(jnp.bfloat16)
    return jnp.dot(chosen, rows, preferred_element_type=jnp.float32).astype(jnp.bfloat16)


def spread_more_kernel(plan, unit_ref, target_ref, out_ref):
    lane, _ = my_lane(plan)
    for part in range(0, plan.lanes, 2):
        moved = spread_pair(plan, part, target_ref[...], unit_ref[:, plan.chunks[0] :])
        for number in range(2):
            whole = pl.multiple_of((part + number ^ lane) * plan.part, plan.part)
            here = moved[number * plan.part : (number + 1) * plan.part, :]
            out_ref[pl.ds(whole, plan.part), :] = here


def spread_kernel(plan, run_len_ref, cluster_ref, rank_ref, rows_ref, *rest):
    outs, (unit_ref, target_ref) = rest[:-2], rest[-2:]
    step = 128

    @pl.loop(0, plan.rows // step)
    def _(number):
        here = pl.ds(pl.multiple_of(number * step, step), step)
        widened = rows_ref[here, :].astype(jnp.float32)
        total = jnp.sum(widened * widened, axis=1, keepdims=True) + EPSILON
        unit_ref[here, :] = (widened * lax.rsqrt(total)).astype(jnp.bfloat16)

    lane, _ = my_lane(plan)
    group, slot, within = row_slot(plan, run_len_ref, cluster_ref[...], rank_ref[...])
    owner = group * plan.run + slot
    number = lax.broadcasted_iota(jnp.int32, (plan.devices, plan.rows), 0)
    member = number == owner
    block = jnp.max(jnp.where(member, within // plan.cap + 1, 0), axis=1, keepdims=True)
    present = jnp.where(block > 0, 1.0, 0.0)
    before = lax.broadcasted_iota(jnp.int32, (plan.devices, plan.devices), 0) > (
        lax.broadcasted_iota(jnp.int32, (plan.devices, plan.devices), 1)
    )
    order = jnp.dot(
        jnp.where(before, 1.0, 0.0),
        jnp.broadcast_to(present, (plan.devices, 128)),
        preferred_element_type=jnp.float32,
    )
    mine = jnp.sum(jnp.where(member, order[:, :1], 0.0), axis=0, keepdims=True)
    residue = within % plan.cap
    target = (
        (residue // plan.slice ^ lane) * plan.part
        + mine.astype(jnp.int32) * plan.slice
        + residue % plan.slice
    )
    target_ref[...] = target
    for part in range(0, plan.lanes, 2):
        moved = spread_pair(plan, part, target, unit_ref[:, : plan.chunks[0]])
        outs[part][: plan.part, :] = moved[: plan.part, :]
        outs[part + 1][: plan.part, :] = moved[plan.part :, :]

    place = lax.broadcasted_iota(jnp.int32, (plan.devices, plan.part), 1) // plan.slice
    here = (place.astype(jnp.float32) == order[:, :1]) & (block > 0)
    who = lax.broadcasted_iota(jnp.int32, (plan.devices, plan.part), 0)
    owners = jnp.sum(jnp.where(here, who, 0), axis=0, keepdims=True)
    blocks = jnp.sum(jnp.where(here, block - 1, 0), axis=0, keepdims=True)
    line = lax.broadcasted_iota(jnp.int32, (16, plan.part), 0)
    table = jnp.where(line == 0, owners, jnp.where(line == 1, blocks, 0))
    for out in outs:
        out[plan.part :, : plan.part] = table.astype(jnp.float32).astype(jnp.bfloat16)


def permute_into(target, first, inputs_ref, outs, room, stride):
    columns = inputs_ref.shape[0]
    for number, out in enumerate(outs):
        row = lax.broadcasted_iota(jnp.int32, (room, columns), 0) + first + number * stride
        chosen = jnp.where(row == target, 1.0, 0.0).astype(jnp.bfloat16)
        moved = jnp.dot(chosen, inputs_ref[...], preferred_element_type=jnp.float32)
        out[:room, :] = moved.astype(jnp.bfloat16)


def route_kernel(plan, *refs):
    ins, rest = refs[: plan.lanes], refs[plan.lanes :]
    outs, (target_ref, inputs_ref, owner_ref, block_ref, value_ref) = rest[:-5], rest[-5:]
    _, layer = my_lane(plan)
    for number, part in enumerate(ins):
        inputs_ref[number * plan.part : (number + 1) * plan.part, :] = part[: plan.part, :]
        table = part[plan.part :, : plan.part].astype(jnp.float32)
        owner_ref[number : number + 1, :] = table[0:1, :].astype(jnp.int32)
        block_ref[number : number + 1, :] = table[1:2, :].astype(jnp.int32)
    owner = owner_ref[...]
    shape = (plan.part, plan.part)
    earlier = lax.broadcasted_iota(jnp.int32, shape, 0) < lax.broadcasted_iota(jnp.int32, shape, 1)
    earlier = jnp.where(earlier, 1.0, 0.0)
    ones = jnp.ones(shape, jnp.float32)
    shape = (plan.lanes, plan.lanes)
    above = lax.broadcasted_iota(jnp.int32, shape, 0) > lax.broadcasted_iota(jnp.int32, shape, 1)
    above = jnp.where(above, 1.0, 0.0)
    target = jnp.zeros(owner.shape, jnp.int32)
    most = jnp.float32(0.0)
    for other in range(plan.layers):
        chosen = owner // plan.run == other
        marks = jnp.where(chosen, 1.0, 0.0)
        lines = jnp.dot(marks, ones, preferred_element_type=jnp.float32)
        count = jnp.dot(marks, earlier, preferred_element_type=jnp.float32) + jnp.dot(
            above, lines, preferred_element_type=jnp.float32
        )
        count = count.astype(jnp.int32)
        there = jnp.where(count < plan.room, (layer ^ other) * plan.stride + count, -1)
        target = jnp.where(chosen, there, target)
        most = jnp.maximum(most, jnp.sum(marks))
    full = jnp.where(most > plan.room, 1.0, 0.0)
    value = owner % plan.run * plan.blocks + block_ref[...] + 1
    for number in range(plan.lanes):
        here = slice(number * plan.part, (number + 1) * plan.part)
        target_ref[:, here] = target[number : number + 1, :]
        value_ref[:, here] = value[number : number + 1, :].astype(jnp.float32)
    target = target_ref[...]
    values = jnp.broadcast_to(value_ref[...], (8, plan.rows)).astype(jnp.bfloat16)
    for number, out in enumerate(outs):
        row = lax.broadcasted_iota(jnp.int32, (plan.stride, plan.rows), 0) + number * plan.stride
        chosen = jnp.where(row == target, 1.0, 0.0).astype(jnp.bfloat16)
        moved = jnp.dot(
            chosen[: plan.room, :], inputs_ref[...], preferred_element_type=jnp.float32
        )
        out[: plan.room, :] = moved.astype(jnp.bfloat16)
        listed = lax.dot_general(
            values, chosen, (((1,), (1,)), ((), ())), preferred_element_type=jnp.float32
        )
        line = lax.broadcasted_iota(jnp.int32, (16, 128), 0)
        table = jnp.where(line == 15, full, 0.0)
        for piece in range(plan.stride // 128):
            here = listed[0:1, piece * 128 : (piece + 1) * 128]
            table = jnp.where(line == piece, here, table)
        out[plan.room :, :128] = table.astype(jnp.bfloat16)


def route_more_kernel(plan, target_ref, rows_ref, *refs, chunk):
    outs, inputs_ref = refs[:-1], refs[-1]
    lane, _ = my_lane(plan)
    first = sum(plan.chunks[1:chunk])
    for number in range(plan.lanes):
        whole = pl.multiple_of((number ^ lane) * plan.part, plan.part)
        inputs_ref[number * plan.part : (number + 1) * plan.part, :] = rows_ref[
            pl.ds(whole, plan.part), first : first + plan.chunks[chunk]
        ]
    permute_into(target_ref[...], 0, inputs_ref, outs, plan.room, plan.stride)


def gather_rows(plan, ins, inputs_ref):
    for number, part in enumerate(ins):
        first = number * plan.stride
        inputs_ref[first : first + plan.room, :] = part[: plan.room, :]
        if plan.stride > plan.room:
            inputs_ref[first + plan.room : first + plan.stride, :] = jnp.zeros(
                (plan.stride - plan.room, inputs_ref.shape[1]), jnp.bfloat16
            )


def sort_parts(plan, target, inputs_ref, outs, sorted_ref):
    tile = 2 * plan.part
    for chip, out in enumerate(outs):
        row = lax.broadcasted_iota(jnp.int32, (tile, inputs_ref.shape[0]), 0) + chip * tile
        chosen = jnp.where(row == target, 1.0, 0.0).astype(jnp.bfloat16)
        moved = jnp.dot(chosen, inputs_ref[...], preferred_element_type=jnp.float32)
        moved = moved.astype(jnp.bfloat16)
        sorted_ref[chip * tile : (chip + 1) * tile, :] = moved
        out[:tile, :] = moved
    lane, _ = my_lane(plan)
    chip, _ = chip_change(plan, lane_of(plan, 0) ^ lane)
    ahead = sorted_ref[pl.ds(pl.multiple_of(chip * tile, tile), tile), :]
    for out in outs:
        out[tile:, :] = ahead


def deliver_kernel(plan, *refs):
    ins, rest = refs[: plan.layers], refs[plan.layers :]
    outs, (target_ref, full_ref, inputs_ref, sorted_ref) = rest[:-4], rest[-4:]
    lane, _ = my_lane(plan)
    gather_rows(plan, ins, inputs_ref)
    full = jnp.zeros((8, 128), jnp.float32)
    for number, part in enumerate(ins):
        table = part[plan.room :, :128].astype(jnp.float32)
        lines = [table[piece : piece + 1, :] for piece in range(plan.stride // 128)]
        value = jnp.concatenate(lines, axis=1).astype(jnp.int32) - 1
        full = jnp.maximum(full, jnp.broadcast_to(table[15:, :], (8, 128)))
        slot = value // plan.blocks
        within = lax.broadcasted_iota(jnp.int32, value.shape, 1) % plan.slice
        chip, _ = chip_change(plan, lane_of(plan, slot) ^ lane)
        target = (2 * chip + slot % 2) * plan.part + value % plan.blocks * plan.slice + within
        target_ref[:, number * plan.stride : (number + 1) * plan.stride] = jnp.where(
            value >= 0, target, -1
        )
    full_ref[...] = full.astype(jnp.int32)
    sort_parts(plan, target_ref[...], inputs_ref, outs, sorted_ref)


def deliver_more_kernel(plan, target_ref, *refs):
    ins, rest = refs[: plan.layers], refs[plan.layers :]
    outs, (inputs_ref, sorted_ref) = rest[:-2], rest[-2:]
    gather_rows(plan, ins, inputs_ref)
    sort_parts(plan, target_ref[...], inputs_ref, outs, sorted_ref)


def join_kernel(plan, *refs):
    ins, outs = refs[:-2], refs[-2:]
    tile = 2 * plan.part
    for number, part in enumerate(ins):
        for half, out in enumerate(outs):
            out[number * tile : (number + 1) * tile, :] = part[half * tile : (half + 1) * tile, :]


def add_best(keys, queries_ref, best_ref, allowed=None):
    scores = lax.dot_general(
        keys, queries_ref[...], (((1,), (1,)), ((), ())), preferred_element_type=jnp.float32
    )
    if allowed is not None:
        scores = jnp.where(allowed, scores, -2.0)
    best_ref[...] = jnp.maximum(best_ref[...], jnp.max(scores, axis=0, keepdims=True))


def staged_best_kernel(plan, run_len_ref, *refs):
    count = len(plan.chunks)
    own, mate, behind, far = (refs[n * count : (n + 1) * count] for n in range(4))
    out_ref, best_ref, queries_ref, lines_ref = refs[4 * count :]
    lane, _ = my_lane(plan)
    group, slot = plan.slot(lax.axis_index("ingest"), lax.axis_index("run"))
    core = slot % 2
    begin = jnp.int32(0)
    for number, start in enumerate(cluster_starts(plan, run_len_ref)):
        here = (number // plan.per_group == group) & (start <= slot)
        begin = jnp.where(here, jnp.maximum(begin, start), begin)
    chips = plan.lanes // 2
    for side, parts in enumerate((own, mate)):
        for chip in range(chips):
            there = pl.ds(pl.multiple_of((2 * chip + core) * plan.part, plan.part), plan.part)
            here = slice((side * chips + chip) * plan.part, (side * chips + chip + 1) * plan.part)
            first = 0
            for part in parts:
                queries_ref[here, first : first + part.shape[1]] = part[there, :]
                first += part.shape[1]

    def slots(row):
        line = row // plan.part
        source = lane_change(plan, line % chips, line // chips) ^ lane
        block = row // plan.slice % plan.blocks
        return block * plan.cap + source * plan.slice + row % plan.slice

    best_ref[...] = jnp.full(best_ref.shape, -1.0, jnp.float32)
    query = slots(lax.broadcasted_iota(jnp.int32, (1, plan.rows), 1))
    for first in range(0, plan.rows, TILE):
        key = slots(lax.broadcasted_iota(jnp.int32, (TILE, 1), 0) + first)
        add_best(queries_ref[first : first + TILE, :], queries_ref, best_ref, key < query)

    @pl.when(core == 1)
    def _():
        for parts in (own, mate):
            for pair in range(0, chips, 2):
                keys = []
                for number in (pair, pair + 1):
                    here = slice(2 * number * plan.part, (2 * number + 1) * plan.part)
                    keys.append(jnp.concatenate([part[here, :] for part in parts], axis=1))
                add_best(jnp.concatenate(keys, axis=0), queries_ref, best_ref)

    @pl.when(slot - core - 2 >= begin)
    def _():
        for parts in (behind, far):
            for first in range(0, plan.rows, TILE):
                keys = [part[first : first + TILE, :] for part in parts]
                add_best(jnp.concatenate(keys, axis=1), queries_ref, best_ref)

    for number in range(plan.lanes):
        lines_ref[number : number + 1, :] = best_ref[
            :, number * plan.part : (number + 1) * plan.part
        ]
    for device in range(plan.devices):
        out_ref[device] = lines_ref[...]


def staged_unpack_kernel(plan, run_len_ref, cluster_ref, rank_ref, reply_ref, out_ref):
    group, slot, within = row_slot(plan, run_len_ref, cluster_ref[...], rank_ref[...])
    residue = within % plan.cap
    chip, core = chip_change(plan, residue // plan.slice ^ lane_of(plan, slot))
    line = plan.device(group, slot) * plan.lanes + core * (plan.lanes // 2) + chip
    column = within // plan.cap * plan.slice + residue % plan.slice
    number = lax.broadcasted_iota(jnp.int32, (plan.devices * plan.lanes, plan.rows), 0)
    columns = lax.dot_general(
        reply_ref[...],
        jnp.where(number == line, 1.0, 0.0),
        (((0,), (0,)), ((), ())),
        precision=lax.Precision.HIGHEST,
        preferred_element_type=jnp.float32,
    )
    place = lax.broadcasted_iota(jnp.int32, (plan.part, plan.rows), 0)
    out_ref[...] = jnp.sum(jnp.where(place == column, columns, 0.0), axis=0, keepdims=True)


SMEM = pl.BlockSpec(memory_space=pltpu.SMEM)
VMEM = pl.BlockSpec(memory_space=pltpu.VMEM)


def call(kernel, plan, shapes, specs, scratch=(), flops=0, moved=0, memory=32):
    return pl.pallas_call(
        functools.partial(kernel, plan),
        out_shape=shapes,
        in_specs=specs,
        out_specs=[VMEM] * len(shapes),
        scratch_shapes=scratch,
        compiler_params=pltpu.CompilerParams(vmem_limit_bytes=memory * MIB),
        cost_estimate=pl.CostEstimate(flops=flops, bytes_accessed=moved, transcendentals=0),
    )


def exchange(block):
    return lax.all_to_all(block, AXES, split_axis=0, concat_axis=0, tiled=True)


def direct(plan, embeddings, clusters, ranks, run_len):
    rows, width = embeddings.shape
    slots = plan.devices * plan.cap
    wide = jax.ShapeDtypeStruct
    outgoing, groups = call(
        pack_kernel,
        plan,
        [wide((slots, width), jnp.bfloat16), wide((plan.devices, 128), jnp.int32)],
        [SMEM, VMEM, VMEM, VMEM],
        [pltpu.VMEM((rows, width), jnp.bfloat16)],
        2 * slots * rows * width,
        3 * rows * width * 2,
    )(run_len, clusters, ranks, embeddings)
    groups = exchange(groups)
    arrived = exchange(outgoing)
    (own,) = call(
        sort_kernel, plan, [wide((rows, width), jnp.bfloat16)], [SMEM, VMEM],
        moved=3 * rows * width * 2,
    )(groups, arrived)

    def swap(block):
        pairs = [
            (i * plan.run + r, (i ^ 1) * plan.run + r)
            for i in range(plan.ingest)
            for r in range(plan.run)
        ]
        return lax.ppermute(block, AXES, pairs)

    mate = swap(own)
    behind = []
    for distance, chips in enumerate(plan.links()):
        if distance == 0:
            continue
        pairs = [
            (plan.device(i, 2 * chip + core), plan.device(i, 2 * (chip + distance) + core))
            for i in range(plan.ingest)
            for chip in chips
            for core in range(2)
        ]
        moved = lax.ppermute(own, AXES, pairs)
        behind += [moved, swap(moved)]
    place = jnp.stack([lax.axis_index("ingest"), lax.axis_index("run")]).astype(jnp.int32)
    (replies,) = call(
        best_kernel,
        plan,
        [wide((plan.devices, 128), jnp.float32)],
        [SMEM, SMEM, SMEM] + [VMEM] * (2 + len(behind)),
        [pltpu.VMEM((1, rows), jnp.float32), pltpu.VMEM((rows // plan.cap, 128), jnp.float32)],
        2 * rows * rows * width * 3,
        4 * rows * width * 2,
    )(run_len, place, groups, own, mate, *behind)
    returned = exchange(replies)
    (best,) = call(
        unpack_kernel, plan, [wide((1, rows), jnp.float32)], [SMEM, VMEM, VMEM, VMEM],
        moved=4 * rows * 4,
    )(run_len, clusters, ranks, returned)
    return best


def staged(plan, embeddings, clusters, ranks, run_len):
    rows, width = embeddings.shape
    wide = jax.ShapeDtypeStruct
    half = jnp.bfloat16
    lanes, layers = range(plan.lanes), range(plan.layers)

    def along_lanes(block, change):
        pairs = [
            (lane_device(plan, layer, lane), lane_device(plan, layer, lane ^ change))
            for layer in layers
            for lane in lanes
        ]
        return lax.ppermute(block, AXES, pairs)

    def along_layers(block, change):
        pairs = [
            (lane_device(plan, layer, lane), lane_device(plan, layer ^ change, lane))
            for layer in layers
            for lane in lanes
        ]
        return lax.ppermute(block, AXES, pairs)

    far_first = sorted(lanes[1:], key=lambda change: -(change & 1) - (change // plan.width // 2))

    *spread, unit, target = call(
        spread_kernel,
        plan,
        [wide((plan.part + 16, plan.chunks[0]), half) for _ in lanes]
        + [wide((rows, width), half), wide((1, rows), jnp.int32)],
        [SMEM, VMEM, VMEM, VMEM],
        (),
        2 * rows * rows * plan.chunks[0],
        3 * rows * width * 2,
        memory=24,
    )(run_len, clusters, ranks, embeddings)
    (later,) = call(
        spread_more_kernel,
        plan,
        [wide((rows, width - plan.chunks[0]), half)],
        [VMEM, VMEM],
        (),
        2 * rows * rows * (width - plan.chunks[0]),
        3 * rows * width * 2,
        memory=16,
    )(unit, target)
    swapped = {change: along_lanes(spread[change], change) for change in far_first}
    spread = [spread[0]] + [swapped[change] for change in lanes[1:]]
    pair, mates, behind, fars = [], [], [], []
    table = targets = full = None
    arrivals, routes = [], []
    for chunk, f in enumerate(plan.chunks):
        spec = dict(flops=2 * rows * rows * f, moved=3 * rows * f * 2, memory=12)
        rooms = [wide((plan.room + (0 if chunk else 16), f), half) for _ in layers]
        inputs = pltpu.VMEM((rows, f), half)
        if chunk == 0:
            *routed, table = call(
                route_kernel,
                plan,
                [*rooms, wide((1, rows), jnp.int32)],
                [VMEM] * plan.lanes,
                [
                    inputs,
                    pltpu.VMEM((plan.lanes, plan.part), jnp.int32),
                    pltpu.VMEM((plan.lanes, plan.part), jnp.int32),
                    pltpu.VMEM((1, rows), jnp.float32),
                ],
                **spec,
            )(*spread)
        else:
            if chunk == 1:
                later, _ = lax.optimization_barrier((later, table))
                groups = [[lane_device(plan, layer, lane) for lane in lanes] for layer in layers]
                later = lax.all_to_all(
                    later, AXES, 0, 0, tiled=True, axis_index_groups=groups
                )
            more = functools.partial(route_more_kernel, chunk=chunk)
            routed = call(more, plan, rooms, [VMEM] * 2, [inputs], **spec)(table, later)
        moved = {change: along_layers(routed[change], change) for change in reversed(layers[1:])}
        arrived = [routed[0]] + [moved[change] for change in layers[1:]]
        arrivals.append(arrived)
        routes.append(routed)
    for chunk, f in enumerate(plan.chunks):
        spec = dict(flops=2 * rows * rows * f, moved=3 * rows * f * 2, memory=12)
        inputs = pltpu.VMEM((rows, f), half)
        arrived = arrivals[chunk]
        ahead = chunk + 1
        if chunk:
            arrived, _ = lax.optimization_barrier((arrived, parts))
        if ahead < len(plan.chunks):
            arrived, _ = lax.optimization_barrier((arrived, arrivals[ahead][1] if ahead == 2 else routes[ahead]))
        shapes = [wide((4 * plan.part, f), half) for _ in range(plan.lanes // 2)]
        scratch = [pltpu.VMEM((plan.layers * plan.stride, f), half), inputs]
        if chunk == 0:
            *parts, targets, full = call(
                deliver_kernel,
                plan,
                [
                    *shapes,
                    wide((1, plan.layers * plan.stride), jnp.int32),
                    wide((8, 128), jnp.int32),
                ],
                [VMEM] * plan.layers,
                scratch,
                **spec,
            )(*arrived)
        else:
            parts = call(
                deliver_more_kernel, plan, shapes, [VMEM] * (1 + plan.layers), scratch, **spec
            )(targets, *arrived)
        parts = [
            along_lanes(part, lane_change(plan, chip, 0)) if chip else part
            for chip, part in enumerate(parts)
        ]
        spec = dict(moved=8 * rows * f * 2, memory=8)
        joined = call(
            join_kernel, plan, [wide((rows, f), half)] * 2, [VMEM] * len(parts), **spec
        )(*parts)
        for kept, block in zip((pair, behind), joined):
            kept.append(block)
        for kept, block in zip((mates, fars), joined):
            kept.append(along_lanes(block, plan.width))
    count = len(plan.chunks)
    (replies,) = call(
        staged_best_kernel,
        plan,
        [wide((plan.devices, plan.lanes, 128), jnp.float32)],
        [SMEM] + [VMEM] * (4 * count),
        [
            pltpu.VMEM((1, rows), jnp.float32),
            pltpu.VMEM((rows, width), half),
            pltpu.VMEM((plan.lanes, 128), jnp.float32),
        ],
        2 * rows * rows * width * 3,
        4 * rows * width * 2,
        memory=24,
    )(run_len, *pair, *mates, *behind, *fars)
    returned = exchange(replies).reshape(plan.devices * plan.lanes, 128)
    (best,) = call(
        staged_unpack_kernel,
        plan,
        [wide((1, rows), jnp.float32)],
        [SMEM, VMEM, VMEM, VMEM],
        moved=4 * rows * 4,
        memory=8,
    )(run_len, clusters, ranks, returned)
    return best, full[0, 0]


def local(embeddings, cluster_id, rank, run_len):
    rows, width = embeddings.shape
    plan = Plan(lax.axis_size("ingest"), lax.axis_size("run"), run_len.shape[0], rows, width)
    given = (embeddings, cluster_id.reshape(1, rows), rank.reshape(1, rows), run_len)
    if not plan.staged():
        return direct(plan, *given).reshape(rows)
    best, full = staged(plan, *given)
    best = lax.cond(full > 0, lambda: direct(plan, *given), lambda: best)
    return best.reshape(rows)


def solution(mesh):
    return jax.shard_map(
        local,
        mesh=mesh,
        in_specs=(P(AXES, None), P(AXES), P(AXES), P()),
        out_specs=P(AXES),
        check_vma=False,
    )
```

```python
import functools

import jax
import jax.numpy as jnp
from jax import lax
from jax.experimental import pallas as pl
from jax.experimental.pallas import tpu as pltpu
from jax.sharding import PartitionSpec as P

EPSILON = 1e-06
AXES = ("ingest", "run")
TILE = 512
SHARES = (1, 1, 1)
MIB = 1024 * 1024


class Plan:
    def __init__(self, ingest, run, clusters, rows, features):
        self.ingest, self.run, self.clusters, self.rows = ingest, run, clusters, rows
        self.devices = ingest * run
        self.per_group = clusters // ingest
        self.cap = 2 * rows // self.devices
        self.reach = min(8, run // 2)
        self.width = run // ingest
        self.pairs = run // 2
        self.blocks = rows // self.cap
        self.layers, self.lanes = ingest, ingest * self.width
        self.slice = self.cap // self.lanes
        self.part = self.blocks * self.slice
        self.chunks = tuple(features * share // sum(SHARES) for share in SHARES)
        mean = rows // self.layers
        self.room = mean + mean // 8
        self.stride = -(-self.room // 128) * 128

    def staged(self):
        powers = all(n & (n - 1) == 0 for n in (self.layers, self.lanes, self.width))
        return (
            powers
            and self.cap % (8 * self.lanes) == 0
            and self.part == 128
            and self.room % 16 == 0
            and all(width % 128 == 0 for width in self.chunks)
            and self.links()[1:] == [[0]]
        )

    def device(self, group, slot):
        core, chip = slot % 2, slot // 2
        column, place = chip // self.width, chip % self.width
        odd = column % 2
        place = place + odd * (self.width - 1 - 2 * place)
        return (2 * column + core) * self.run + group * self.width + place

    def slot(self, device_ingest, device_run):
        core, column = device_ingest % 2, device_ingest // 2
        place = device_run % self.width
        place = place + (column % 2) * (self.width - 1 - 2 * place)
        return device_run // self.width, 2 * (column * self.width + place) + core

    def splits(self):
        def parts(total, count, top):
            if count == 0:
                if total == 0:
                    yield ()
                return
            for first in range(min(top, total), 0, -1):
                for rest in parts(total - first, count - 1, first):
                    yield (first, *rest)

        return list(parts(self.pairs, self.per_group, self.reach // 2))

    def links(self):
        found = [set() for _ in range(self.reach // 2)]
        for split in self.splits():
            begin = 0
            for length in split:
                for first in range(length):
                    for second in range(first + 1, length):
                        found[second - first].add(begin + first)
                begin += length
        return [sorted(chips) for chips in found]


def cluster_starts(plan, run_len_ref):
    starts = []
    for cluster in range(plan.clusters):
        base = cluster // plan.per_group * plan.per_group
        mine = run_len_ref[cluster]
        total = jnp.int32(0)
        for other in range(base, base + plan.per_group):
            if other == cluster:
                continue
            theirs = run_len_ref[other]
            ahead = (theirs >= mine) if other < cluster else (theirs > mine)
            total = total + jnp.where(ahead, theirs, 0)
        starts.append(total)
    return starts


def row_slot(plan, run_len_ref, cluster, rank):
    starts = cluster_starts(plan, run_len_ref)
    begin = jnp.zeros_like(cluster)
    group = jnp.zeros_like(cluster)
    for number, start in enumerate(starts):
        here = cluster == number
        begin = jnp.where(here, start, begin)
        group = jnp.where(here, number // plan.per_group, group)
    return group, begin + rank // plan.rows, rank % plan.rows


def row_owner(plan, run_len_ref, cluster, rank):
    group, slot, within = row_slot(plan, run_len_ref, cluster, rank)
    return plan.device(group, slot), within


def pack_kernel(plan, run_len_ref, cluster_ref, rank_ref, rows_ref, out_ref, group_ref, unit_ref):
    step = 128

    @pl.loop(0, plan.rows // step)
    def _(number):
        here = pl.ds(pl.multiple_of(number * step, step), step)
        widened = rows_ref[here, :].astype(jnp.float32)
        total = jnp.sum(widened * widened, axis=1, keepdims=True) + EPSILON
        unit_ref[here, :] = (widened * lax.rsqrt(total)).astype(jnp.bfloat16)

    owner, within = row_owner(plan, run_len_ref, cluster_ref[...], rank_ref[...])
    number = lax.broadcasted_iota(jnp.int32, (plan.devices, plan.rows), 0)
    group = jnp.max(
        jnp.where(number == owner, within // plan.cap + 1, 0), axis=1, keepdims=True
    )
    group_ref[...] = jnp.broadcast_to(group, group_ref.shape)
    position = owner * plan.cap + within % plan.cap

    @pl.loop(0, plan.devices * plan.cap // TILE)
    def _(tile):
        row = lax.broadcasted_iota(jnp.int32, (TILE, plan.rows), 0) + tile * TILE
        chosen = jnp.where(row == position, 1.0, 0.0).astype(jnp.bfloat16)
        moved = jnp.dot(chosen, unit_ref[...], preferred_element_type=jnp.float32)
        here = pl.ds(pl.multiple_of(tile * TILE, TILE), TILE)
        out_ref[here, :] = moved.astype(jnp.bfloat16)


def sort_kernel(plan, group_ref, arrived_ref, out_ref):
    for source in range(plan.devices):
        group = group_ref[source, 0]

        @pl.when(group > 0)
        def _():
            here = pl.ds(pl.multiple_of((group - 1) * plan.cap, plan.cap), plan.cap)
            out_ref[here, :] = arrived_ref[source * plan.cap : (source + 1) * plan.cap, :]


def block_best(keys_ref, queries_ref, best_ref):
    rows = keys_ref.shape[0]

    @pl.loop(0, rows // TILE)
    def _(tile):
        keys = keys_ref[pl.ds(pl.multiple_of(tile * TILE, TILE), TILE), :]
        scores = lax.dot_general(
            keys, queries_ref[...], (((1,), (1,)), ((), ())), preferred_element_type=jnp.float32
        )
        best_ref[...] = jnp.maximum(best_ref[...], jnp.max(scores, axis=0, keepdims=True))


def triangle_best(rows_ref, best_ref):
    rows = rows_ref.shape[0]
    for first in range(0, rows, TILE):
        scores = lax.dot_general(
            rows_ref[first : first + TILE, :],
            rows_ref[first:, :],
            (((1,), (1,)), ((), ())),
            preferred_element_type=jnp.float32,
        )
        key = lax.broadcasted_iota(jnp.int32, (TILE, TILE), 0)
        query = lax.broadcasted_iota(jnp.int32, (TILE, TILE), 1)
        corner = jnp.max(
            jnp.where(key < query, scores[:, :TILE], -2.0), axis=0, keepdims=True
        )
        here = slice(first, first + TILE)
        best_ref[:, here] = jnp.maximum(best_ref[:, here], corner)
        if first + TILE < rows:
            rest = jnp.max(scores[:, TILE:], axis=0, keepdims=True)
            there = slice(first + TILE, rows)
            best_ref[:, there] = jnp.maximum(best_ref[:, there], rest)


def best_kernel(plan, run_len_ref, place_ref, group_ref, own_ref, mate_ref, *rest):
    behind, (out_ref, best_ref, blocks_ref) = rest[:-3], rest[-3:]
    group, slot = plan.slot(place_ref[0], place_ref[1])
    begin = jnp.int32(0)
    for number, start in enumerate(cluster_starts(plan, run_len_ref)):
        here = (number // plan.per_group == group) & (start <= slot)
        begin = jnp.where(here, jnp.maximum(begin, start), begin)
    best_ref[...] = jnp.full(best_ref.shape, -1.0, jnp.float32)
    triangle_best(own_ref, best_ref)

    @pl.when(slot % 2 == 1)
    def _():
        block_best(mate_ref, own_ref, best_ref)

    for distance in range(1, plan.reach // 2):
        first, second = behind[2 * distance - 2], behind[2 * distance - 1]

        @pl.when(slot - slot % 2 - 2 * distance >= begin)
        def _():
            block_best(first, own_ref, best_ref)
            block_best(second, own_ref, best_ref)

    for number in range(plan.rows // plan.cap):
        part = best_ref[:, number * plan.cap : (number + 1) * plan.cap]
        blocks_ref[number : number + 1, : plan.cap] = part
    for source in range(plan.devices):
        chosen = jnp.maximum(group_ref[source, 0] - 1, 0)
        out_ref[source : source + 1, :] = blocks_ref[pl.ds(chosen, 1), :]


def unpack_kernel(plan, run_len_ref, cluster_ref, rank_ref, reply_ref, out_ref):
    owner, within = row_owner(plan, run_len_ref, cluster_ref[...], rank_ref[...])
    number = lax.broadcasted_iota(jnp.int32, (plan.devices, plan.rows), 0)
    chosen = jnp.where(number == owner, 1.0, 0.0)
    columns = lax.dot_general(
        reply_ref[:, : plan.cap],
        chosen,
        (((0,), (0,)), ((), ())),
        precision=lax.Precision.HIGHEST,
        preferred_element_type=jnp.float32,
    )
    lane = lax.broadcasted_iota(jnp.int32, (plan.cap, plan.rows), 0)
    out_ref[...] = jnp.sum(
        jnp.where(lane == within % plan.cap, columns, 0.0), axis=0, keepdims=True
    )


def lane_of(plan, slot):
    device = plan.device(0, slot)
    return device // plan.run * plan.width + device % plan.run


def chip_change(plan, change):
    width = plan.width
    return change % width + change // (2 * width) * width, change // width % 2


def lane_change(plan, chip, core):
    width = plan.width
    return chip % width + core * width + chip // width * 2 * width


def lane_device(plan, layer, lane):
    return lane // plan.width * plan.run + layer * plan.width + lane % plan.width


def my_lane(plan):
    run = lax.axis_index("run")
    return lax.axis_index("ingest") * plan.width + run % plan.width, run // plan.width


def spread_pair(plan, part, target, rows):
    row = lax.broadcasted_iota(jnp.int32, (2 * plan.part, plan.rows), 0) + part * plan.part
    chosen = jnp.where(row == target, 1.0, 0.0).astype(jnp.bfloat16)
    return jnp.dot(chosen, rows, preferred_element_type=jnp.float32).astype(jnp.bfloat16)


def spread_more_kernel(plan, unit_ref, target_ref, out_ref):
    lane, _ = my_lane(plan)
    for part in range(0, plan.lanes, 2):
        moved = spread_pair(plan, part, target_ref[...], unit_ref[:, plan.chunks[0] :])
        for number in range(2):
            whole = pl.multiple_of((part + number ^ lane) * plan.part, plan.part)
            here = moved[number * plan.part : (number + 1) * plan.part, :]
            out_ref[pl.ds(whole, plan.part), :] = here


def spread_kernel(plan, run_len_ref, cluster_ref, rank_ref, rows_ref, *rest):
    outs, (unit_ref, target_ref) = rest[:-2], rest[-2:]
    step = 128

    @pl.loop(0, plan.rows // step, unroll=True)
    def _(number):
        here = pl.ds(pl.multiple_of(number * step, step), step)
        widened = rows_ref[here, :].astype(jnp.float32)
        total = jnp.sum(widened * widened, axis=1, keepdims=True) + EPSILON
        unit_ref[here, :] = (widened * lax.rsqrt(total)).astype(jnp.bfloat16)

    lane, _ = my_lane(plan)
    group, slot, within = row_slot(plan, run_len_ref, cluster_ref[...], rank_ref[...])
    owner = group * plan.run + slot
    number = lax.broadcasted_iota(jnp.int32, (plan.devices, plan.rows), 0)
    member = number == owner
    block = jnp.max(jnp.where(member, within // plan.cap + 1, 0), axis=1, keepdims=True)
    present = jnp.where(block > 0, 1.0, 0.0)
    before = lax.broadcasted_iota(jnp.int32, (plan.devices, plan.devices), 0) > (
        lax.broadcasted_iota(jnp.int32, (plan.devices, plan.devices), 1)
    )
    order = jnp.dot(
        jnp.where(before, 1.0, 0.0),
        jnp.broadcast_to(present, (plan.devices, 128)),
        preferred_element_type=jnp.float32,
    )
    mine = jnp.sum(jnp.where(member, order[:, :1], 0.0), axis=0, keepdims=True)
    residue = within % plan.cap
    target = (
        (residue // plan.slice ^ lane) * plan.part
        + mine.astype(jnp.int32) * plan.slice
        + residue % plan.slice
    )
    target_ref[...] = target
    for part in range(0, plan.lanes, 2):
        moved = spread_pair(plan, part, target, unit_ref[:, : plan.chunks[0]])
        outs[part][: plan.part, :] = moved[: plan.part, :]
        outs[part + 1][: plan.part, :] = moved[plan.part :, :]

    place = lax.broadcasted_iota(jnp.int32, (plan.devices, plan.part), 1) // plan.slice
    here = (place.astype(jnp.float32) == order[:, :1]) & (block > 0)
    who = lax.broadcasted_iota(jnp.int32, (plan.devices, plan.part), 0)
    owners = jnp.sum(jnp.where(here, who, 0), axis=0, keepdims=True)
    blocks = jnp.sum(jnp.where(here, block - 1, 0), axis=0, keepdims=True)
    line = lax.broadcasted_iota(jnp.int32, (16, plan.part), 0)
    table = jnp.where(line == 0, owners, jnp.where(line == 1, blocks, 0))
    for out in outs:
        out[plan.part :, : plan.part] = table.astype(jnp.float32).astype(jnp.bfloat16)


def permute_into(target, first, inputs_ref, outs, room, stride):
    columns = inputs_ref.shape[0]
    for number, out in enumerate(outs):
        row = lax.broadcasted_iota(jnp.int32, (room, columns), 0) + first + number * stride
        chosen = jnp.where(row == target, 1.0, 0.0).astype(jnp.bfloat16)
        moved = jnp.dot(chosen, inputs_ref[...], preferred_element_type=jnp.float32)
        out[:room, :] = moved.astype(jnp.bfloat16)


def route_kernel(plan, *refs):
    ins, rest = refs[: plan.lanes], refs[plan.lanes :]
    outs, (target_ref, inputs_ref, owner_ref, block_ref, value_ref) = rest[:-5], rest[-5:]
    _, layer = my_lane(plan)
    for number, part in enumerate(ins):
        inputs_ref[number * plan.part : (number + 1) * plan.part, :] = part[: plan.part, :]
        table = part[plan.part :, : plan.part].astype(jnp.float32)
        owner_ref[number : number + 1, :] = table[0:1, :].astype(jnp.int32)
        block_ref[number : number + 1, :] = table[1:2, :].astype(jnp.int32)
    owner = owner_ref[...]
    shape = (plan.part, plan.part)
    earlier = lax.broadcasted_iota(jnp.int32, shape, 0) < lax.broadcasted_iota(jnp.int32, shape, 1)
    earlier = jnp.where(earlier, 1.0, 0.0)
    ones = jnp.ones(shape, jnp.float32)
    shape = (plan.lanes, plan.lanes)
    above = lax.broadcasted_iota(jnp.int32, shape, 0) > lax.broadcasted_iota(jnp.int32, shape, 1)
    above = jnp.where(above, 1.0, 0.0)
    target = jnp.zeros(owner.shape, jnp.int32)
    most = jnp.float32(0.0)
    for other in range(plan.layers):
        chosen = owner // plan.run == other
        marks = jnp.where(chosen, 1.0, 0.0)
        lines = jnp.dot(marks, ones, preferred_element_type=jnp.float32)
        count = jnp.dot(marks, earlier, preferred_element_type=jnp.float32) + jnp.dot(
            above, lines, preferred_element_type=jnp.float32
        )
        count = count.astype(jnp.int32)
        there = jnp.where(count < plan.room, (layer ^ other) * plan.stride + count, -1)
        target = jnp.where(chosen, there, target)
        most = jnp.maximum(most, jnp.sum(marks))
    full = jnp.where(most > plan.room, 1.0, 0.0)
    value = owner % plan.run * plan.blocks + block_ref[...] + 1
    for number in range(plan.lanes):
        here = slice(number * plan.part, (number + 1) * plan.part)
        target_ref[:, here] = target[number : number + 1, :]
        value_ref[:, here] = value[number : number + 1, :].astype(jnp.float32)
    target = target_ref[...]
    values = jnp.broadcast_to(value_ref[...], (8, plan.rows)).astype(jnp.bfloat16)
    for number, out in enumerate(outs):
        row = lax.broadcasted_iota(jnp.int32, (plan.stride, plan.rows), 0) + number * plan.stride
        chosen = jnp.where(row == target, 1.0, 0.0).astype(jnp.bfloat16)
        moved = jnp.dot(
            chosen[: plan.room, :], inputs_ref[...], preferred_element_type=jnp.float32
        )
        out[: plan.room, :] = moved.astype(jnp.bfloat16)
        listed = lax.dot_general(
            values, chosen, (((1,), (1,)), ((), ())), preferred_element_type=jnp.float32
        )
        line = lax.broadcasted_iota(jnp.int32, (16, 128), 0)
        table = jnp.where(line == 15, full, 0.0)
        for piece in range(plan.stride // 128):
            here = listed[0:1, piece * 128 : (piece + 1) * 128]
            table = jnp.where(line == piece, here, table)
        out[plan.room :, :128] = table.astype(jnp.bfloat16)


def route_more_kernel(plan, target_ref, rows_ref, *refs, chunk):
    outs, inputs_ref = refs[:-1], refs[-1]
    lane, _ = my_lane(plan)
    first = sum(plan.chunks[1:chunk])
    for number in range(plan.lanes):
        whole = pl.multiple_of((number ^ lane) * plan.part, plan.part)
        inputs_ref[number * plan.part : (number + 1) * plan.part, :] = rows_ref[
            pl.ds(whole, plan.part), first : first + plan.chunks[chunk]
        ]
    permute_into(target_ref[...], 0, inputs_ref, outs, plan.room, plan.stride)


def gather_rows(plan, ins, inputs_ref):
    for number, part in enumerate(ins):
        first = number * plan.stride
        inputs_ref[first : first + plan.room, :] = part[: plan.room, :]
        if plan.stride > plan.room:
            inputs_ref[first + plan.room : first + plan.stride, :] = jnp.zeros(
                (plan.stride - plan.room, inputs_ref.shape[1]), jnp.bfloat16
            )


def sort_parts(plan, target, inputs_ref, outs, sorted_ref):
    tile = 2 * plan.part
    for chip, out in enumerate(outs):
        row = lax.broadcasted_iota(jnp.int32, (tile, inputs_ref.shape[0]), 0) + chip * tile
        chosen = jnp.where(row == target, 1.0, 0.0).astype(jnp.bfloat16)
        moved = jnp.dot(chosen, inputs_ref[...], preferred_element_type=jnp.float32)
        moved = moved.astype(jnp.bfloat16)
        sorted_ref[chip * tile : (chip + 1) * tile, :] = moved
        out[:tile, :] = moved
    lane, _ = my_lane(plan)
    chip, _ = chip_change(plan, lane_of(plan, 0) ^ lane)
    ahead = sorted_ref[pl.ds(pl.multiple_of(chip * tile, tile), tile), :]
    for out in outs:
        out[tile:, :] = ahead


def deliver_kernel(plan, *refs):
    ins, rest = refs[: plan.layers], refs[plan.layers :]
    outs, (target_ref, full_ref, inputs_ref, sorted_ref) = rest[:-4], rest[-4:]
    lane, _ = my_lane(plan)
    gather_rows(plan, ins, inputs_ref)
    full = jnp.zeros((8, 128), jnp.float32)
    for number, part in enumerate(ins):
        table = part[plan.room :, :128].astype(jnp.float32)
        lines = [table[piece : piece + 1, :] for piece in range(plan.stride // 128)]
        value = jnp.concatenate(lines, axis=1).astype(jnp.int32) - 1
        full = jnp.maximum(full, jnp.broadcast_to(table[15:, :], (8, 128)))
        slot = value // plan.blocks
        within = lax.broadcasted_iota(jnp.int32, value.shape, 1) % plan.slice
        chip, _ = chip_change(plan, lane_of(plan, slot) ^ lane)
        target = (2 * chip + slot % 2) * plan.part + value % plan.blocks * plan.slice + within
        target_ref[:, number * plan.stride : (number + 1) * plan.stride] = jnp.where(
            value >= 0, target, -1
        )
    full_ref[...] = full.astype(jnp.int32)
    sort_parts(plan, target_ref[...], inputs_ref, outs, sorted_ref)


def deliver_more_kernel(plan, target_ref, *refs):
    ins, rest = refs[: plan.layers], refs[plan.layers :]
    outs, (inputs_ref, sorted_ref) = rest[:-2], rest[-2:]
    gather_rows(plan, ins, inputs_ref)
    sort_parts(plan, target_ref[...], inputs_ref, outs, sorted_ref)


def join_kernel(plan, *refs):
    ins, outs = refs[:-2], refs[-2:]
    tile = 2 * plan.part
    for number, part in enumerate(ins):
        for half, out in enumerate(outs):
            out[number * tile : (number + 1) * tile, :] = part[half * tile : (half + 1) * tile, :]


def add_best(keys, queries_ref, best_ref, allowed=None):
    scores = lax.dot_general(
        keys, queries_ref[...], (((1,), (1,)), ((), ())), preferred_element_type=jnp.float32
    )
    if allowed is not None:
        scores = jnp.where(allowed, scores, -2.0)
    best_ref[...] = jnp.maximum(best_ref[...], jnp.max(scores, axis=0, keepdims=True))


def staged_best_kernel(plan, run_len_ref, *refs):
    count = len(plan.chunks)
    own, mate, behind, far = (refs[n * count : (n + 1) * count] for n in range(4))
    out_ref, best_ref, queries_ref, lines_ref = refs[4 * count :]
    lane, _ = my_lane(plan)
    group, slot = plan.slot(lax.axis_index("ingest"), lax.axis_index("run"))
    core = slot % 2
    begin = jnp.int32(0)
    for number, start in enumerate(cluster_starts(plan, run_len_ref)):
        here = (number // plan.per_group == group) & (start <= slot)
        begin = jnp.where(here, jnp.maximum(begin, start), begin)
    chips = plan.lanes // 2
    for side, parts in enumerate((own, mate)):
        for chip in range(chips):
            there = pl.ds(pl.multiple_of((2 * chip + core) * plan.part, plan.part), plan.part)
            here = slice((side * chips + chip) * plan.part, (side * chips + chip + 1) * plan.part)
            first = 0
            for part in parts:
                queries_ref[here, first : first + part.shape[1]] = part[there, :]
                first += part.shape[1]

    def slots(row):
        line = row // plan.part
        source = lane_change(plan, line % chips, line // chips) ^ lane
        block = row // plan.slice % plan.blocks
        return block * plan.cap + source * plan.slice + row % plan.slice

    best_ref[...] = jnp.full(best_ref.shape, -1.0, jnp.float32)
    query = slots(lax.broadcasted_iota(jnp.int32, (1, plan.rows), 1))
    for first in range(0, plan.rows, TILE):
        key = slots(lax.broadcasted_iota(jnp.int32, (TILE, 1), 0) + first)
        add_best(queries_ref[first : first + TILE, :], queries_ref, best_ref, key < query)

    @pl.when(core == 1)
    def _():
        for parts in (own, mate):
            for pair in range(0, chips, 2):
                keys = []
                for number in (pair, pair + 1):
                    here = slice(2 * number * plan.part, (2 * number + 1) * plan.part)
                    keys.append(jnp.concatenate([part[here, :] for part in parts], axis=1))
                add_best(jnp.concatenate(keys, axis=0), queries_ref, best_ref)

    @pl.when(slot - core - 2 >= begin)
    def _():
        for parts in (behind, far):
            for first in range(0, plan.rows, TILE):
                keys = [part[first : first + TILE, :] for part in parts]
                add_best(jnp.concatenate(keys, axis=1), queries_ref, best_ref)

    for number in range(plan.lanes):
        lines_ref[number : number + 1, :] = best_ref[
            :, number * plan.part : (number + 1) * plan.part
        ]
    for device in range(plan.devices):
        out_ref[device] = lines_ref[...]


def staged_unpack_kernel(plan, run_len_ref, cluster_ref, rank_ref, reply_ref, out_ref):
    group, slot, within = row_slot(plan, run_len_ref, cluster_ref[...], rank_ref[...])
    residue = within % plan.cap
    chip, core = chip_change(plan, residue // plan.slice ^ lane_of(plan, slot))
    line = plan.device(group, slot) * plan.lanes + core * (plan.lanes // 2) + chip
    column = within // plan.cap * plan.slice + residue % plan.slice
    number = lax.broadcasted_iota(jnp.int32, (plan.devices * plan.lanes, plan.rows), 0)
    columns = lax.dot_general(
        reply_ref[...],
        jnp.where(number == line, 1.0, 0.0),
        (((0,), (0,)), ((), ())),
        precision=lax.Precision.HIGHEST,
        preferred_element_type=jnp.float32,
    )
    place = lax.broadcasted_iota(jnp.int32, (plan.part, plan.rows), 0)
    out_ref[...] = jnp.sum(jnp.where(place == column, columns, 0.0), axis=0, keepdims=True)


SMEM = pl.BlockSpec(memory_space=pltpu.SMEM)
VMEM = pl.BlockSpec(memory_space=pltpu.VMEM)


def call(kernel, plan, shapes, specs, scratch=(), flops=0, moved=0, memory=32):
    return pl.pallas_call(
        functools.partial(kernel, plan),
        out_shape=shapes,
        in_specs=specs,
        out_specs=[VMEM] * len(shapes),
        scratch_shapes=scratch,
        compiler_params=pltpu.CompilerParams(vmem_limit_bytes=memory * MIB),
        cost_estimate=pl.CostEstimate(flops=flops, bytes_accessed=moved, transcendentals=0),
    )


def exchange(block):
    return lax.all_to_all(block, AXES, split_axis=0, concat_axis=0, tiled=True)


def direct(plan, embeddings, clusters, ranks, run_len):
    rows, width = embeddings.shape
    slots = plan.devices * plan.cap
    wide = jax.ShapeDtypeStruct
    outgoing, groups = call(
        pack_kernel,
        plan,
        [wide((slots, width), jnp.bfloat16), wide((plan.devices, 128), jnp.int32)],
        [SMEM, VMEM, VMEM, VMEM],
        [pltpu.VMEM((rows, width), jnp.bfloat16)],
        2 * slots * rows * width,
        3 * rows * width * 2,
    )(run_len, clusters, ranks, embeddings)
    groups = exchange(groups)
    arrived = exchange(outgoing)
    (own,) = call(
        sort_kernel, plan, [wide((rows, width), jnp.bfloat16)], [SMEM, VMEM],
        moved=3 * rows * width * 2,
    )(groups, arrived)

    def swap(block):
        pairs = [
            (i * plan.run + r, (i ^ 1) * plan.run + r)
            for i in range(plan.ingest)
            for r in range(plan.run)
        ]
        return lax.ppermute(block, AXES, pairs)

    mate = swap(own)
    behind = []
    for distance, chips in enumerate(plan.links()):
        if distance == 0:
            continue
        pairs = [
            (plan.device(i, 2 * chip + core), plan.device(i, 2 * (chip + distance) + core))
            for i in range(plan.ingest)
            for chip in chips
            for core in range(2)
        ]
        moved = lax.ppermute(own, AXES, pairs)
        behind += [moved, swap(moved)]
    place = jnp.stack([lax.axis_index("ingest"), lax.axis_index("run")]).astype(jnp.int32)
    (replies,) = call(
        best_kernel,
        plan,
        [wide((plan.devices, 128), jnp.float32)],
        [SMEM, SMEM, SMEM] + [VMEM] * (2 + len(behind)),
        [pltpu.VMEM((1, rows), jnp.float32), pltpu.VMEM((rows // plan.cap, 128), jnp.float32)],
        2 * rows * rows * width * 3,
        4 * rows * width * 2,
    )(run_len, place, groups, own, mate, *behind)
    returned = exchange(replies)
    (best,) = call(
        unpack_kernel, plan, [wide((1, rows), jnp.float32)], [SMEM, VMEM, VMEM, VMEM],
        moved=4 * rows * 4,
    )(run_len, clusters, ranks, returned)
    return best


def staged(plan, embeddings, clusters, ranks, run_len):
    rows, width = embeddings.shape
    wide = jax.ShapeDtypeStruct
    half = jnp.bfloat16
    lanes, layers = range(plan.lanes), range(plan.layers)

    def along_lanes(block, change):
        pairs = [
            (lane_device(plan, layer, lane), lane_device(plan, layer, lane ^ change))
            for layer in layers
            for lane in lanes
        ]
        return lax.ppermute(block, AXES, pairs)

    def along_layers(block, change):
        pairs = [
            (lane_device(plan, layer, lane), lane_device(plan, layer ^ change, lane))
            for layer in layers
            for lane in lanes
        ]
        return lax.ppermute(block, AXES, pairs)

    far_first = sorted(lanes[1:], key=lambda change: -(change & 1) - (change // plan.width // 2))

    *spread, unit, target = call(
        spread_kernel,
        plan,
        [wide((plan.part + 16, plan.chunks[0]), half) for _ in lanes]
        + [wide((rows, width), half), wide((1, rows), jnp.int32)],
        [SMEM, VMEM, VMEM, VMEM],
        (),
        2 * rows * rows * plan.chunks[0],
        3 * rows * width * 2,
        memory=24,
    )(run_len, clusters, ranks, embeddings)
    (later,) = call(
        spread_more_kernel,
        plan,
        [wide((rows, width - plan.chunks[0]), half)],
        [VMEM, VMEM],
        (),
        2 * rows * rows * (width - plan.chunks[0]),
        3 * rows * width * 2,
        memory=16,
    )(unit, target)
    swapped = {change: along_lanes(spread[change], change) for change in far_first}
    spread = [spread[0]] + [swapped[change] for change in lanes[1:]]
    pair, mates, behind, fars = [], [], [], []
    table = targets = full = None
    arrivals, routes = [], []
    for chunk, f in enumerate(plan.chunks):
        spec = dict(flops=2 * rows * rows * f, moved=3 * rows * f * 2, memory=12)
        rooms = [wide((plan.room + (0 if chunk else 16), f), half) for _ in layers]
        inputs = pltpu.VMEM((rows, f), half)
        if chunk == 0:
            *routed, table = call(
                route_kernel,
                plan,
                [*rooms, wide((1, rows), jnp.int32)],
                [VMEM] * plan.lanes,
                [
                    inputs,
                    pltpu.VMEM((plan.lanes, plan.part), jnp.int32),
                    pltpu.VMEM((plan.lanes, plan.part), jnp.int32),
                    pltpu.VMEM((1, rows), jnp.float32),
                ],
                **spec,
            )(*spread)
        else:
            if chunk == 1:
                later, _ = lax.optimization_barrier((later, table))
                groups = [[lane_device(plan, layer, lane) for lane in lanes] for layer in layers]
                later = lax.all_to_all(
                    later, AXES, 0, 0, tiled=True, axis_index_groups=groups
                )
            more = functools.partial(route_more_kernel, chunk=chunk)
            routed = call(more, plan, rooms, [VMEM] * 2, [inputs], **spec)(table, later)
        moved = {change: along_layers(routed[change], change) for change in reversed(layers[1:])}
        arrived = [routed[0]] + [moved[change] for change in layers[1:]]
        arrivals.append(arrived)
        routes.append(routed)
    for chunk, f in enumerate(plan.chunks):
        spec = dict(flops=2 * rows * rows * f, moved=3 * rows * f * 2, memory=12)
        inputs = pltpu.VMEM((rows, f), half)
        arrived = arrivals[chunk]
        ahead = chunk + 1
        if chunk:
            arrived, _ = lax.optimization_barrier((arrived, parts))
        if ahead < len(plan.chunks):
            arrived, _ = lax.optimization_barrier((arrived, arrivals[ahead][1] if ahead + 1 == len(plan.chunks) else routes[ahead]))
        shapes = [wide((4 * plan.part, f), half) for _ in range(plan.lanes // 2)]
        scratch = [pltpu.VMEM((plan.layers * plan.stride, f), half), inputs]
        if chunk == 0:
            *parts, targets, full = call(
                deliver_kernel,
                plan,
                [
                    *shapes,
                    wide((1, plan.layers * plan.stride), jnp.int32),
                    wide((8, 128), jnp.int32),
                ],
                [VMEM] * plan.layers,
                scratch,
                **spec,
            )(*arrived)
        else:
            parts = call(
                deliver_more_kernel, plan, shapes, [VMEM] * (1 + plan.layers), scratch, **spec
            )(targets, *arrived)
        parts = [
            along_lanes(part, lane_change(plan, chip, 0)) if chip else part
            for chip, part in enumerate(parts)
        ]
        spec = dict(moved=8 * rows * f * 2, memory=8)
        joined = call(
            join_kernel, plan, [wide((rows, f), half)] * 2, [VMEM] * len(parts), **spec
        )(*parts)
        for kept, block in zip((pair, behind), joined):
            kept.append(block)
        for kept, block in zip((mates, fars), joined):
            kept.append(along_lanes(block, plan.width))
    count = len(plan.chunks)
    (replies,) = call(
        staged_best_kernel,
        plan,
        [wide((plan.devices, plan.lanes, 128), jnp.float32)],
        [SMEM] + [VMEM] * (4 * count),
        [
            pltpu.VMEM((1, rows), jnp.float32),
            pltpu.VMEM((rows, width), half),
            pltpu.VMEM((plan.lanes, 128), jnp.float32),
        ],
        2 * rows * rows * width * 3,
        4 * rows * width * 2,
        memory=24,
    )(run_len, *pair, *mates, *behind, *fars)
    returned = exchange(replies).reshape(plan.devices * plan.lanes, 128)
    (best,) = call(
        staged_unpack_kernel,
        plan,
        [wide((1, rows), jnp.float32)],
        [SMEM, VMEM, VMEM, VMEM],
        moved=4 * rows * 4,
        memory=8,
    )(run_len, clusters, ranks, returned)
    return best, full[0, 0]


def local(embeddings, cluster_id, rank, run_len):
    rows, width = embeddings.shape
    plan = Plan(lax.axis_size("ingest"), lax.axis_size("run"), run_len.shape[0], rows, width)
    given = (embeddings, cluster_id.reshape(1, rows), rank.reshape(1, rows), run_len)
    if not plan.staged():
        return direct(plan, *given).reshape(rows)
    best, full = staged(plan, *given)
    best = lax.cond(full > 0, lambda: direct(plan, *given), lambda: best)
    return best.reshape(rows)


def solution(mesh):
    return jax.shard_map(
        local,
        mesh=mesh,
        in_specs=(P(AXES, None), P(AXES), P(AXES), P()),
        out_specs=P(AXES),
        check_vma=False,
    )
```

```python
import functools

import jax
import jax.numpy as jnp
from jax import lax
from jax.experimental import pallas as pl
from jax.experimental.pallas import tpu as pltpu
from jax.sharding import PartitionSpec as P

EPSILON = 1e-06
AXES = ("ingest", "run")
TILE = 512
SHARES = (1, 1, 1)
MIB = 1024 * 1024


class Plan:
    def __init__(self, ingest, run, clusters, rows, features):
        self.ingest, self.run, self.clusters, self.rows = ingest, run, clusters, rows
        self.devices = ingest * run
        self.per_group = clusters // ingest
        self.cap = 2 * rows // self.devices
        self.reach = min(8, run // 2)
        self.width = run // ingest
        self.pairs = run // 2
        self.blocks = rows // self.cap
        self.layers, self.lanes = ingest, ingest * self.width
        self.slice = self.cap // self.lanes
        self.part = self.blocks * self.slice
        self.chunks = tuple(features * share // sum(SHARES) for share in SHARES)
        mean = rows // self.layers
        self.room = mean + mean // 8
        self.stride = -(-self.room // 128) * 128

    def staged(self):
        powers = all(n & (n - 1) == 0 for n in (self.layers, self.lanes, self.width))
        return (
            powers
            and self.cap % (8 * self.lanes) == 0
            and self.part == 128
            and self.room % 16 == 0
            and all(width % 128 == 0 for width in self.chunks)
            and self.links()[1:] == [[0]]
        )

    def device(self, group, slot):
        core, chip = slot % 2, slot // 2
        column, place = chip // self.width, chip % self.width
        odd = column % 2
        place = place + odd * (self.width - 1 - 2 * place)
        return (2 * column + core) * self.run + group * self.width + place

    def slot(self, device_ingest, device_run):
        core, column = device_ingest % 2, device_ingest // 2
        place = device_run % self.width
        place = place + (column % 2) * (self.width - 1 - 2 * place)
        return device_run // self.width, 2 * (column * self.width + place) + core

    def splits(self):
        def parts(total, count, top):
            if count == 0:
                if total == 0:
                    yield ()
                return
            for first in range(min(top, total), 0, -1):
                for rest in parts(total - first, count - 1, first):
                    yield (first, *rest)

        return list(parts(self.pairs, self.per_group, self.reach // 2))

    def links(self):
        found = [set() for _ in range(self.reach // 2)]
        for split in self.splits():
            begin = 0
            for length in split:
                for first in range(length):
                    for second in range(first + 1, length):
                        found[second - first].add(begin + first)
                begin += length
        return [sorted(chips) for chips in found]


def cluster_starts(plan, run_len_ref):
    starts = []
    for cluster in range(plan.clusters):
        base = cluster // plan.per_group * plan.per_group
        mine = run_len_ref[cluster]
        total = jnp.int32(0)
        for other in range(base, base + plan.per_group):
            if other == cluster:
                continue
            theirs = run_len_ref[other]
            ahead = (theirs >= mine) if other < cluster else (theirs > mine)
            total = total + jnp.where(ahead, theirs, 0)
        starts.append(total)
    return starts


def row_slot(plan, run_len_ref, cluster, rank):
    starts = cluster_starts(plan, run_len_ref)
    begin = jnp.zeros_like(cluster)
    group = jnp.zeros_like(cluster)
    for number, start in enumerate(starts):
        here = cluster == number
        begin = jnp.where(here, start, begin)
        group = jnp.where(here, number // plan.per_group, group)
    return group, begin + rank // plan.rows, rank % plan.rows


def row_owner(plan, run_len_ref, cluster, rank):
    group, slot, within = row_slot(plan, run_len_ref, cluster, rank)
    return plan.device(group, slot), within


def pack_kernel(plan, run_len_ref, cluster_ref, rank_ref, rows_ref, out_ref, group_ref, unit_ref):
    step = 128

    @pl.loop(0, plan.rows // step)
    def _(number):
        here = pl.ds(pl.multiple_of(number * step, step), step)
        widened = rows_ref[here, :].astype(jnp.float32)
        total = jnp.sum(widened * widened, axis=1, keepdims=True) + EPSILON
        unit_ref[here, :] = (widened * lax.rsqrt(total)).astype(jnp.bfloat16)

    owner, within = row_owner(plan, run_len_ref, cluster_ref[...], rank_ref[...])
    number = lax.broadcasted_iota(jnp.int32, (plan.devices, plan.rows), 0)
    group = jnp.max(
        jnp.where(number == owner, within // plan.cap + 1, 0), axis=1, keepdims=True
    )
    group_ref[...] = jnp.broadcast_to(group, group_ref.shape)
    position = owner * plan.cap + within % plan.cap

    @pl.loop(0, plan.devices * plan.cap // TILE)
    def _(tile):
        row = lax.broadcasted_iota(jnp.int32, (TILE, plan.rows), 0) + tile * TILE
        chosen = jnp.where(row == position, 1.0, 0.0).astype(jnp.bfloat16)
        moved = jnp.dot(chosen, unit_ref[...], preferred_element_type=jnp.float32)
        here = pl.ds(pl.multiple_of(tile * TILE, TILE), TILE)
        out_ref[here, :] = moved.astype(jnp.bfloat16)


def sort_kernel(plan, group_ref, arrived_ref, out_ref):
    for source in range(plan.devices):
        group = group_ref[source, 0]

        @pl.when(group > 0)
        def _():
            here = pl.ds(pl.multiple_of((group - 1) * plan.cap, plan.cap), plan.cap)
            out_ref[here, :] = arrived_ref[source * plan.cap : (source + 1) * plan.cap, :]


def block_best(keys_ref, queries_ref, best_ref):
    rows = keys_ref.shape[0]

    @pl.loop(0, rows // TILE)
    def _(tile):
        keys = keys_ref[pl.ds(pl.multiple_of(tile * TILE, TILE), TILE), :]
        scores = lax.dot_general(
            keys, queries_ref[...], (((1,), (1,)), ((), ())), preferred_element_type=jnp.float32
        )
        best_ref[...] = jnp.maximum(best_ref[...], jnp.max(scores, axis=0, keepdims=True))


def triangle_best(rows_ref, best_ref):
    rows = rows_ref.shape[0]
    for first in range(0, rows, TILE):
        scores = lax.dot_general(
            rows_ref[first : first + TILE, :],
            rows_ref[first:, :],
            (((1,), (1,)), ((), ())),
            preferred_element_type=jnp.float32,
        )
        key = lax.broadcasted_iota(jnp.int32, (TILE, TILE), 0)
        query = lax.broadcasted_iota(jnp.int32, (TILE, TILE), 1)
        corner = jnp.max(
            jnp.where(key < query, scores[:, :TILE], -2.0), axis=0, keepdims=True
        )
        here = slice(first, first + TILE)
        best_ref[:, here] = jnp.maximum(best_ref[:, here], corner)
        if first + TILE < rows:
            rest = jnp.max(scores[:, TILE:], axis=0, keepdims=True)
            there = slice(first + TILE, rows)
            best_ref[:, there] = jnp.maximum(best_ref[:, there], rest)


def best_kernel(plan, run_len_ref, place_ref, group_ref, own_ref, mate_ref, *rest):
    behind, (out_ref, best_ref, blocks_ref) = rest[:-3], rest[-3:]
    group, slot = plan.slot(place_ref[0], place_ref[1])
    begin = jnp.int32(0)
    for number, start in enumerate(cluster_starts(plan, run_len_ref)):
        here = (number // plan.per_group == group) & (start <= slot)
        begin = jnp.where(here, jnp.maximum(begin, start), begin)
    best_ref[...] = jnp.full(best_ref.shape, -1.0, jnp.float32)
    triangle_best(own_ref, best_ref)

    @pl.when(slot % 2 == 1)
    def _():
        block_best(mate_ref, own_ref, best_ref)

    for distance in range(1, plan.reach // 2):
        first, second = behind[2 * distance - 2], behind[2 * distance - 1]

        @pl.when(slot - slot % 2 - 2 * distance >= begin)
        def _():
            block_best(first, own_ref, best_ref)
            block_best(second, own_ref, best_ref)

    for number in range(plan.rows // plan.cap):
        part = best_ref[:, number * plan.cap : (number + 1) * plan.cap]
        blocks_ref[number : number + 1, : plan.cap] = part
    for source in range(plan.devices):
        chosen = jnp.maximum(group_ref[source, 0] - 1, 0)
        out_ref[source : source + 1, :] = blocks_ref[pl.ds(chosen, 1), :]


def unpack_kernel(plan, run_len_ref, cluster_ref, rank_ref, reply_ref, out_ref):
    owner, within = row_owner(plan, run_len_ref, cluster_ref[...], rank_ref[...])
    number = lax.broadcasted_iota(jnp.int32, (plan.devices, plan.rows), 0)
    chosen = jnp.where(number == owner, 1.0, 0.0)
    columns = lax.dot_general(
        reply_ref[:, : plan.cap],
        chosen,
        (((0,), (0,)), ((), ())),
        precision=lax.Precision.HIGHEST,
        preferred_element_type=jnp.float32,
    )
    lane = lax.broadcasted_iota(jnp.int32, (plan.cap, plan.rows), 0)
    out_ref[...] = jnp.sum(
        jnp.where(lane == within % plan.cap, columns, 0.0), axis=0, keepdims=True
    )


def lane_of(plan, slot):
    device = plan.device(0, slot)
    return device // plan.run * plan.width + device % plan.run


def chip_change(plan, change):
    width = plan.width
    return change % width + change // (2 * width) * width, change // width % 2


def lane_change(plan, chip, core):
    width = plan.width
    return chip % width + core * width + chip // width * 2 * width


def lane_device(plan, layer, lane):
    return lane // plan.width * plan.run + layer * plan.width + lane % plan.width


def my_lane(plan):
    run = lax.axis_index("run")
    return lax.axis_index("ingest") * plan.width + run % plan.width, run // plan.width


def spread_pair(plan, part, target, rows):
    row = lax.broadcasted_iota(jnp.int32, (2 * plan.part, plan.rows), 0) + part * plan.part
    chosen = jnp.where(row == target, 1.0, 0.0).astype(jnp.bfloat16)
    return jnp.dot(chosen, rows, preferred_element_type=jnp.float32).astype(jnp.bfloat16)


def spread_more_kernel(plan, unit_ref, target_ref, out_ref):
    lane, _ = my_lane(plan)
    for part in range(0, plan.lanes, 2):
        moved = spread_pair(plan, part, target_ref[...], unit_ref[:, plan.chunks[0] :])
        for number in range(2):
            whole = pl.multiple_of((part + number ^ lane) * plan.part, plan.part)
            here = moved[number * plan.part : (number + 1) * plan.part, :]
            out_ref[pl.ds(whole, plan.part), :] = here


def spread_kernel(plan, run_len_ref, cluster_ref, rank_ref, rows_ref, *rest):
    outs, (unit_ref, target_ref) = rest[:-2], rest[-2:]
    step = 128

    @pl.loop(0, plan.rows // step, unroll=True)
    def _(number):
        here = pl.ds(pl.multiple_of(number * step, step), step)
        widened = rows_ref[here, :].astype(jnp.float32)
        total = jnp.sum(widened * widened, axis=1, keepdims=True) + EPSILON
        unit_ref[here, :] = (widened * lax.rsqrt(total)).astype(jnp.bfloat16)

    lane, _ = my_lane(plan)
    group, slot, within = row_slot(plan, run_len_ref, cluster_ref[...], rank_ref[...])
    owner = group * plan.run + slot
    number = lax.broadcasted_iota(jnp.int32, (plan.devices, plan.rows), 0)
    member = number == owner
    block = jnp.max(jnp.where(member, within // plan.cap + 1, 0), axis=1, keepdims=True)
    present = jnp.where(block > 0, 1.0, 0.0)
    before = lax.broadcasted_iota(jnp.int32, (plan.devices, plan.devices), 0) > (
        lax.broadcasted_iota(jnp.int32, (plan.devices, plan.devices), 1)
    )
    order = jnp.dot(
        jnp.where(before, 1.0, 0.0),
        jnp.broadcast_to(present, (plan.devices, 128)),
        preferred_element_type=jnp.float32,
    )
    mine = jnp.sum(jnp.where(member, order[:, :1], 0.0), axis=0, keepdims=True)
    residue = within % plan.cap
    target = (
        (residue // plan.slice ^ lane) * plan.part
        + mine.astype(jnp.int32) * plan.slice
        + residue % plan.slice
    )
    target_ref[...] = target
    for part in range(0, plan.lanes, 2):
        moved = spread_pair(plan, part, target, unit_ref[:, : plan.chunks[0]])
        outs[part][: plan.part, :] = moved[: plan.part, :]
        outs[part + 1][: plan.part, :] = moved[plan.part :, :]

    place = lax.broadcasted_iota(jnp.int32, (plan.devices, plan.part), 1) // plan.slice
    here = (place.astype(jnp.float32) == order[:, :1]) & (block > 0)
    who = lax.broadcasted_iota(jnp.int32, (plan.devices, plan.part), 0)
    owners = jnp.sum(jnp.where(here, who, 0), axis=0, keepdims=True)
    blocks = jnp.sum(jnp.where(here, block - 1, 0), axis=0, keepdims=True)
    line = lax.broadcasted_iota(jnp.int32, (16, plan.part), 0)
    table = jnp.where(line == 0, owners, jnp.where(line == 1, blocks, 0))
    for out in outs:
        out[plan.part :, : plan.part] = table.astype(jnp.float32).astype(jnp.bfloat16)


def permute_into(target, first, inputs_ref, outs, room, stride):
    columns = inputs_ref.shape[0]
    for number, out in enumerate(outs):
        row = lax.broadcasted_iota(jnp.int32, (room, columns), 0) + first + number * stride
        chosen = jnp.where(row == target, 1.0, 0.0).astype(jnp.bfloat16)
        moved = jnp.dot(chosen, inputs_ref[...], preferred_element_type=jnp.float32)
        out[:room, :] = moved.astype(jnp.bfloat16)


def route_kernel(plan, *refs):
    ins, rest = refs[: plan.lanes], refs[plan.lanes :]
    outs, (target_ref, inputs_ref, owner_ref, block_ref, value_ref) = rest[:-5], rest[-5:]
    _, layer = my_lane(plan)
    for number, part in enumerate(ins):
        inputs_ref[number * plan.part : (number + 1) * plan.part, :] = part[: plan.part, :]
        table = part[plan.part :, : plan.part].astype(jnp.float32)
        owner_ref[number : number + 1, :] = table[0:1, :].astype(jnp.int32)
        block_ref[number : number + 1, :] = table[1:2, :].astype(jnp.int32)
    owner = owner_ref[...]
    marks = [jnp.where(owner // plan.run == other, 1.0, 0.0) for other in range(plan.layers)]
    most = functools.reduce(jnp.maximum, [jnp.sum(mark) for mark in marks])
    stacked = jnp.concatenate(marks, axis=0).astype(jnp.bfloat16)
    shape = (plan.part, plan.part)
    earlier = lax.broadcasted_iota(jnp.int32, shape, 0) < lax.broadcasted_iota(jnp.int32, shape, 1)
    earlier = jnp.where(earlier, 1.0, 0.0).astype(jnp.bfloat16)
    shape = (plan.layers * plan.lanes, plan.layers * plan.lanes)
    line, above = (lax.broadcasted_iota(jnp.int32, shape, axis) for axis in range(2))
    above = (line > above) & (line // plan.lanes == above // plan.lanes)
    above = jnp.where(above, 1.0, 0.0).astype(jnp.bfloat16)
    lines = jnp.dot(above, stacked, preferred_element_type=jnp.float32)
    counts = jnp.dot(stacked, earlier, preferred_element_type=jnp.float32) + jnp.sum(
        lines, axis=1, keepdims=True
    )
    counts = counts.astype(jnp.int32)
    target = jnp.zeros(owner.shape, jnp.int32)
    for other in range(plan.layers):
        count = counts[other * plan.lanes : (other + 1) * plan.lanes, :]
        there = jnp.where(count < plan.room, (layer ^ other) * plan.stride + count, -1)
        target = jnp.where(owner // plan.run == other, there, target)
    full = jnp.where(most > plan.room, 1.0, 0.0)
    value = owner % plan.run * plan.blocks + block_ref[...] + 1
    for number in range(plan.lanes):
        here = slice(number * plan.part, (number + 1) * plan.part)
        target_ref[:, here] = target[number : number + 1, :]
        value_ref[:, here] = value[number : number + 1, :].astype(jnp.float32)
    target = target_ref[...]
    values = jnp.broadcast_to(value_ref[...], (8, plan.rows)).astype(jnp.bfloat16)
    for number, out in enumerate(outs):
        row = lax.broadcasted_iota(jnp.int32, (plan.stride, plan.rows), 0) + number * plan.stride
        chosen = jnp.where(row == target, 1.0, 0.0).astype(jnp.bfloat16)
        moved = jnp.dot(
            chosen[: plan.room, :], inputs_ref[...], preferred_element_type=jnp.float32
        )
        out[: plan.room, :] = moved.astype(jnp.bfloat16)
        listed = lax.dot_general(
            values, chosen, (((1,), (1,)), ((), ())), preferred_element_type=jnp.float32
        )
        line = lax.broadcasted_iota(jnp.int32, (16, 128), 0)
        table = jnp.where(line == 15, full, 0.0)
        for piece in range(plan.stride // 128):
            here = listed[0:1, piece * 128 : (piece + 1) * 128]
            table = jnp.where(line == piece, here, table)
        out[plan.room :, :128] = table.astype(jnp.bfloat16)


def route_more_kernel(plan, target_ref, rows_ref, *refs, chunk):
    outs, inputs_ref = refs[:-1], refs[-1]
    lane, _ = my_lane(plan)
    first = sum(plan.chunks[1:chunk])
    for number in range(plan.lanes):
        whole = pl.multiple_of((number ^ lane) * plan.part, plan.part)
        inputs_ref[number * plan.part : (number + 1) * plan.part, :] = rows_ref[
            pl.ds(whole, plan.part), first : first + plan.chunks[chunk]
        ]
    permute_into(target_ref[...], 0, inputs_ref, outs, plan.room, plan.stride)


def gather_rows(plan, ins, inputs_ref):
    for number, part in enumerate(ins):
        first = number * plan.stride
        inputs_ref[first : first + plan.room, :] = part[: plan.room, :]
        if plan.stride > plan.room:
            inputs_ref[first + plan.room : first + plan.stride, :] = jnp.zeros(
                (plan.stride - plan.room, inputs_ref.shape[1]), jnp.bfloat16
            )


def sort_parts(plan, target, inputs_ref, outs, sorted_ref):
    tile = 2 * plan.part
    for chip, out in enumerate(outs):
        row = lax.broadcasted_iota(jnp.int32, (tile, inputs_ref.shape[0]), 0) + chip * tile
        chosen = jnp.where(row == target, 1.0, 0.0).astype(jnp.bfloat16)
        moved = jnp.dot(chosen, inputs_ref[...], preferred_element_type=jnp.float32)
        moved = moved.astype(jnp.bfloat16)
        sorted_ref[chip * tile : (chip + 1) * tile, :] = moved
        out[:tile, :] = moved
    lane, _ = my_lane(plan)
    chip, _ = chip_change(plan, lane_of(plan, 0) ^ lane)
    ahead = sorted_ref[pl.ds(pl.multiple_of(chip * tile, tile), tile), :]
    for out in outs:
        out[tile:, :] = ahead


def deliver_kernel(plan, *refs):
    ins, rest = refs[: plan.layers], refs[plan.layers :]
    outs, (target_ref, full_ref, inputs_ref, sorted_ref) = rest[:-4], rest[-4:]
    lane, _ = my_lane(plan)
    gather_rows(plan, ins, inputs_ref)
    full = jnp.zeros((8, 128), jnp.float32)
    for number, part in enumerate(ins):
        table = part[plan.room :, :128].astype(jnp.float32)
        lines = [table[piece : piece + 1, :] for piece in range(plan.stride // 128)]
        value = jnp.concatenate(lines, axis=1).astype(jnp.int32) - 1
        full = jnp.maximum(full, jnp.broadcast_to(table[15:, :], (8, 128)))
        slot = value // plan.blocks
        within = lax.broadcasted_iota(jnp.int32, value.shape, 1) % plan.slice
        chip, _ = chip_change(plan, lane_of(plan, slot) ^ lane)
        target = (2 * chip + slot % 2) * plan.part + value % plan.blocks * plan.slice + within
        target_ref[:, number * plan.stride : (number + 1) * plan.stride] = jnp.where(
            value >= 0, target, -1
        )
    full_ref[...] = full.astype(jnp.int32)
    sort_parts(plan, target_ref[...], inputs_ref, outs, sorted_ref)


def deliver_more_kernel(plan, target_ref, *refs):
    ins, rest = refs[: plan.layers], refs[plan.layers :]
    outs, (inputs_ref, sorted_ref) = rest[:-2], rest[-2:]
    gather_rows(plan, ins, inputs_ref)
    sort_parts(plan, target_ref[...], inputs_ref, outs, sorted_ref)


def join_kernel(plan, *refs):
    ins, outs = refs[:-2], refs[-2:]
    tile = 2 * plan.part
    for number, part in enumerate(ins):
        for half, out in enumerate(outs):
            out[number * tile : (number + 1) * tile, :] = part[half * tile : (half + 1) * tile, :]


def add_best(keys, queries_ref, best_ref, allowed=None):
    scores = lax.dot_general(
        keys, queries_ref[...], (((1,), (1,)), ((), ())), preferred_element_type=jnp.float32
    )
    if allowed is not None:
        scores = jnp.where(allowed, scores, -2.0)
    best_ref[...] = jnp.maximum(best_ref[...], jnp.max(scores, axis=0, keepdims=True))


def staged_best_kernel(plan, run_len_ref, *refs):
    count = len(plan.chunks)
    own, mate, behind, far = (refs[n * count : (n + 1) * count] for n in range(4))
    out_ref, best_ref, queries_ref, lines_ref = refs[4 * count :]
    lane, _ = my_lane(plan)
    group, slot = plan.slot(lax.axis_index("ingest"), lax.axis_index("run"))
    core = slot % 2
    begin = jnp.int32(0)
    for number, start in enumerate(cluster_starts(plan, run_len_ref)):
        here = (number // plan.per_group == group) & (start <= slot)
        begin = jnp.where(here, jnp.maximum(begin, start), begin)
    chips = plan.lanes // 2
    for side, parts in enumerate((own, mate)):
        for chip in range(chips):
            there = pl.ds(pl.multiple_of((2 * chip + core) * plan.part, plan.part), plan.part)
            here = slice((side * chips + chip) * plan.part, (side * chips + chip + 1) * plan.part)
            first = 0
            for part in parts:
                queries_ref[here, first : first + part.shape[1]] = part[there, :]
                first += part.shape[1]

    def slots(row):
        line = row // plan.part
        source = lane_change(plan, line % chips, line // chips) ^ lane
        block = row // plan.slice % plan.blocks
        return block * plan.cap + source * plan.slice + row % plan.slice

    best_ref[...] = jnp.full(best_ref.shape, -1.0, jnp.float32)
    query = slots(lax.broadcasted_iota(jnp.int32, (1, plan.rows), 1))
    for first in range(0, plan.rows, TILE):
        key = slots(lax.broadcasted_iota(jnp.int32, (TILE, 1), 0) + first)
        add_best(queries_ref[first : first + TILE, :], queries_ref, best_ref, key < query)

    @pl.when(core == 1)
    def _():
        for parts in (own, mate):
            for pair in range(0, chips, 2):
                keys = []
                for number in (pair, pair + 1):
                    here = slice(2 * number * plan.part, (2 * number + 1) * plan.part)
                    keys.append(jnp.concatenate([part[here, :] for part in parts], axis=1))
                add_best(jnp.concatenate(keys, axis=0), queries_ref, best_ref)

    @pl.when(slot - core - 2 >= begin)
    def _():
        for parts in (behind, far):
            for first in range(0, plan.rows, TILE):
                keys = [part[first : first + TILE, :] for part in parts]
                add_best(jnp.concatenate(keys, axis=1), queries_ref, best_ref)

    for number in range(plan.lanes):
        lines_ref[number : number + 1, :] = best_ref[
            :, number * plan.part : (number + 1) * plan.part
        ]
    for device in range(plan.devices):
        out_ref[device] = lines_ref[...]


def staged_unpack_kernel(plan, run_len_ref, cluster_ref, rank_ref, reply_ref, out_ref):
    group, slot, within = row_slot(plan, run_len_ref, cluster_ref[...], rank_ref[...])
    residue = within % plan.cap
    chip, core = chip_change(plan, residue // plan.slice ^ lane_of(plan, slot))
    line = plan.device(group, slot) * plan.lanes + core * (plan.lanes // 2) + chip
    column = within // plan.cap * plan.slice + residue % plan.slice
    number = lax.broadcasted_iota(jnp.int32, (plan.devices * plan.lanes, plan.rows), 0)
    left, pieces = reply_ref[...], []
    for _ in range(3):
        pieces.append(left.astype(jnp.bfloat16))
        left = left - pieces[-1].astype(jnp.float32)
    columns = lax.dot_general(
        jnp.concatenate(pieces, axis=1),
        jnp.where(number == line, 1.0, 0.0).astype(jnp.bfloat16),
        (((0,), (0,)), ((), ())),
        preferred_element_type=jnp.float32,
    )
    high, middle, low = (columns[n * plan.part : (n + 1) * plan.part, :] for n in range(3))
    columns = high + middle + low
    place = lax.broadcasted_iota(jnp.int32, (plan.part, plan.rows), 0)
    out_ref[...] = jnp.sum(jnp.where(place == column, columns, 0.0), axis=0, keepdims=True)


SMEM = pl.BlockSpec(memory_space=pltpu.SMEM)
VMEM = pl.BlockSpec(memory_space=pltpu.VMEM)


def call(kernel, plan, shapes, specs, scratch=(), flops=0, moved=0, memory=32):
    return pl.pallas_call(
        functools.partial(kernel, plan),
        out_shape=shapes,
        in_specs=specs,
        out_specs=[VMEM] * len(shapes),
        scratch_shapes=scratch,
        compiler_params=pltpu.CompilerParams(vmem_limit_bytes=memory * MIB),
        cost_estimate=pl.CostEstimate(flops=flops, bytes_accessed=moved, transcendentals=0),
    )


def exchange(block):
    return lax.all_to_all(block, AXES, split_axis=0, concat_axis=0, tiled=True)


def direct(plan, embeddings, clusters, ranks, run_len):
    rows, width = embeddings.shape
    slots = plan.devices * plan.cap
    wide = jax.ShapeDtypeStruct
    outgoing, groups = call(
        pack_kernel,
        plan,
        [wide((slots, width), jnp.bfloat16), wide((plan.devices, 128), jnp.int32)],
        [SMEM, VMEM, VMEM, VMEM],
        [pltpu.VMEM((rows, width), jnp.bfloat16)],
        2 * slots * rows * width,
        3 * rows * width * 2,
    )(run_len, clusters, ranks, embeddings)
    groups = exchange(groups)
    arrived = exchange(outgoing)
    (own,) = call(
        sort_kernel, plan, [wide((rows, width), jnp.bfloat16)], [SMEM, VMEM],
        moved=3 * rows * width * 2,
    )(groups, arrived)

    def swap(block):
        pairs = [
            (i * plan.run + r, (i ^ 1) * plan.run + r)
            for i in range(plan.ingest)
            for r in range(plan.run)
        ]
        return lax.ppermute(block, AXES, pairs)

    mate = swap(own)
    behind = []
    for distance, chips in enumerate(plan.links()):
        if distance == 0:
            continue
        pairs = [
            (plan.device(i, 2 * chip + core), plan.device(i, 2 * (chip + distance) + core))
            for i in range(plan.ingest)
            for chip in chips
            for core in range(2)
        ]
        moved = lax.ppermute(own, AXES, pairs)
        behind += [moved, swap(moved)]
    place = jnp.stack([lax.axis_index("ingest"), lax.axis_index("run")]).astype(jnp.int32)
    (replies,) = call(
        best_kernel,
        plan,
        [wide((plan.devices, 128), jnp.float32)],
        [SMEM, SMEM, SMEM] + [VMEM] * (2 + len(behind)),
        [pltpu.VMEM((1, rows), jnp.float32), pltpu.VMEM((rows // plan.cap, 128), jnp.float32)],
        2 * rows * rows * width * 3,
        4 * rows * width * 2,
    )(run_len, place, groups, own, mate, *behind)
    returned = exchange(replies)
    (best,) = call(
        unpack_kernel, plan, [wide((1, rows), jnp.float32)], [SMEM, VMEM, VMEM, VMEM],
        moved=4 * rows * 4,
    )(run_len, clusters, ranks, returned)
    return best


def staged(plan, embeddings, clusters, ranks, run_len):
    rows, width = embeddings.shape
    wide = jax.ShapeDtypeStruct
    half = jnp.bfloat16
    lanes, layers = range(plan.lanes), range(plan.layers)

    def along_lanes(block, change):
        pairs = [
            (lane_device(plan, layer, lane), lane_device(plan, layer, lane ^ change))
            for layer in layers
            for lane in lanes
        ]
        return lax.ppermute(block, AXES, pairs)

    def along_layers(block, change):
        pairs = [
            (lane_device(plan, layer, lane), lane_device(plan, layer ^ change, lane))
            for layer in layers
            for lane in lanes
        ]
        return lax.ppermute(block, AXES, pairs)

    far_first = sorted(lanes[1:], key=lambda change: -(change & 1) - (change // plan.width // 2))

    *spread, unit, target = call(
        spread_kernel,
        plan,
        [wide((plan.part + 16, plan.chunks[0]), half) for _ in lanes]
        + [wide((rows, width), half), wide((1, rows), jnp.int32)],
        [SMEM, VMEM, VMEM, VMEM],
        (),
        2 * rows * rows * plan.chunks[0],
        3 * rows * width * 2,
        memory=24,
    )(run_len, clusters, ranks, embeddings)
    (later,) = call(
        spread_more_kernel,
        plan,
        [wide((rows, width - plan.chunks[0]), half)],
        [VMEM, VMEM],
        (),
        2 * rows * rows * (width - plan.chunks[0]),
        3 * rows * width * 2,
        memory=16,
    )(unit, target)
    swapped = {change: along_lanes(spread[change], change) for change in far_first}
    spread = [spread[0]] + [swapped[change] for change in lanes[1:]]
    pair, mates, behind, fars = [], [], [], []
    table = targets = full = None
    arrivals, routes = [], []
    for chunk, f in enumerate(plan.chunks):
        spec = dict(flops=2 * rows * rows * f, moved=3 * rows * f * 2, memory=12)
        rooms = [wide((plan.room + (0 if chunk else 16), f), half) for _ in layers]
        inputs = pltpu.VMEM((rows, f), half)
        if chunk == 0:
            *routed, table = call(
                route_kernel,
                plan,
                [*rooms, wide((1, rows), jnp.int32)],
                [VMEM] * plan.lanes,
                [
                    inputs,
                    pltpu.VMEM((plan.lanes, plan.part), jnp.int32),
                    pltpu.VMEM((plan.lanes, plan.part), jnp.int32),
                    pltpu.VMEM((1, rows), jnp.float32),
                ],
                **spec,
            )(*spread)
        else:
            if chunk == 1:
                later, _ = lax.optimization_barrier((later, table))
                groups = [[lane_device(plan, layer, lane) for lane in lanes] for layer in layers]
                later = lax.all_to_all(
                    later, AXES, 0, 0, tiled=True, axis_index_groups=groups
                )
            more = functools.partial(route_more_kernel, chunk=chunk)
            routed = call(more, plan, rooms, [VMEM] * 2, [inputs], **spec)(table, later)
        moved = {change: along_layers(routed[change], change) for change in reversed(layers[1:])}
        arrived = [routed[0]] + [moved[change] for change in layers[1:]]
        arrivals.append(arrived)
        routes.append(routed)
    for chunk, f in enumerate(plan.chunks):
        spec = dict(flops=2 * rows * rows * f, moved=3 * rows * f * 2, memory=12)
        inputs = pltpu.VMEM((rows, f), half)
        arrived = arrivals[chunk]
        ahead = chunk + 1
        if chunk == len(plan.chunks) - 1:
            arrived, _ = lax.optimization_barrier((arrived, parts))
        if ahead < len(plan.chunks):
            arrived, _ = lax.optimization_barrier((arrived, arrivals[ahead][1] if ahead + 1 == len(plan.chunks) else routes[ahead]))
        shapes = [wide((4 * plan.part, f), half) for _ in range(plan.lanes // 2)]
        scratch = [pltpu.VMEM((plan.layers * plan.stride, f), half), inputs]
        if chunk == 0:
            *parts, targets, full = call(
                deliver_kernel,
                plan,
                [
                    *shapes,
                    wide((1, plan.layers * plan.stride), jnp.int32),
                    wide((8, 128), jnp.int32),
                ],
                [VMEM] * plan.layers,
                scratch,
                **spec,
            )(*arrived)
        else:
            parts = call(
                deliver_more_kernel, plan, shapes, [VMEM] * (1 + plan.layers), scratch, **spec
            )(targets, *arrived)
        parts = [
            along_lanes(part, lane_change(plan, chip, 0)) if chip else part
            for chip, part in enumerate(parts)
        ]
        spec = dict(moved=8 * rows * f * 2, memory=8)
        joined = call(
            join_kernel, plan, [wide((rows, f), half)] * 2, [VMEM] * len(parts), **spec
        )(*parts)
        for kept, block in zip((pair, behind), joined):
            kept.append(block)
        for kept, block in zip((mates, fars), joined):
            kept.append(along_lanes(block, plan.width))
    count = len(plan.chunks)
    (replies,) = call(
        staged_best_kernel,
        plan,
        [wide((plan.devices, plan.lanes, 128), jnp.float32)],
        [SMEM] + [VMEM] * (4 * count),
        [
            pltpu.VMEM((1, rows), jnp.float32),
            pltpu.VMEM((rows, width), half),
            pltpu.VMEM((plan.lanes, 128), jnp.float32),
        ],
        2 * rows * rows * width * 3,
        4 * rows * width * 2,
        memory=24,
    )(run_len, *pair, *mates, *behind, *fars)
    returned = exchange(replies).reshape(plan.devices * plan.lanes, 128)
    (best,) = call(
        staged_unpack_kernel,
        plan,
        [wide((1, rows), jnp.float32)],
        [SMEM, VMEM, VMEM, VMEM],
        moved=4 * rows * 4,
        memory=8,
    )(run_len, clusters, ranks, returned)
    return best, full[0, 0]


def local(embeddings, cluster_id, rank, run_len):
    rows, width = embeddings.shape
    plan = Plan(lax.axis_size("ingest"), lax.axis_size("run"), run_len.shape[0], rows, width)
    given = (embeddings, cluster_id.reshape(1, rows), rank.reshape(1, rows), run_len)
    if not plan.staged():
        return direct(plan, *given).reshape(rows)
    best, full = staged(plan, *given)
    best = lax.cond(full > 0, lambda: direct(plan, *given), lambda: best)
    return best.reshape(rows)


def solution(mesh):
    return jax.shard_map(
        local,
        mesh=mesh,
        in_specs=(P(AXES, None), P(AXES), P(AXES), P()),
        out_specs=P(AXES),
        check_vma=False,
    )
```

```python
import functools

import jax
import jax.numpy as jnp
from jax import lax
from jax.experimental import pallas as pl
from jax.experimental.pallas import tpu as pltpu
from jax.sharding import PartitionSpec as P

EPSILON = 1e-06
AXES = ("ingest", "run")
TILE = 512
SHARES = (1, 1, 1)
MIB = 1024 * 1024


class Plan:
    def __init__(self, ingest, run, clusters, rows, features):
        self.ingest, self.run, self.clusters, self.rows = ingest, run, clusters, rows
        self.devices = ingest * run
        self.per_group = clusters // ingest
        self.cap = 2 * rows // self.devices
        self.reach = min(8, run // 2)
        self.width = run // ingest
        self.pairs = run // 2
        self.blocks = rows // self.cap
        self.layers, self.lanes = ingest, ingest * self.width
        self.slice = self.cap // self.lanes
        self.part = self.blocks * self.slice
        self.chunks = tuple(features * share // sum(SHARES) for share in SHARES)
        mean = rows // self.layers
        self.room = mean + mean // 8
        self.stride = -(-self.room // 128) * 128

    def staged(self):
        powers = all(n & (n - 1) == 0 for n in (self.layers, self.lanes, self.width))
        return (
            powers
            and self.cap % (8 * self.lanes) == 0
            and self.part == 128
            and self.room % 16 == 0
            and all(width % 128 == 0 for width in self.chunks)
            and self.links()[1:] == [[0]]
        )

    def device(self, group, slot):
        core, chip = slot % 2, slot // 2
        column, place = chip // self.width, chip % self.width
        odd = column % 2
        place = place + odd * (self.width - 1 - 2 * place)
        return (2 * column + core) * self.run + group * self.width + place

    def slot(self, device_ingest, device_run):
        core, column = device_ingest % 2, device_ingest // 2
        place = device_run % self.width
        place = place + (column % 2) * (self.width - 1 - 2 * place)
        return device_run // self.width, 2 * (column * self.width + place) + core

    def splits(self):
        def parts(total, count, top):
            if count == 0:
                if total == 0:
                    yield ()
                return
            for first in range(min(top, total), 0, -1):
                for rest in parts(total - first, count - 1, first):
                    yield (first, *rest)

        return list(parts(self.pairs, self.per_group, self.reach // 2))

    def links(self):
        found = [set() for _ in range(self.reach // 2)]
        for split in self.splits():
            begin = 0
            for length in split:
                for first in range(length):
                    for second in range(first + 1, length):
                        found[second - first].add(begin + first)
                begin += length
        return [sorted(chips) for chips in found]


def cluster_starts(plan, run_len_ref):
    starts = []
    for cluster in range(plan.clusters):
        base = cluster // plan.per_group * plan.per_group
        mine = run_len_ref[cluster]
        total = jnp.int32(0)
        for other in range(base, base + plan.per_group):
            if other == cluster:
                continue
            theirs = run_len_ref[other]
            ahead = (theirs >= mine) if other < cluster else (theirs > mine)
            total = total + jnp.where(ahead, theirs, 0)
        starts.append(total)
    return starts


def row_slot(plan, run_len_ref, cluster, rank):
    starts = cluster_starts(plan, run_len_ref)
    begin = jnp.zeros_like(cluster)
    group = jnp.zeros_like(cluster)
    for number, start in enumerate(starts):
        here = cluster == number
        begin = jnp.where(here, start, begin)
        group = jnp.where(here, number // plan.per_group, group)
    return group, begin + rank // plan.rows, rank % plan.rows


def row_owner(plan, run_len_ref, cluster, rank):
    group, slot, within = row_slot(plan, run_len_ref, cluster, rank)
    return plan.device(group, slot), within


def pack_kernel(plan, run_len_ref, cluster_ref, rank_ref, rows_ref, out_ref, group_ref, unit_ref):
    step = 128

    @pl.loop(0, plan.rows // step)
    def _(number):
        here = pl.ds(pl.multiple_of(number * step, step), step)
        widened = rows_ref[here, :].astype(jnp.float32)
        total = jnp.sum(widened * widened, axis=1, keepdims=True) + EPSILON
        unit_ref[here, :] = (widened * lax.rsqrt(total)).astype(jnp.bfloat16)

    owner, within = row_owner(plan, run_len_ref, cluster_ref[...], rank_ref[...])
    number = lax.broadcasted_iota(jnp.int32, (plan.devices, plan.rows), 0)
    group = jnp.max(
        jnp.where(number == owner, within // plan.cap + 1, 0), axis=1, keepdims=True
    )
    group_ref[...] = jnp.broadcast_to(group, group_ref.shape)
    position = owner * plan.cap + within % plan.cap

    @pl.loop(0, plan.devices * plan.cap // TILE)
    def _(tile):
        row = lax.broadcasted_iota(jnp.int32, (TILE, plan.rows), 0) + tile * TILE
        chosen = jnp.where(row == position, 1.0, 0.0).astype(jnp.bfloat16)
        moved = jnp.dot(chosen, unit_ref[...], preferred_element_type=jnp.float32)
        here = pl.ds(pl.multiple_of(tile * TILE, TILE), TILE)
        out_ref[here, :] = moved.astype(jnp.bfloat16)


def sort_kernel(plan, group_ref, arrived_ref, out_ref):
    for source in range(plan.devices):
        group = group_ref[source, 0]

        @pl.when(group > 0)
        def _():
            here = pl.ds(pl.multiple_of((group - 1) * plan.cap, plan.cap), plan.cap)
            out_ref[here, :] = arrived_ref[source * plan.cap : (source + 1) * plan.cap, :]


def block_best(keys_ref, queries_ref, best_ref):
    rows = keys_ref.shape[0]

    @pl.loop(0, rows // TILE)
    def _(tile):
        keys = keys_ref[pl.ds(pl.multiple_of(tile * TILE, TILE), TILE), :]
        scores = lax.dot_general(
            keys, queries_ref[...], (((1,), (1,)), ((), ())), preferred_element_type=jnp.float32
        )
        best_ref[...] = jnp.maximum(best_ref[...], jnp.max(scores, axis=0, keepdims=True))


def triangle_best(rows_ref, best_ref):
    rows = rows_ref.shape[0]
    for first in range(0, rows, TILE):
        scores = lax.dot_general(
            rows_ref[first : first + TILE, :],
            rows_ref[first:, :],
            (((1,), (1,)), ((), ())),
            preferred_element_type=jnp.float32,
        )
        key = lax.broadcasted_iota(jnp.int32, (TILE, TILE), 0)
        query = lax.broadcasted_iota(jnp.int32, (TILE, TILE), 1)
        corner = jnp.max(
            jnp.where(key < query, scores[:, :TILE], -2.0), axis=0, keepdims=True
        )
        here = slice(first, first + TILE)
        best_ref[:, here] = jnp.maximum(best_ref[:, here], corner)
        if first + TILE < rows:
            rest = jnp.max(scores[:, TILE:], axis=0, keepdims=True)
            there = slice(first + TILE, rows)
            best_ref[:, there] = jnp.maximum(best_ref[:, there], rest)


def best_kernel(plan, run_len_ref, place_ref, group_ref, own_ref, mate_ref, *rest):
    behind, (out_ref, best_ref, blocks_ref) = rest[:-3], rest[-3:]
    group, slot = plan.slot(place_ref[0], place_ref[1])
    begin = jnp.int32(0)
    for number, start in enumerate(cluster_starts(plan, run_len_ref)):
        here = (number // plan.per_group == group) & (start <= slot)
        begin = jnp.where(here, jnp.maximum(begin, start), begin)
    best_ref[...] = jnp.full(best_ref.shape, -1.0, jnp.float32)
    triangle_best(own_ref, best_ref)

    @pl.when(slot % 2 == 1)
    def _():
        block_best(mate_ref, own_ref, best_ref)

    for distance in range(1, plan.reach // 2):
        first, second = behind[2 * distance - 2], behind[2 * distance - 1]

        @pl.when(slot - slot % 2 - 2 * distance >= begin)
        def _():
            block_best(first, own_ref, best_ref)
            block_best(second, own_ref, best_ref)

    for number in range(plan.rows // plan.cap):
        part = best_ref[:, number * plan.cap : (number + 1) * plan.cap]
        blocks_ref[number : number + 1, : plan.cap] = part
    for source in range(plan.devices):
        chosen = jnp.maximum(group_ref[source, 0] - 1, 0)
        out_ref[source : source + 1, :] = blocks_ref[pl.ds(chosen, 1), :]


def unpack_kernel(plan, run_len_ref, cluster_ref, rank_ref, reply_ref, out_ref):
    owner, within = row_owner(plan, run_len_ref, cluster_ref[...], rank_ref[...])
    number = lax.broadcasted_iota(jnp.int32, (plan.devices, plan.rows), 0)
    chosen = jnp.where(number == owner, 1.0, 0.0)
    columns = lax.dot_general(
        reply_ref[:, : plan.cap],
        chosen,
        (((0,), (0,)), ((), ())),
        precision=lax.Precision.HIGHEST,
        preferred_element_type=jnp.float32,
    )
    lane = lax.broadcasted_iota(jnp.int32, (plan.cap, plan.rows), 0)
    out_ref[...] = jnp.sum(
        jnp.where(lane == within % plan.cap, columns, 0.0), axis=0, keepdims=True
    )


def lane_of(plan, slot):
    device = plan.device(0, slot)
    return device // plan.run * plan.width + device % plan.run


def chip_change(plan, change):
    width = plan.width
    return change % width + change // (2 * width) * width, change // width % 2


def lane_change(plan, chip, core):
    width = plan.width
    return chip % width + core * width + chip // width * 2 * width


def lane_device(plan, layer, lane):
    return lane // plan.width * plan.run + layer * plan.width + lane % plan.width


def my_lane(plan):
    run = lax.axis_index("run")
    return lax.axis_index("ingest") * plan.width + run % plan.width, run // plan.width


def spread_pair(plan, part, target, rows):
    row = lax.broadcasted_iota(jnp.int32, (2 * plan.part, plan.rows), 0) + part * plan.part
    chosen = jnp.where(row == target, 1.0, 0.0).astype(jnp.bfloat16)
    return jnp.dot(chosen, rows, preferred_element_type=jnp.float32).astype(jnp.bfloat16)


def spread_more_kernel(plan, unit_ref, target_ref, out_ref):
    lane, _ = my_lane(plan)
    for part in range(0, plan.lanes, 2):
        moved = spread_pair(plan, part, target_ref[...], unit_ref[:, plan.chunks[0] :])
        for number in range(2):
            whole = pl.multiple_of((part + number ^ lane) * plan.part, plan.part)
            here = moved[number * plan.part : (number + 1) * plan.part, :]
            out_ref[pl.ds(whole, plan.part), :] = here


def spread_kernel(plan, run_len_ref, cluster_ref, rank_ref, rows_ref, *rest):
    outs, (unit_ref, target_ref) = rest[:-2], rest[-2:]
    step = 128

    @pl.loop(0, plan.rows // step, unroll=True)
    def _(number):
        here = pl.ds(pl.multiple_of(number * step, step), step)
        widened = rows_ref[here, :].astype(jnp.float32)
        total = jnp.sum(widened * widened, axis=1, keepdims=True) + EPSILON
        unit_ref[here, :] = (widened * lax.rsqrt(total)).astype(jnp.bfloat16)

    lane, _ = my_lane(plan)
    group, slot, within = row_slot(plan, run_len_ref, cluster_ref[...], rank_ref[...])
    owner = group * plan.run + slot
    number = lax.broadcasted_iota(jnp.int32, (plan.devices, plan.rows), 0)
    member = number == owner
    block = jnp.max(jnp.where(member, within // plan.cap + 1, 0), axis=1, keepdims=True)
    present = jnp.where(block > 0, 1.0, 0.0)
    before = lax.broadcasted_iota(jnp.int32, (plan.devices, plan.devices), 0) > (
        lax.broadcasted_iota(jnp.int32, (plan.devices, plan.devices), 1)
    )
    order = jnp.dot(
        jnp.where(before, 1.0, 0.0),
        jnp.broadcast_to(present, (plan.devices, 128)),
        preferred_element_type=jnp.float32,
    )
    mine = jnp.sum(jnp.where(member, order[:, :1], 0.0), axis=0, keepdims=True)
    residue = within % plan.cap
    target = (
        (residue // plan.slice ^ lane) * plan.part
        + mine.astype(jnp.int32) * plan.slice
        + residue % plan.slice
    )
    target_ref[...] = target
    for part in range(0, plan.lanes, 2):
        moved = spread_pair(plan, part, target, unit_ref[:, : plan.chunks[0]])
        outs[part][: plan.part, :] = moved[: plan.part, :]
        outs[part + 1][: plan.part, :] = moved[plan.part :, :]

    place = lax.broadcasted_iota(jnp.int32, (plan.devices, plan.part), 1) // plan.slice
    here = (place.astype(jnp.float32) == order[:, :1]) & (block > 0)
    who = lax.broadcasted_iota(jnp.int32, (plan.devices, plan.part), 0)
    owners = jnp.sum(jnp.where(here, who, 0), axis=0, keepdims=True)
    blocks = jnp.sum(jnp.where(here, block - 1, 0), axis=0, keepdims=True)
    line = lax.broadcasted_iota(jnp.int32, (16, plan.part), 0)
    table = jnp.where(line == 0, owners, jnp.where(line == 1, blocks, 0))
    for out in outs:
        out[plan.part :, : plan.part] = table.astype(jnp.float32).astype(jnp.bfloat16)


def permute_into(target, first, inputs_ref, outs, room, stride):
    columns = inputs_ref.shape[0]
    for number, out in enumerate(outs):
        row = lax.broadcasted_iota(jnp.int32, (room, columns), 0) + first + number * stride
        chosen = jnp.where(row == target, 1.0, 0.0).astype(jnp.bfloat16)
        moved = jnp.dot(chosen, inputs_ref[...], preferred_element_type=jnp.float32)
        out[:room, :] = moved.astype(jnp.bfloat16)


def route_kernel(plan, *refs):
    ins, rest = refs[: plan.lanes], refs[plan.lanes :]
    outs, (target_ref, inputs_ref, owner_ref, block_ref, value_ref) = rest[:-5], rest[-5:]
    _, layer = my_lane(plan)
    for number, part in enumerate(ins):
        inputs_ref[number * plan.part : (number + 1) * plan.part, :] = part[: plan.part, :]
        table = part[plan.part :, : plan.part].astype(jnp.float32)
        owner_ref[number : number + 1, :] = table[0:1, :].astype(jnp.int32)
        block_ref[number : number + 1, :] = table[1:2, :].astype(jnp.int32)
    owner = owner_ref[...]
    marks = [jnp.where(owner // plan.run == other, 1.0, 0.0) for other in range(plan.layers)]
    most = functools.reduce(jnp.maximum, [jnp.sum(mark) for mark in marks])
    stacked = jnp.concatenate(marks, axis=0).astype(jnp.bfloat16)
    shape = (plan.part, plan.part)
    earlier = lax.broadcasted_iota(jnp.int32, shape, 0) < lax.broadcasted_iota(jnp.int32, shape, 1)
    earlier = jnp.where(earlier, 1.0, 0.0).astype(jnp.bfloat16)
    shape = (plan.layers * plan.lanes, plan.layers * plan.lanes)
    line, above = (lax.broadcasted_iota(jnp.int32, shape, axis) for axis in range(2))
    above = (line > above) & (line // plan.lanes == above // plan.lanes)
    above = jnp.where(above, 1.0, 0.0).astype(jnp.bfloat16)
    lines = jnp.dot(above, stacked, preferred_element_type=jnp.float32)
    counts = jnp.dot(stacked, earlier, preferred_element_type=jnp.float32) + jnp.sum(
        lines, axis=1, keepdims=True
    )
    counts = counts.astype(jnp.int32)
    target = jnp.zeros(owner.shape, jnp.int32)
    for other in range(plan.layers):
        count = counts[other * plan.lanes : (other + 1) * plan.lanes, :]
        there = jnp.where(count < plan.room, (layer ^ other) * plan.stride + count, -1)
        target = jnp.where(owner // plan.run == other, there, target)
    full = jnp.where(most > plan.room, 1.0, 0.0)
    value = owner % plan.run * plan.blocks + block_ref[...] + 1
    for number in range(plan.lanes):
        here = slice(number * plan.part, (number + 1) * plan.part)
        target_ref[:, here] = target[number : number + 1, :]
        value_ref[:, here] = value[number : number + 1, :].astype(jnp.float32)
    target = target_ref[...]
    values = jnp.broadcast_to(value_ref[...], (8, plan.rows)).astype(jnp.bfloat16)
    for number, out in enumerate(outs):
        row = lax.broadcasted_iota(jnp.int32, (plan.stride, plan.rows), 0) + number * plan.stride
        chosen = jnp.where(row == target, 1.0, 0.0).astype(jnp.bfloat16)
        moved = jnp.dot(
            chosen[: plan.room, :], inputs_ref[...], preferred_element_type=jnp.float32
        )
        out[: plan.room, :] = moved.astype(jnp.bfloat16)
        listed = lax.dot_general(
            values, chosen, (((1,), (1,)), ((), ())), preferred_element_type=jnp.float32
        )
        line = lax.broadcasted_iota(jnp.int32, (16, 128), 0)
        table = jnp.where(line == 15, full, 0.0)
        for piece in range(plan.stride // 128):
            here = listed[0:1, piece * 128 : (piece + 1) * 128]
            table = jnp.where(line == piece, here, table)
        out[plan.room :, :128] = table.astype(jnp.bfloat16)


def route_more_kernel(plan, target_ref, rows_ref, *refs, chunk):
    outs, inputs_ref = refs[:-1], refs[-1]
    lane, _ = my_lane(plan)
    first = sum(plan.chunks[1:chunk])
    for number in range(plan.lanes):
        whole = pl.multiple_of((number ^ lane) * plan.part, plan.part)
        inputs_ref[number * plan.part : (number + 1) * plan.part, :] = rows_ref[
            pl.ds(whole, plan.part), first : first + plan.chunks[chunk]
        ]
    permute_into(target_ref[...], 0, inputs_ref, outs, plan.room, plan.stride)


def gather_rows(plan, ins, inputs_ref):
    for number, part in enumerate(ins):
        first = number * plan.stride
        inputs_ref[first : first + plan.room, :] = part[: plan.room, :]
        if plan.stride > plan.room:
            inputs_ref[first + plan.room : first + plan.stride, :] = jnp.zeros(
                (plan.stride - plan.room, inputs_ref.shape[1]), jnp.bfloat16
            )


def sort_parts(plan, target, inputs_ref, outs, sorted_ref):
    tile = 2 * plan.part
    for chip, out in enumerate(outs):
        row = lax.broadcasted_iota(jnp.int32, (tile, inputs_ref.shape[0]), 0) + chip * tile
        chosen = jnp.where(row == target, 1.0, 0.0).astype(jnp.bfloat16)
        moved = jnp.dot(chosen, inputs_ref[...], preferred_element_type=jnp.float32)
        moved = moved.astype(jnp.bfloat16)
        sorted_ref[chip * tile : (chip + 1) * tile, :] = moved
        out[:tile, :] = moved
    lane, _ = my_lane(plan)
    chip, _ = chip_change(plan, lane_of(plan, 0) ^ lane)
    ahead = sorted_ref[pl.ds(pl.multiple_of(chip * tile, tile), tile), :]
    for out in outs:
        out[tile:, :] = ahead


def deliver_kernel(plan, *refs):
    ins, rest = refs[: plan.layers], refs[plan.layers :]
    outs, (target_ref, full_ref, inputs_ref, sorted_ref) = rest[:-4], rest[-4:]
    lane, _ = my_lane(plan)
    gather_rows(plan, ins, inputs_ref)
    full = jnp.zeros((8, 128), jnp.float32)
    for number, part in enumerate(ins):
        table = part[plan.room :, :128].astype(jnp.float32)
        lines = [table[piece : piece + 1, :] for piece in range(plan.stride // 128)]
        value = jnp.concatenate(lines, axis=1).astype(jnp.int32) - 1
        full = jnp.maximum(full, jnp.broadcast_to(table[15:, :], (8, 128)))
        slot = value // plan.blocks
        within = lax.broadcasted_iota(jnp.int32, value.shape, 1) % plan.slice
        chip, _ = chip_change(plan, lane_of(plan, slot) ^ lane)
        target = (2 * chip + slot % 2) * plan.part + value % plan.blocks * plan.slice + within
        target_ref[:, number * plan.stride : (number + 1) * plan.stride] = jnp.where(
            value >= 0, target, -1
        )
    full_ref[...] = full.astype(jnp.int32)
    sort_parts(plan, target_ref[...], inputs_ref, outs, sorted_ref)


def deliver_more_kernel(plan, target_ref, *refs):
    ins, rest = refs[: plan.layers], refs[plan.layers :]
    outs, (inputs_ref, sorted_ref) = rest[:-2], rest[-2:]
    gather_rows(plan, ins, inputs_ref)
    sort_parts(plan, target_ref[...], inputs_ref, outs, sorted_ref)


def join_kernel(plan, *refs):
    ins, outs = refs[:-2], refs[-2:]
    tile = 2 * plan.part
    for number, part in enumerate(ins):
        for half, out in enumerate(outs):
            out[number * tile : (number + 1) * tile, :] = part[half * tile : (half + 1) * tile, :]


def add_best(keys, queries_ref, best_ref, allowed=None):
    scores = lax.dot_general(
        keys, queries_ref[...], (((1,), (1,)), ((), ())), preferred_element_type=jnp.float32
    )
    if allowed is not None:
        scores = jnp.where(allowed, scores, -2.0)
    scores = jnp.max(scores.reshape(-1, 8, scores.shape[1]), axis=0)
    best_ref[...] = jnp.maximum(best_ref[...], scores)


def staged_best_kernel(plan, run_len_ref, *refs):
    count = len(plan.chunks)
    own, mate, behind, far = (refs[n * count : (n + 1) * count] for n in range(4))
    out_ref, best_ref, queries_ref, lines_ref = refs[4 * count :]
    lane, _ = my_lane(plan)
    group, slot = plan.slot(lax.axis_index("ingest"), lax.axis_index("run"))
    core = slot % 2
    begin = jnp.int32(0)
    for number, start in enumerate(cluster_starts(plan, run_len_ref)):
        here = (number // plan.per_group == group) & (start <= slot)
        begin = jnp.where(here, jnp.maximum(begin, start), begin)
    chips = plan.lanes // 2
    for side, parts in enumerate((own, mate)):
        for chip in range(chips):
            there = pl.ds(pl.multiple_of((2 * chip + core) * plan.part, plan.part), plan.part)
            here = slice((side * chips + chip) * plan.part, (side * chips + chip + 1) * plan.part)
            first = 0
            for part in parts:
                queries_ref[here, first : first + part.shape[1]] = part[there, :]
                first += part.shape[1]

    def slots(row):
        line = row // plan.part
        source = lane_change(plan, line % chips, line // chips) ^ lane
        block = row // plan.slice % plan.blocks
        return block * plan.cap + source * plan.slice + row % plan.slice

    best_ref[...] = jnp.full(best_ref.shape, -1.0, jnp.float32)
    query = slots(lax.broadcasted_iota(jnp.int32, (1, plan.rows), 1))
    for first in range(0, plan.rows, TILE):
        key = slots(lax.broadcasted_iota(jnp.int32, (TILE, 1), 0) + first)
        add_best(queries_ref[first : first + TILE, :], queries_ref, best_ref, key < query)

    @pl.when(core == 1)
    def _():
        for parts in (own, mate):
            for pair in range(0, chips, 2):
                keys = []
                for number in (pair, pair + 1):
                    here = slice(2 * number * plan.part, (2 * number + 1) * plan.part)
                    keys.append(jnp.concatenate([part[here, :] for part in parts], axis=1))
                add_best(jnp.concatenate(keys, axis=0), queries_ref, best_ref)

    @pl.when(slot - core - 2 >= begin)
    def _():
        for parts in (behind, far):
            for first in range(0, plan.rows, TILE):
                keys = [part[first : first + TILE, :] for part in parts]
                add_best(jnp.concatenate(keys, axis=1), queries_ref, best_ref)

    best = jnp.max(best_ref[...], axis=0, keepdims=True)
    for number in range(plan.lanes):
        here = slice(number * plan.part, (number + 1) * plan.part)
        lines_ref[number : number + 1, :] = best[:, here]
    for device in range(plan.devices):
        out_ref[device] = lines_ref[...]


def staged_unpack_kernel(plan, run_len_ref, cluster_ref, rank_ref, reply_ref, out_ref):
    group, slot, within = row_slot(plan, run_len_ref, cluster_ref[...], rank_ref[...])
    residue = within % plan.cap
    chip, core = chip_change(plan, residue // plan.slice ^ lane_of(plan, slot))
    line = plan.device(group, slot) * plan.lanes + core * (plan.lanes // 2) + chip
    column = within // plan.cap * plan.slice + residue % plan.slice
    number = lax.broadcasted_iota(jnp.int32, (plan.devices * plan.lanes, plan.rows), 0)
    left, pieces = reply_ref[...], []
    for _ in range(3):
        pieces.append(left.astype(jnp.bfloat16))
        left = left - pieces[-1].astype(jnp.float32)
    columns = lax.dot_general(
        jnp.concatenate(pieces, axis=1),
        jnp.where(number == line, 1.0, 0.0).astype(jnp.bfloat16),
        (((0,), (0,)), ((), ())),
        preferred_element_type=jnp.float32,
    )
    high, middle, low = (columns[n * plan.part : (n + 1) * plan.part, :] for n in range(3))
    columns = high + middle + low
    place = lax.broadcasted_iota(jnp.int32, (plan.part, plan.rows), 0)
    out_ref[...] = jnp.sum(jnp.where(place == column, columns, 0.0), axis=0, keepdims=True)


SMEM = pl.BlockSpec(memory_space=pltpu.SMEM)
VMEM = pl.BlockSpec(memory_space=pltpu.VMEM)


def call(kernel, plan, shapes, specs, scratch=(), flops=0, moved=0, memory=32):
    return pl.pallas_call(
        functools.partial(kernel, plan),
        out_shape=shapes,
        in_specs=specs,
        out_specs=[VMEM] * len(shapes),
        scratch_shapes=scratch,
        compiler_params=pltpu.CompilerParams(vmem_limit_bytes=memory * MIB),
        cost_estimate=pl.CostEstimate(flops=flops, bytes_accessed=moved, transcendentals=0),
    )


def exchange(block):
    return lax.all_to_all(block, AXES, split_axis=0, concat_axis=0, tiled=True)


def direct(plan, embeddings, clusters, ranks, run_len):
    rows, width = embeddings.shape
    slots = plan.devices * plan.cap
    wide = jax.ShapeDtypeStruct
    outgoing, groups = call(
        pack_kernel,
        plan,
        [wide((slots, width), jnp.bfloat16), wide((plan.devices, 128), jnp.int32)],
        [SMEM, VMEM, VMEM, VMEM],
        [pltpu.VMEM((rows, width), jnp.bfloat16)],
        2 * slots * rows * width,
        3 * rows * width * 2,
    )(run_len, clusters, ranks, embeddings)
    groups = exchange(groups)
    arrived = exchange(outgoing)
    (own,) = call(
        sort_kernel, plan, [wide((rows, width), jnp.bfloat16)], [SMEM, VMEM],
        moved=3 * rows * width * 2,
    )(groups, arrived)

    def swap(block):
        pairs = [
            (i * plan.run + r, (i ^ 1) * plan.run + r)
            for i in range(plan.ingest)
            for r in range(plan.run)
        ]
        return lax.ppermute(block, AXES, pairs)

    mate = swap(own)
    behind = []
    for distance, chips in enumerate(plan.links()):
        if distance == 0:
            continue
        pairs = [
            (plan.device(i, 2 * chip + core), plan.device(i, 2 * (chip + distance) + core))
            for i in range(plan.ingest)
            for chip in chips
            for core in range(2)
        ]
        moved = lax.ppermute(own, AXES, pairs)
        behind += [moved, swap(moved)]
    place = jnp.stack([lax.axis_index("ingest"), lax.axis_index("run")]).astype(jnp.int32)
    (replies,) = call(
        best_kernel,
        plan,
        [wide((plan.devices, 128), jnp.float32)],
        [SMEM, SMEM, SMEM] + [VMEM] * (2 + len(behind)),
        [pltpu.VMEM((1, rows), jnp.float32), pltpu.VMEM((rows // plan.cap, 128), jnp.float32)],
        2 * rows * rows * width * 3,
        4 * rows * width * 2,
    )(run_len, place, groups, own, mate, *behind)
    returned = exchange(replies)
    (best,) = call(
        unpack_kernel, plan, [wide((1, rows), jnp.float32)], [SMEM, VMEM, VMEM, VMEM],
        moved=4 * rows * 4,
    )(run_len, clusters, ranks, returned)
    return best


def staged(plan, embeddings, clusters, ranks, run_len):
    rows, width = embeddings.shape
    wide = jax.ShapeDtypeStruct
    half = jnp.bfloat16
    lanes, layers = range(plan.lanes), range(plan.layers)

    def along_lanes(block, change):
        pairs = [
            (lane_device(plan, layer, lane), lane_device(plan, layer, lane ^ change))
            for layer in layers
            for lane in lanes
        ]
        return lax.ppermute(block, AXES, pairs)

    def along_layers(block, change):
        pairs = [
            (lane_device(plan, layer, lane), lane_device(plan, layer ^ change, lane))
            for layer in layers
            for lane in lanes
        ]
        return lax.ppermute(block, AXES, pairs)

    far_first = sorted(lanes[1:], key=lambda change: -(change & 1) - (change // plan.width // 2))

    *spread, unit, target = call(
        spread_kernel,
        plan,
        [wide((plan.part + 16, plan.chunks[0]), half) for _ in lanes]
        + [wide((rows, width), half), wide((1, rows), jnp.int32)],
        [SMEM, VMEM, VMEM, VMEM],
        (),
        2 * rows * rows * plan.chunks[0],
        3 * rows * width * 2,
        memory=24,
    )(run_len, clusters, ranks, embeddings)
    (later,) = call(
        spread_more_kernel,
        plan,
        [wide((rows, width - plan.chunks[0]), half)],
        [VMEM, VMEM],
        (),
        2 * rows * rows * (width - plan.chunks[0]),
        3 * rows * width * 2,
        memory=16,
    )(unit, target)
    swapped = {change: along_lanes(spread[change], change) for change in far_first}
    spread = [spread[0]] + [swapped[change] for change in lanes[1:]]
    pair, mates, behind, fars = [], [], [], []
    table = targets = full = None
    arrivals, routes = [], []
    for chunk, f in enumerate(plan.chunks):
        spec = dict(flops=2 * rows * rows * f, moved=3 * rows * f * 2, memory=12)
        rooms = [wide((plan.room + (0 if chunk else 16), f), half) for _ in layers]
        inputs = pltpu.VMEM((rows, f), half)
        if chunk == 0:
            *routed, table = call(
                route_kernel,
                plan,
                [*rooms, wide((1, rows), jnp.int32)],
                [VMEM] * plan.lanes,
                [
                    inputs,
                    pltpu.VMEM((plan.lanes, plan.part), jnp.int32),
                    pltpu.VMEM((plan.lanes, plan.part), jnp.int32),
                    pltpu.VMEM((1, rows), jnp.float32),
                ],
                **spec,
            )(*spread)
        else:
            if chunk == 1:
                later, _ = lax.optimization_barrier((later, table))
                groups = [[lane_device(plan, layer, lane) for lane in lanes] for layer in layers]
                later = lax.all_to_all(
                    later, AXES, 0, 0, tiled=True, axis_index_groups=groups
                )
            more = functools.partial(route_more_kernel, chunk=chunk)
            routed = call(more, plan, rooms, [VMEM] * 2, [inputs], **spec)(table, later)
        moved = {change: along_layers(routed[change], change) for change in reversed(layers[1:])}
        arrived = [routed[0]] + [moved[change] for change in layers[1:]]
        arrivals.append(arrived)
        routes.append(routed)
    for chunk, f in enumerate(plan.chunks):
        spec = dict(flops=2 * rows * rows * f, moved=3 * rows * f * 2, memory=12)
        inputs = pltpu.VMEM((rows, f), half)
        arrived = arrivals[chunk]
        ahead = chunk + 1
        if chunk == len(plan.chunks) - 1:
            arrived, _ = lax.optimization_barrier((arrived, parts))
        if ahead < len(plan.chunks):
            arrived, _ = lax.optimization_barrier((arrived, arrivals[ahead][1] if ahead + 1 == len(plan.chunks) else routes[ahead]))
        shapes = [wide((4 * plan.part, f), half) for _ in range(plan.lanes // 2)]
        scratch = [pltpu.VMEM((plan.layers * plan.stride, f), half), inputs]
        if chunk == 0:
            *parts, targets, full = call(
                deliver_kernel,
                plan,
                [
                    *shapes,
                    wide((1, plan.layers * plan.stride), jnp.int32),
                    wide((8, 128), jnp.int32),
                ],
                [VMEM] * plan.layers,
                scratch,
                **spec,
            )(*arrived)
        else:
            parts = call(
                deliver_more_kernel, plan, shapes, [VMEM] * (1 + plan.layers), scratch, **spec
            )(targets, *arrived)
        parts = [
            along_lanes(part, lane_change(plan, chip, 0)) if chip else part
            for chip, part in enumerate(parts)
        ]
        spec = dict(moved=8 * rows * f * 2, memory=8)
        joined = call(
            join_kernel, plan, [wide((rows, f), half)] * 2, [VMEM] * len(parts), **spec
        )(*parts)
        for kept, block in zip((pair, behind), joined):
            kept.append(block)
        for kept, block in zip((mates, fars), joined):
            kept.append(along_lanes(block, plan.width))
    count = len(plan.chunks)
    (replies,) = call(
        staged_best_kernel,
        plan,
        [wide((plan.devices, plan.lanes, 128), jnp.float32)],
        [SMEM] + [VMEM] * (4 * count),
        [
            pltpu.VMEM((8, rows), jnp.float32),
            pltpu.VMEM((rows, width), half),
            pltpu.VMEM((plan.lanes, 128), jnp.float32),
        ],
        2 * rows * rows * width * 3,
        4 * rows * width * 2,
        memory=24,
    )(run_len, *pair, *mates, *behind, *fars)
    returned = exchange(replies).reshape(plan.devices * plan.lanes, 128)
    (best,) = call(
        staged_unpack_kernel,
        plan,
        [wide((1, rows), jnp.float32)],
        [SMEM, VMEM, VMEM, VMEM],
        moved=4 * rows * 4,
        memory=8,
    )(run_len, clusters, ranks, returned)
    return best, full[0, 0]


def local(embeddings, cluster_id, rank, run_len):
    rows, width = embeddings.shape
    plan = Plan(lax.axis_size("ingest"), lax.axis_size("run"), run_len.shape[0], rows, width)
    given = (embeddings, cluster_id.reshape(1, rows), rank.reshape(1, rows), run_len)
    if not plan.staged():
        return direct(plan, *given).reshape(rows)
    best, full = staged(plan, *given)
    best = lax.cond(full > 0, lambda: direct(plan, *given), lambda: best)
    return best.reshape(rows)


def solution(mesh):
    return jax.shard_map(
        local,
        mesh=mesh,
        in_specs=(P(AXES, None), P(AXES), P(AXES), P()),
        out_specs=P(AXES),
        check_vma=False,
    )
```
